32 devices in a mesh: groups: 2 (over x), tile: 16 (over z, y, core).
Axes of the slice: x: 2, y: 2, z: 4, core: 2. Of those that a mesh axis runs over, the one named last changes fastest.
Arguments:
- model_field: float32 [16, 524288], P(None, ('groups', 'tile')), parts along dimension 1, may hold values from -6 to 6
- direction: float32 [16, 524288], P(None, ('groups', 'tile')), parts along dimension 1, may hold values from -100 to 100
- old_grad: float32 [16, 524288], P(None, ('groups', 'tile')), parts along dimension 1, may hold values from -100 to 100
- residual: float32 [16, 65536], P(None, ('groups', 'tile')), parts along dimension 1, may hold values from -6 to 6
- block_pairs: int32 [256, 8], P(('groups', 'tile')), parts along dimension 0, may hold values from 0 to 159, as said below
- depth_band: int32 [524288], P(('groups', 'tile')), parts along dimension 0, may hold values from 0 to 15
- station_offsets: float32 [2, 65536], P(None, ('groups', 'tile')), parts along dimension 1, may hold values from -1.25 to 2.25, as said below
Outputs:
- new_model: float32 [16, 524288], P(None, ('groups', 'tile')), parts along dimension 1
- new_residual: float32 [16, 65536], P(None, ('groups', 'tile')), parts along dimension 1
- new_direction: float32 [16, 524288], P(None, ('groups', 'tile')), parts along dimension 1
The draws below stay inside these ranges and needn't reach their ends.
There are 2 independent parts, one for each index of `groups`. The reference program is written for one: setup_inputs(seed, part) draws one part's arguments, and reference() takes and returns one part's arrays. A program takes and returns all parts, laid end to end along the dimension named above; each array names one. Nothing has to cross between parts.
Inputs may be any that keep to these rules, and one draw needn't show every extreme that they name: `block_pairs`: each row lists 8 different codes. `station_offsets`: row 1 (along) lies between 0 and 1.
All inputs are finite; a program needn't handle non-finite values.
Results may differ from the reference program's by a relative error of at most 0.0003.
Values sent between devices are 32-bit elements; how exact they have to be, the bound alone decides.
No kernel may reach another device: no remote copies, remote signals or barrier semaphores. Data moves between devices by JAX's collectives and lax.ppermute only.
A program may use at most 128 MiB of HBM per device.

```python
import math
import jax
import jax.numpy as jnp
from jax import lax

E = 16
C_DEV = 16384
S_DEV = 2048
CBLOCK = 512
SBLOCK = 256
PAIRS = 8
REACH = 2
BANDS = 16
COL_SIDE = 32
CELLS = 262144
STATIONS = 32768
PAIR_ROWS = 128
CODES = 160
N_TILE = 16


def spread_field(key, ceiling):
    key_rows, key_values = jax.random.split(key, 2)
    row_scale = jnp.exp(jax.random.uniform(key_rows, (E, 1), jnp.float32) * math.log(ceiling))
    position = jnp.arange(CELLS, dtype=jnp.int32).astype(jnp.float32)[None, :] / CELLS
    column_scale = jnp.exp(position * math.log(ceiling))
    own_part = jnp.clip(jax.random.normal(key_values, (E, CELLS), jnp.float32), -6.0, 6.0)
    return own_part * row_scale * column_scale / ceiling


def draw_direction(key, part):
    return spread_field(jax.random.fold_in(key, 11), 10.0)


def draw_old_grad(key, part):
    return spread_field(jax.random.fold_in(key, 23), 10.0)


def draw_block_pairs(key, part):
    code_ids = jnp.arange(CODES, dtype=jnp.int32)[None, :]
    row_ids = jnp.arange(PAIR_ROWS, dtype=jnp.int32)[:, None]
    scores = jax.random.randint(jax.random.fold_in(key, 37), (PAIR_ROWS, CODES), 0, 1 << 20, dtype=jnp.int32) * CODES + code_ids
    chosen = jnp.logical_and(row_ids == PAIR_ROWS // 2, jnp.logical_or(code_ids == 0, code_ids == CODES - 1))
    scores = scores + jnp.where(chosen, (1 << 21) * CODES, 0)
    ordered = jnp.argsort(-scores, axis=1)
    return ordered[:, :PAIRS].astype(jnp.int32)


def draw_station_offsets(key, part):
    key_across, key_along = jax.random.split(jax.random.fold_in(key, 41))
    across = jax.random.uniform(key_across, (STATIONS,), jnp.float32) * 3.5 - 1.25
    along = jax.random.uniform(key_along, (STATIONS,), jnp.float32)
    return jnp.stack([across, along], axis=0)


def place_ends(array, key, smallest, high):
    longest = array.shape.index(max(array.shape))
    spots = []
    for shift in (0, 1):
        where = [jax.random.randint(jax.random.fold_in(key, axis), (), 0, length) for axis, length in enumerate(array.shape)]
        where[longest] = (where[longest] + shift) % array.shape[longest]
        spots.append(tuple(where))
    return array.at[spots[0]].set(smallest).at[spots[1]].set(high)


def steps_of(stream_key, extent, cuts, low, high):
    level = 1.0
    for axis_at, blocks in cuts:
        steps = jax.random.uniform(jax.random.fold_in(jax.random.fold_in(stream_key, 6), axis_at), (blocks,), jnp.float32, low / len(cuts), high / len(cuts))
        level = level * jnp.repeat(jnp.exp(steps), extent[axis_at] // blocks).reshape((-1,) + (1,) * (len(extent) - 1 - axis_at))
    return level


def gaussian(stream_key, shape, width, bound, cuts=(), held_as=jnp.bfloat16):
    array = width * jax.random.normal(stream_key, shape, jnp.float32)
    if cuts:
        array = array * steps_of(stream_key, shape, cuts, -0.22, 0.18)
    return jnp.clip(array, -bound, bound).astype(held_as)


def setup_inputs(seed: int = 0, part: int = 0) -> dict:
    streams_of = jax.random.split(jax.random.key(seed), 8)
    own_keys = jax.random.split(jax.random.fold_in(streams_of[7], part), 8)
    return {
        "model_field": gaussian(own_keys[0], (E, CELLS), 1.0, 6.0, ((1, 16),), jnp.float32),
        "direction": draw_direction(jax.random.fold_in(jax.random.fold_in(streams_of[7], part), 71), part),
        "old_grad": draw_old_grad(jax.random.fold_in(jax.random.fold_in(streams_of[7], part), 71), part),
        "residual": gaussian(own_keys[3], (E, STATIONS), 1.0, 6.0, ((1, 16),), jnp.float32),
        "block_pairs": draw_block_pairs(jax.random.fold_in(jax.random.fold_in(streams_of[7], part), 71), part),
        "depth_band": place_ends(jax.random.randint(own_keys[5], (CELLS,), 0, BANDS), jax.random.fold_in(own_keys[5], 1), 0, BANDS - 1).astype(jnp.int32),
        "station_offsets": draw_station_offsets(jax.random.fold_in(jax.random.fold_in(streams_of[7], part), 71), part),
    }


HIGHEST = lax.Precision.HIGHEST
DEPTH_RANGE = 2.0
DEPTH_SHIFT = 0.25
DAMPING = 1.0
GUARD = 1e-06

def point_kernel(station_across, station_along, cell_across, cell_along, cell_depth):
    across_gap = station_across[..., :, None] - cell_across[..., None, :]
    along_gap = station_along[..., :, None] - cell_along[..., None, :]
    depth_column = cell_depth[..., None, :]
    inverse = lax.rsqrt(across_gap * across_gap + along_gap * along_gap + depth_column * depth_column)
    return depth_column * inverse * inverse * inverse

def reference(model_field, direction, old_grad, residual, block_pairs, depth_band, station_offsets):
    cell_index = jnp.arange(CELLS, dtype=jnp.int32)
    column = cell_index % C_DEV % (COL_SIDE * COL_SIDE)
    cell_across = ((column % COL_SIDE).astype(jnp.float32) + 0.5) / COL_SIDE + (cell_index // C_DEV).astype(jnp.float32)
    cell_along = ((column // COL_SIDE).astype(jnp.float32) + 0.5) / COL_SIDE
    cell_depth = (depth_band.astype(jnp.float32) + 0.5) * (DEPTH_RANGE / BANDS)
    weight = (cell_depth + DEPTH_SHIFT) ** 1.5
    station_index = jnp.arange(STATIONS, dtype=jnp.int32)
    station_across = station_offsets[0] + (station_index // S_DEV).astype(jnp.float32)
    station_along = station_offsets[1]
    kernel_scale = 2.0 / math.sqrt(C_DEV)
    cell_blocks = C_DEV // CBLOCK
    block_rows = jnp.arange(PAIR_ROWS, dtype=jnp.int32)

    def block_matrix(row_id, code_value):
        tile_id = row_id // (S_DEV // SBLOCK)
        target = tile_id + code_value // cell_blocks - REACH
        inside = jnp.logical_and(target >= 0, target < N_TILE).astype(jnp.float32)
        cell_start = (jnp.clip(target, 0, N_TILE - 1) * C_DEV + code_value % cell_blocks * CBLOCK).astype(jnp.int32)
        station_start = (row_id * SBLOCK).astype(jnp.int32)
        matrix = point_kernel(lax.dynamic_slice_in_dim(station_across, station_start, SBLOCK), lax.dynamic_slice_in_dim(station_along, station_start, SBLOCK), lax.dynamic_slice_in_dim(cell_across, cell_start, CBLOCK), lax.dynamic_slice_in_dim(cell_along, cell_start, CBLOCK), lax.dynamic_slice_in_dim(cell_depth, cell_start, CBLOCK))
        return (matrix * (kernel_scale * inside), cell_start)
    weighted = weight[None, :] * direction

    def forward_row(row_id):

        def add_pair(running, code_value):
            built = block_matrix(row_id, code_value)
            values = lax.dynamic_slice_in_dim(weighted, built[1], CBLOCK, 1)
            return (running + jnp.dot(values, built[0].T, precision=HIGHEST, preferred_element_type=jnp.float32), None)
        result, unused = lax.scan(add_pair, jnp.zeros((E, SBLOCK), jnp.float32), block_pairs[row_id])
        return result
    image_blocks = lax.map(forward_row, block_rows)
    image_data = jnp.transpose(image_blocks, (1, 0, 2)).reshape(E, STATIONS)

    def adjoint(values):

        def per_row(accumulated, row_id):
            station_values = lax.dynamic_slice_in_dim(values, (row_id * SBLOCK).astype(jnp.int32), SBLOCK, 1)

            def add_pair(running, code_value):
                built = block_matrix(row_id, code_value)
                contribution = jnp.dot(station_values, built[0], precision=HIGHEST, preferred_element_type=jnp.float32)
                current = lax.dynamic_slice_in_dim(running, built[1], CBLOCK, 1)
                return (lax.dynamic_update_slice_in_dim(running, current + contribution, built[1], 1), None)
            accumulated, unused = lax.scan(add_pair, accumulated, block_pairs[row_id])
            return (accumulated, None)
        accumulated, unused = lax.scan(per_row, jnp.zeros((E, CELLS), jnp.float32), block_rows)
        return weight[None, :] * accumulated
    gamma_old = jnp.sum(old_grad * old_grad)
    curvature = jnp.sum(image_data * image_data) + DAMPING * jnp.sum(direction * direction)
    step_length = gamma_old / (curvature + GUARD)
    new_model = model_field + step_length * direction
    new_residual = residual - step_length * image_data
    gradient = adjoint(new_residual) - DAMPING * new_model
    gamma_new = jnp.sum(gradient * gradient)
    new_direction = gradient + gamma_new / (gamma_old + GUARD) * direction
    return (new_model, new_residual, new_direction)
```

```python
import functools
import math

import jax
import jax.numpy as jnp
from jax import lax
from jax.experimental import pallas as pl
from jax.experimental.pallas import tpu as pltpu
from jax.sharding import PartitionSpec as P

CBLOCK = 512
SBLOCK = 256
REACH = 2
BANDS = 16
COL_SIDE = 32
DEPTH_RANGE = 2.0
DEPTH_SHIFT = 0.25
DAMPING = 1.0
GUARD = 1e-06

F32 = jnp.float32
BF16 = jnp.bfloat16
SLOTS = 2 * REACH + 1
LANES = 128

SMEM = pl.BlockSpec(memory_space=pltpu.SMEM)
VMEM = pl.BlockSpec(memory_space=pltpu.VMEM)


def params():
    return pltpu.CompilerParams(vmem_limit_bytes=48 * 2**20)


def split(values):
    high = values.astype(BF16)
    return high, (values - high.astype(F32)).astype(BF16)


def dot(left, right):
    return jnp.dot(left, right, preferred_element_type=F32)


def prepare_kernel(scale, band_ref, band_row_ref, direction_ref, old_ref, values_ref, cells_ref, turned_ref, sums_ref):
    blocks = values_ref.shape[0]
    epochs = direction_ref.shape[0]
    depth = (band_ref[...].astype(F32) + 0.5) * (DEPTH_RANGE / BANDS)
    turned_ref[...] = (depth * depth).T

    def block(w, sums):
        at = pl.ds(pl.multiple_of(w * CBLOCK, CBLOCK), CBLOCK)
        row = (band_row_ref[:, at].astype(F32) + 0.5) * (DEPTH_RANGE / BANDS)
        shifted = row + DEPTH_SHIFT
        factor = row * scale * (shifted * jnp.sqrt(shifted))
        cells_ref[pl.ds(0, 1), at] = row * row
        cells_ref[pl.ds(1, 1), at] = factor
        values = direction_ref[:, at]
        old = old_ref[:, at]
        high, low = split(values * factor)
        values_ref[w, pl.ds(0, epochs), :] = high
        values_ref[w, pl.ds(epochs, epochs), :] = low
        return sums[0] + old * old, sums[1] + values * values

    zero = jnp.zeros((epochs, CBLOCK), F32)
    old_sum, direction_sum = lax.fori_loop(0, blocks, block, (zero, zero), unroll=2)
    sums_ref[pl.ds(0, 1), :] = jnp.broadcast_to(jnp.sum(old_sum).reshape(1, 1), (1, LANES))
    sums_ref[pl.ds(1, 1), :] = jnp.broadcast_to(jnp.sum(direction_sum).reshape(1, 1), (1, LANES))


def prepare(scale, depth_band, direction, old_grad):
    epochs, cells = direction.shape
    blocks = cells // CBLOCK
    return pl.pallas_call(
        functools.partial(prepare_kernel, scale),
        out_shape=(
            jax.ShapeDtypeStruct((blocks, 2 * epochs, CBLOCK), BF16),
            jax.ShapeDtypeStruct((2, cells), F32),
            jax.ShapeDtypeStruct((cells // LANES, LANES), F32),
            jax.ShapeDtypeStruct((2, LANES), F32),
        ),
        in_specs=[VMEM] * 4,
        out_specs=(VMEM,) * 4,
        compiler_params=params(),
        cost_estimate=pl.CostEstimate(flops=8 * epochs * cells, bytes_accessed=12 * epochs * cells, transcendentals=0),
        name="prepare",
    )(depth_band.reshape(cells // LANES, LANES), depth_band.reshape(1, cells), direction, old_grad)


def list_pairs(slot, first_ref, codes_ref, list_ref, count, cell_blocks, station_blocks, pairs):
    first = first_ref[slot]
    for i in range(station_blocks * pairs):
        within = codes_ref[2, i].astype(jnp.int32) - first
        hit = jnp.logical_and(within >= 0, within < cell_blocks)
        list_ref[count] = (slot * station_blocks + i // pairs) * cell_blocks + within
        count = count + hit.astype(jnp.int32)
    return count


def pipelined(count, build, multiply, buffers):
    (high0, low0), (high1, low1) = buffers

    def step(j, unused):
        build(2 * j + 1, high1, low1)
        multiply(2 * j, high0, low0)
        build(2 * j + 2, high0, low0)
        multiply(2 * j + 1, high1, low1)
        return 0

    build(0, high0, low0)
    lax.fori_loop(0, (count + 1) // 2, step, 0)


def inverse_cube(squared):
    return lax.rsqrt(squared * squared * squared)


def forward_kernel(sizes, first_ref, shift_ref, *refs):
    cell_blocks, station_blocks, pairs, epochs, slots = sizes
    codes = refs[:slots]
    messages = refs[slots : 2 * slots]
    values_ref, turned_ref = refs[2 * slots : 2 * slots + 2]
    images = refs[2 * slots + 2 : 3 * slots + 2]
    list_ref, count_ref = refs[3 * slots + 2 : 3 * slots + 4]
    across_ref, along_ref, image_ref, high0, low0, high1, low1 = refs[3 * slots + 4 :]
    dummy = slots * station_blocks
    across_ref[pl.ds(dummy, 1), :] = jnp.zeros((1, SBLOCK), F32)
    along_ref[pl.ds(dummy, 1), :] = jnp.zeros((1, SBLOCK), F32)
    image_ref[...] = jnp.zeros_like(image_ref)
    count = jnp.int32(0)
    for slot in range(slots):
        for q in range(station_blocks):
            at = pl.ds(q * SBLOCK, SBLOCK)
            row = pl.ds(slot * station_blocks + q, 1)
            across_ref[row, :] = messages[slot][pl.ds(0, 1), at] + shift_ref[slot]
            along_ref[row, :] = messages[slot][pl.ds(1, 1), at]
        count = list_pairs(slot, first_ref, codes[slot], list_ref, count, cell_blocks, station_blocks, pairs)
    for i in range(4):
        list_ref[count + i] = dummy * cell_blocks
    count_ref[0] = count
    column = lax.broadcasted_iota(jnp.int32, (COL_SIDE, SBLOCK), 0).astype(F32)
    column = (column + 0.5) / COL_SIDE
    rows = CBLOCK // COL_SIDE

    def build(i, high_ref, low_ref):
        code = list_ref[i]
        q, w = code // cell_blocks, code % cell_blocks
        across = across_ref[pl.ds(q, 1), :] - column
        across = across * across
        along = along_ref[pl.ds(q, 1), :] - (w % 2).astype(F32) * (rows / COL_SIDE)
        turned = pltpu.roll(turned_ref[...], (LANES - w * (CBLOCK // LANES)) % LANES, 1)
        for y in range(rows):
            part = (y * COL_SIDE) // LANES
            at = (y * COL_SIDE) % LANES
            depth = jnp.broadcast_to(turned[at : at + COL_SIDE, part : part + 1], (COL_SIDE, SBLOCK))
            gap = along - (y + 0.5) / COL_SIDE
            high, low = split(inverse_cube((across + gap * gap) + depth))
            high_ref[pl.ds(y * COL_SIDE, COL_SIDE), :] = high
            low_ref[pl.ds(y * COL_SIDE, COL_SIDE), :] = low

    def multiply(i, high_ref, low_ref):
        code = list_ref[i]
        q, w = code // cell_blocks, code % cell_blocks
        values = values_ref[w]
        first = dot(values, high_ref[...])
        second = dot(values[:epochs], low_ref[...])
        image_ref[q] += first[:epochs] + first[epochs:] + second

    pipelined(count, build, multiply, ((high0, low0), (high1, low1)))
    for slot in range(slots):
        images[slot][...] = image_ref[pl.ds(slot * station_blocks, station_blocks)]


def forward(sizes, first, shift, messages, values, turned):
    cell_blocks, station_blocks, pairs, epochs, slots = sizes
    kernel_matrix = pltpu.VMEM((CBLOCK, SBLOCK), BF16)
    head = pl.BlockSpec((8, LANES), lambda i: (0, 0), memory_space=pltpu.SMEM)
    rows = (slots * station_blocks + 8) // 8 * 8
    return pl.pallas_call(
        functools.partial(forward_kernel, sizes),
        out_shape=(jax.ShapeDtypeStruct((station_blocks, epochs, SBLOCK), F32),) * slots
        + (
            jax.ShapeDtypeStruct((slots * station_blocks * pairs + 8,), jnp.int32),
            jax.ShapeDtypeStruct((1,), jnp.int32),
        ),
        grid=(1,),
        in_specs=[SMEM, SMEM] + [head] * slots + [VMEM] * (slots + 2),
        out_specs=(VMEM,) * slots + (SMEM, SMEM),
        scratch_shapes=[
            pltpu.VMEM((rows, SBLOCK), F32),
            pltpu.VMEM((rows, SBLOCK), F32),
            pltpu.VMEM((slots * station_blocks + 1, epochs, SBLOCK), F32),
        ]
        + [kernel_matrix] * 4,
        compiler_params=params(),
        cost_estimate=pl.CostEstimate(flops=5 * 10**9, bytes_accessed=2 * 10**6, transcendentals=8 * 10**6),
        name="forward",
    )(first, shift, *messages, *messages, values, turned)


def adjoint_kernel(sizes, list_ref, count_ref, shift_ref, *refs):
    cell_blocks, station_blocks, pairs, epochs, slots = sizes
    messages = refs[:slots]
    images = refs[slots : 2 * slots]
    cells_ref, model_ref, direction_ref, sums_ref = refs[2 * slots : 2 * slots + 4]
    constant_ref, slope_ref, stats_ref = refs[2 * slots + 4 : 2 * slots + 7]
    stations_ref, terms_ref, total_ref, high0, low0, high1, low1 = refs[2 * slots + 7 :]
    dummy = slots * station_blocks
    terms_ref[dummy] = jnp.zeros(terms_ref.shape[1:], BF16)
    stations_ref[slots] = jnp.zeros(stations_ref.shape[1:], F32)
    total_ref[...] = jnp.zeros_like(total_ref)
    per_block = SBLOCK // LANES
    lane_rows = station_blocks * per_block
    for slot in range(slots):
        parts = [messages[slot][pl.ds(0, 1), pl.ds(i * LANES, LANES)] + shift_ref[slot] for i in range(lane_rows)]
        parts += [messages[slot][pl.ds(1, 1), pl.ds(i * LANES, LANES)] for i in range(lane_rows)]
        parts.append(jnp.zeros((LANES - 2 * lane_rows, LANES), F32))
        stations_ref[slot] = jnp.concatenate(parts, axis=0).T
        for q in range(station_blocks):
            stacked = jnp.concatenate(
                [messages[slot][pl.ds(8, epochs), pl.ds(q * SBLOCK, SBLOCK)], images[slot][q]], axis=0
            )
            high, low = split(stacked)
            terms_ref[slot * station_blocks + q, pl.ds(0, 2 * epochs), :] = high
            terms_ref[slot * station_blocks + q, pl.ds(2 * epochs, 2 * epochs), :] = low
    lane = lax.broadcasted_iota(jnp.int32, (16, LANES), 1)
    column = ((lane % COL_SIDE).astype(F32) + 0.5) / COL_SIDE
    line = ((lane // COL_SIDE).astype(F32) + 0.5) / COL_SIDE
    rows = CBLOCK // COL_SIDE
    chunks = CBLOCK // LANES

    def build(i, high_ref, low_ref):
        code = list_ref[i]
        q, w = code // cell_blocks, code % cell_blocks
        slot, within = q // station_blocks, q % station_blocks
        at_cells = pl.ds(pl.multiple_of(w * CBLOCK, CBLOCK), CBLOCK)
        depth = cells_ref[pl.ds(0, 1), at_cells]
        half = (w % 2).astype(F32) * (rows / COL_SIDE)
        stations = pltpu.roll(stations_ref[slot], (LANES - within * per_block) % LANES, 1)
        for part in range(per_block):
            for at in range(0, LANES, 16):
                across = jnp.broadcast_to(stations[at : at + 16, part : part + 1], (16, LANES)) - column
                across = across * across
                part_along = lane_rows + part
                along = jnp.broadcast_to(stations[at : at + 16, part_along : part_along + 1], (16, LANES))
                along = along - (line + half)
                for chunk in range(chunks):
                    gap = along - chunk * (LANES // COL_SIDE) / COL_SIDE
                    squared = (across + gap * gap) + depth[:, chunk * LANES : (chunk + 1) * LANES]
                    high, low = split(inverse_cube(squared))
                    place = (pl.ds(part * LANES + at, 16), pl.ds(chunk * LANES, LANES))
                    high_ref[place] = high
                    low_ref[place] = low

    def multiply(i, high_ref, low_ref):
        code = list_ref[i]
        q, w = code // cell_blocks, code % cell_blocks
        terms = terms_ref[q]
        first = dot(terms, high_ref[...])
        second = dot(terms[: 2 * epochs], low_ref[...])
        total_ref[w] += first[: 2 * epochs] + first[2 * epochs :] + second

    pipelined(count_ref[0], build, multiply, ((high0, low0), (high1, low1)))

    zero = jnp.zeros((epochs, CBLOCK), F32)

    def combine(w, sums):
        at = pl.ds(pl.multiple_of(w * CBLOCK, CBLOCK), CBLOCK)
        total = total_ref[w] * cells_ref[pl.ds(1, 1), at]
        constant = total[:epochs] - DAMPING * model_ref[:, at]
        slope = total[epochs:] + DAMPING * direction_ref[:, at]
        constant_ref[:, at] = constant
        slope_ref[:, at] = slope
        return sums[0] + constant * slope, sums[1] + slope * slope

    cross, square = lax.fori_loop(0, cell_blocks, combine, (zero, zero), unroll=2)
    square = jnp.sum(square).reshape(1, 1)
    cross = jnp.sum(cross).reshape(1, 1)
    local_step = jnp.where(square > 0, cross / jnp.where(square > 0, square, 1.0), 0.0)

    def remainder(w, sums):
        at = pl.ds(pl.multiple_of(w * CBLOCK, CBLOCK), CBLOCK)
        slope = slope_ref[:, at]
        left = constant_ref[:, at] - local_step * slope
        return sums[0] + left * left, sums[1] + left * slope

    left_square, left_cross = lax.fori_loop(0, cell_blocks, remainder, (zero, zero), unroll=2)
    image = images[0][...]
    stats = [
        sums_ref[pl.ds(0, 1), pl.ds(0, 1)],
        sums_ref[pl.ds(1, 1), pl.ds(0, 1)],
        jnp.sum(image * image).reshape(1, 1),
        local_step,
        jnp.sum(left_square).reshape(1, 1),
        jnp.sum(left_cross).reshape(1, 1),
        jnp.sqrt(square),
        jnp.zeros((1, 1), F32),
    ]
    stats = jnp.concatenate([jnp.broadcast_to(value, (1, LANES)) for value in stats], axis=0)
    for i in range(stats_ref.shape[0]):
        stats_ref[i] = stats


def adjoint(sizes, ranks, pair_list, count, shift, messages, images, cell_rows, model_field, direction, sums):
    cell_blocks, station_blocks, pairs, epochs, slots = sizes
    kernel_matrix = pltpu.VMEM((SBLOCK, CBLOCK), BF16)
    return pl.pallas_call(
        functools.partial(adjoint_kernel, sizes),
        out_shape=(
            jax.ShapeDtypeStruct(model_field.shape, F32),
            jax.ShapeDtypeStruct(model_field.shape, F32),
            jax.ShapeDtypeStruct((ranks, 8, LANES), F32),
        ),
        in_specs=[SMEM] * 3 + [VMEM] * (2 * slots + 4),
        out_specs=(VMEM,) * 3,
        scratch_shapes=[
            pltpu.VMEM((slots + 1, LANES, LANES), F32),
            pltpu.VMEM((slots * station_blocks + 1, 4 * epochs, SBLOCK), BF16),
            pltpu.VMEM((cell_blocks, 2 * epochs, CBLOCK), F32),
        ]
        + [kernel_matrix] * 4,
        compiler_params=params(),
        cost_estimate=pl.CostEstimate(flops=5 * 10**9, bytes_accessed=6 * 10**6, transcendentals=8 * 10**6),
        name="adjoint",
    )(pair_list, count, shift, *messages, *images, cell_rows, model_field, direction, sums)


def finish_kernel(
    stats_ref, constant_ref, slope_ref, model_ref, direction_ref, residual_ref, image_ref, model_out, residual_out, direction_out
):
    totals = jnp.sum(stats_ref[...], axis=0)[:, :1]
    gamma_old = totals[0:1]
    step = gamma_old / (totals[2:3] + DAMPING * totals[1:2] + GUARD)
    stats = stats_ref[...]
    ahead = step[None] - stats[:, 3:4, :]
    reach = ahead * stats[:, 6:7, :]
    gamma_new = jnp.sum(stats[:, 4:5, :] - 2.0 * ahead * stats[:, 5:6, :] + reach * reach, axis=0)[:, :1]
    ratio = gamma_new / (gamma_old + GUARD)
    blocks = model_ref.shape[1] // CBLOCK

    def block(w, unused):
        at = pl.ds(pl.multiple_of(w * CBLOCK, CBLOCK), CBLOCK)
        direction = direction_ref[:, at]
        model_out[:, at] = model_ref[:, at] + step * direction
        direction_out[:, at] = (constant_ref[:, at] - step * slope_ref[:, at]) + ratio * direction
        return 0

    lax.fori_loop(0, blocks, block, 0, unroll=2)
    for q in range(image_ref.shape[0]):
        at = pl.ds(q * SBLOCK, SBLOCK)
        residual_out[:, at] = residual_ref[:, at] - step * image_ref[q]


def finish(stats, constant, slope, model_field, direction, residual, image):
    return pl.pallas_call(
        finish_kernel,
        out_shape=(
            jax.ShapeDtypeStruct(model_field.shape, F32),
            jax.ShapeDtypeStruct(residual.shape, F32),
            jax.ShapeDtypeStruct(direction.shape, F32),
        ),
        in_specs=[VMEM] * 7,
        out_specs=(VMEM,) * 3,
        compiler_params=params(),
        name="finish",
    )(stats, constant, slope, model_field, direction, residual, image)


def shards(model_field, direction, old_grad, residual, block_pairs, depth_band, station_offsets):
    ranks = lax.axis_size("tile")
    tile_id = lax.axis_index("tile")
    epochs, cells = model_field.shape
    stations = residual.shape[1]
    station_blocks, pairs = block_pairs.shape
    cell_blocks = cells // CBLOCK
    sizes = (cell_blocks, station_blocks, pairs, epochs, SLOTS)
    side = 2 * (tile_id % 2) - 1

    def to_partner(array):
        return lax.ppermute(array, "tile", [(i, i ^ 1) for i in range(ranks)])

    def across(array):
        ends = [(i, i + 1) for i in range(1, ranks - 1, 2)]
        return lax.ppermute(array, "tile", ends + [(j, i) for i, j in ends])

    codes = jnp.pad(block_pairs.reshape(1, -1).astype(F32) + 1.0, ((0, 0), (0, stations - station_blocks * pairs)))
    own = jnp.concatenate([station_offsets, codes, jnp.zeros((5, stations), F32), residual], axis=0)
    partner = to_partner(own)
    arrived = across(jnp.stack([own, partner]))
    first_far, second_far = arrived[0], arrived[1]
    third_far = to_partner(first_far)
    messages = [own, partner, first_far, second_far, third_far]
    offsets = jnp.stack([0 * side, -side, side, 2 * side, -2 * side]).astype(jnp.int32)
    first_code = cell_blocks * (REACH - offsets) + 1
    shift = offsets.astype(F32)

    values, cell_rows, turned, sums = prepare(2.0 / math.sqrt(cells), depth_band, direction, old_grad)
    outs = forward(sizes, first_code, shift, messages, values, turned)
    partials, (pair_list, count) = outs[:SLOTS], outs[SLOTS:]

    near = partials[2] + to_partner(partials[4])
    given = across(jnp.stack([near, partials[3]]))
    image = partials[0] + given[0] + to_partner(partials[1] + given[1])

    partner_image = to_partner(image)
    arrived = across(jnp.stack([image, partner_image]))
    images = [image, partner_image, arrived[0], arrived[1], to_partner(arrived[0])]

    constant, slope, stats = adjoint(
        sizes, ranks, pair_list, count, shift, messages, images, cell_rows, model_field, direction, sums
    )
    stats = lax.all_to_all(stats, "tile", 0, 0)
    return finish(stats, constant, slope, model_field, direction, residual, image)


def solution(mesh):
    wide = P(None, ("groups", "tile"))
    return jax.shard_map(
        shards,
        mesh=mesh,
        in_specs=(wide, wide, wide, wide, P(("groups", "tile"), None), P(("groups", "tile")), wide),
        out_specs=(wide, wide, wide),
        check_vma=False,
    )
```

```python
import functools
import math

import jax
import jax.numpy as jnp
from jax import lax
from jax.experimental import pallas as pl
from jax.experimental.pallas import tpu as pltpu
from jax.sharding import PartitionSpec as P

CBLOCK = 512
SBLOCK = 256
REACH = 2
BANDS = 16
COL_SIDE = 32
DEPTH_RANGE = 2.0
DEPTH_SHIFT = 0.25
DAMPING = 1.0
GUARD = 1e-06

F32 = jnp.float32
BF16 = jnp.bfloat16
SLOTS = 2 * REACH + 1
LANES = 128
TILE = 256
HALF = TILE // 2

SMEM = pl.BlockSpec(memory_space=pltpu.SMEM)
VMEM = pl.BlockSpec(memory_space=pltpu.VMEM)


def params():
    return pltpu.CompilerParams(vmem_limit_bytes=48 * 2**20)


def split(values):
    high = values.astype(BF16)
    return high, (values - high.astype(F32)).astype(BF16)


def dot(left, right):
    return jnp.dot(left, right, preferred_element_type=F32)


def prepare_kernel(scale, band_ref, band_row_ref, direction_ref, old_ref, values_ref, cells_ref, turned_ref, sums_ref):
    blocks = values_ref.shape[0]
    epochs = direction_ref.shape[0]
    depth = (band_ref[...].astype(F32) + 0.5) * (DEPTH_RANGE / BANDS)
    turned_ref[...] = (depth * depth).T

    def block(w, sums):
        at = pl.ds(pl.multiple_of(w * CBLOCK, CBLOCK), CBLOCK)
        row = (band_row_ref[:, at].astype(F32) + 0.5) * (DEPTH_RANGE / BANDS)
        shifted = row + DEPTH_SHIFT
        factor = row * scale * (shifted * jnp.sqrt(shifted))
        cells_ref[pl.ds(0, 1), at] = row * row
        cells_ref[pl.ds(1, 1), at] = factor
        values = direction_ref[:, at]
        old = old_ref[:, at]
        high, low = split(values * factor)
        values_ref[w, pl.ds(0, epochs), :] = high
        values_ref[w, pl.ds(epochs, epochs), :] = low
        return sums[0] + old * old, sums[1] + values * values

    zero = jnp.zeros((epochs, CBLOCK), F32)
    old_sum, direction_sum = lax.fori_loop(0, blocks, block, (zero, zero), unroll=2)
    sums_ref[pl.ds(0, 1), :] = jnp.broadcast_to(jnp.sum(old_sum).reshape(1, 1), (1, LANES))
    sums_ref[pl.ds(1, 1), :] = jnp.broadcast_to(jnp.sum(direction_sum).reshape(1, 1), (1, LANES))


def prepare(scale, depth_band, direction, old_grad):
    epochs, cells = direction.shape
    blocks = cells // CBLOCK
    return pl.pallas_call(
        functools.partial(prepare_kernel, scale),
        out_shape=(
            jax.ShapeDtypeStruct((blocks, 2 * epochs, CBLOCK), BF16),
            jax.ShapeDtypeStruct((2, cells), F32),
            jax.ShapeDtypeStruct((cells // LANES, LANES), F32),
            jax.ShapeDtypeStruct((2, LANES), F32),
        ),
        in_specs=[VMEM] * 4,
        out_specs=(VMEM,) * 4,
        compiler_params=params(),
        cost_estimate=pl.CostEstimate(flops=8 * epochs * cells, bytes_accessed=12 * epochs * cells, transcendentals=0),
        name="prepare",
    )(depth_band.reshape(cells // LANES, LANES), depth_band.reshape(1, cells), direction, old_grad)


def list_pairs(slot, first_ref, codes_ref, list_ref, count, cell_blocks, station_blocks, pairs):
    first = first_ref[slot]
    for i in range(station_blocks * pairs):
        within = codes_ref[2, i].astype(jnp.int32) - first
        hit = jnp.logical_and(within >= 0, within < cell_blocks)
        list_ref[count] = (slot * station_blocks + i // pairs) * cell_blocks + within
        count = count + hit.astype(jnp.int32)
    return count


UNROLL = 4


def pipelined(count, stage, issue, collect):
    stage(0, 0)
    stage(1, 1)
    issue(0, 0)

    def step(j, unused):
        for k in range(UNROLL):
            i, now, later = UNROLL * j + k, k % 2, 1 - k % 2
            issue(i + 1, later)
            stage(i + 2, now)
            collect(i, now)
        return 0

    rounds = (count + UNROLL - 1) // UNROLL
    lax.fori_loop(0, rounds, step, 0)
    collect(UNROLL * rounds, 0)


def multiply_add(sums_ref, left, pieces, unit, register):
    high, low = zip(*pieces)
    pltpu.matmul_push_rhs(jnp.concatenate(high + low, axis=0), register, unit)
    pltpu.matmul_acc_lhs(sums_ref, jnp.concatenate([left, left], axis=1), load_staged_rhs=register)


def accumulators(rows):
    return [pltpu.ACC(unit)((rows, TILE), F32) for unit in (0, 1)] * 2


def inverse_cube(squared):
    return lax.rsqrt(squared * squared * squared)


def forward_kernel(sizes, first_ref, shift_ref, *refs):
    cell_blocks, station_blocks, pairs, epochs, slots = sizes
    codes = refs[:slots]
    messages = refs[slots : 2 * slots]
    values_ref, turned_ref = refs[2 * slots : 2 * slots + 2]
    images = refs[2 * slots + 2 : 3 * slots + 2]
    list_ref, count_ref = refs[3 * slots + 2 : 3 * slots + 4]
    across_ref, along_ref, image_ref, gaps_ref, lines_ref, depths_ref = refs[3 * slots + 4 :]
    dummy = slots * station_blocks
    across_ref[pl.ds(dummy, 1), :] = jnp.zeros((1, SBLOCK), F32)
    along_ref[pl.ds(dummy, 1), :] = jnp.zeros((1, SBLOCK), F32)
    image_ref[...] = jnp.zeros_like(image_ref)
    count = jnp.int32(0)
    for slot in range(slots):
        for q in range(station_blocks):
            at = pl.ds(q * SBLOCK, SBLOCK)
            row = pl.ds(slot * station_blocks + q, 1)
            across_ref[row, :] = messages[slot][pl.ds(0, 1), at] + shift_ref[slot]
            along_ref[row, :] = messages[slot][pl.ds(1, 1), at]
        count = list_pairs(slot, first_ref, codes[slot], list_ref, count, cell_blocks, station_blocks, pairs)
    for i in range(UNROLL + 4):
        list_ref[count + i] = dummy * cell_blocks
    count_ref[0] = count
    column = lax.broadcasted_iota(jnp.int32, (COL_SIDE, SBLOCK), 0).astype(F32)
    column = (column + 0.5) / COL_SIDE
    rows = CBLOCK // COL_SIDE

    def stage(i, k):
        code = list_ref[i]
        q, w = code // cell_blocks, code % cell_blocks
        across = across_ref[pl.ds(q, 1), :] - column
        gaps_ref[k] = across * across
        lines_ref[k] = along_ref[pl.ds(q, 1), :] - (w % 2).astype(F32) * (rows / COL_SIDE)
        turned = pltpu.roll(turned_ref[...], (LANES - w * (CBLOCK // LANES)) % LANES, 1)
        for part in range(CBLOCK // LANES):
            depths_ref[k, pl.ds(part * LANES, LANES), :] = jnp.broadcast_to(turned[:, part : part + 1], (LANES, LANES))

    def issue(sums, i, k):
        w = list_ref[i] % cell_blocks
        across = gaps_ref[k]
        along = lines_ref[k]
        for tile in range(CBLOCK // HALF):
            pieces = []
            for at in range(0, HALF, COL_SIDE):
                y = (tile * HALF + at) // COL_SIDE
                depth = depths_ref[k, pl.ds(y * COL_SIDE, COL_SIDE), :]
                depth = jnp.concatenate([depth] * (SBLOCK // LANES), axis=1)
                gap = along - (y + 0.5) / COL_SIDE
                pieces.append(split(inverse_cube((across + gap * gap) + depth)))
            left = values_ref[w, :, pl.ds(tile * HALF, HALF)]
            multiply_add(sums[2 * k + tile % 2], left, pieces, tile % 2, tile // 2)

    def collect(sums, i, k):
        q = list_ref[i] // cell_blocks
        both = pltpu.matmul_pop(sums[2 * k]) + pltpu.matmul_pop(sums[2 * k + 1])
        image_ref[q] += both[:epochs] + both[epochs:]

    def run(*sums):
        pipelined(count, stage, functools.partial(issue, sums), functools.partial(collect, sums))

    pl.run_scoped(run, *accumulators(2 * epochs))
    for slot in range(slots):
        images[slot][...] = image_ref[pl.ds(slot * station_blocks, station_blocks)]


def forward(sizes, first, shift, messages, values, turned):
    cell_blocks, station_blocks, pairs, epochs, slots = sizes
    head = pl.BlockSpec((8, LANES), lambda i: (0, 0), memory_space=pltpu.SMEM)
    rows = (slots * station_blocks + 8) // 8 * 8
    return pl.pallas_call(
        functools.partial(forward_kernel, sizes),
        out_shape=(jax.ShapeDtypeStruct((station_blocks, epochs, SBLOCK), F32),) * slots
        + (
            jax.ShapeDtypeStruct((slots * station_blocks * pairs + 16,), jnp.int32),
            jax.ShapeDtypeStruct((1,), jnp.int32),
        ),
        grid=(1,),
        in_specs=[SMEM, SMEM] + [head] * slots + [VMEM] * (slots + 2),
        out_specs=(VMEM,) * slots + (SMEM, SMEM),
        scratch_shapes=[
            pltpu.VMEM((rows, SBLOCK), F32),
            pltpu.VMEM((rows, SBLOCK), F32),
            pltpu.VMEM((slots * station_blocks + 1, epochs, SBLOCK), F32),
            pltpu.VMEM((2, COL_SIDE, SBLOCK), F32),
            pltpu.VMEM((2, 1, SBLOCK), F32),
            pltpu.VMEM((2, CBLOCK, LANES), F32),
        ],
        compiler_params=params(),
        cost_estimate=pl.CostEstimate(flops=5 * 10**9, bytes_accessed=2 * 10**6, transcendentals=8 * 10**6),
        name="forward",
    )(first, shift, *messages, *messages, values, turned)


def adjoint_kernel(sizes, list_ref, count_ref, shift_ref, *refs):
    cell_blocks, station_blocks, pairs, epochs, slots = sizes
    messages = refs[:slots]
    images = refs[slots : 2 * slots]
    cells_ref, model_ref, direction_ref, sums_ref = refs[2 * slots : 2 * slots + 4]
    constant_ref, slope_ref, stats_ref = refs[2 * slots + 4 : 2 * slots + 7]
    stations_ref, terms_ref, total_ref, depths_ref, gaps_ref, lines_ref = refs[2 * slots + 7 :]
    dummy = slots * station_blocks
    terms_ref[dummy] = jnp.zeros(terms_ref.shape[1:], BF16)
    stations_ref[slots] = jnp.zeros(stations_ref.shape[1:], F32)
    total_ref[...] = jnp.zeros_like(total_ref)
    per_block = SBLOCK // LANES
    lane_rows = station_blocks * per_block
    for slot in range(slots):
        parts = [messages[slot][pl.ds(0, 1), pl.ds(i * LANES, LANES)] + shift_ref[slot] for i in range(lane_rows)]
        parts += [messages[slot][pl.ds(1, 1), pl.ds(i * LANES, LANES)] for i in range(lane_rows)]
        parts.append(jnp.zeros((LANES - 2 * lane_rows, LANES), F32))
        stations_ref[slot] = jnp.concatenate(parts, axis=0).T
        for q in range(station_blocks):
            stacked = jnp.concatenate(
                [messages[slot][pl.ds(8, epochs), pl.ds(q * SBLOCK, SBLOCK)], images[slot][q]], axis=0
            )
            high, low = split(stacked)
            terms_ref[slot * station_blocks + q, pl.ds(0, 2 * epochs), :] = high
            terms_ref[slot * station_blocks + q, pl.ds(2 * epochs, 2 * epochs), :] = low
    lane = lax.broadcasted_iota(jnp.int32, (1, LANES), 1)
    column = ((lane % COL_SIDE).astype(F32) + 0.5) / COL_SIDE
    line = ((lane // COL_SIDE).astype(F32) + 0.5) / COL_SIDE
    rows = CBLOCK // COL_SIDE
    chunks = CBLOCK // LANES

    def stage(i, k):
        code = list_ref[i]
        q, w = code // cell_blocks, code % cell_blocks
        slot, within = q // station_blocks, q % station_blocks
        depths_ref[k] = cells_ref[pl.ds(0, 1), pl.ds(pl.multiple_of(w * CBLOCK, CBLOCK), CBLOCK)]
        lines = line + (w % 2).astype(F32) * (rows / COL_SIDE)
        places = pltpu.roll(stations_ref[slot], (LANES - within * per_block) % LANES, 1)
        for part in range(per_block):
            at = pl.ds(part * LANES, LANES)
            across = jnp.broadcast_to(places[:, part : part + 1], (LANES, LANES)) - column
            gaps_ref[k, at, :] = across * across
            along = jnp.broadcast_to(places[:, lane_rows + part : lane_rows + part + 1], (LANES, LANES))
            lines_ref[k, at, :] = along - lines

    def issue(sums, i, k):
        q = list_ref[i] // cell_blocks
        depth = depths_ref[k]
        for part in range(per_block):
            pieces = ([], [])
            for at in range(part * LANES, (part + 1) * LANES, 16):
                across = gaps_ref[k, pl.ds(at, 16), :]
                along = lines_ref[k, pl.ds(at, 16), :]
                for unit in range(2):
                    near = []
                    for chunk in range(unit * chunks // 2, (unit + 1) * chunks // 2):
                        gap = along - chunk * (LANES // COL_SIDE) / COL_SIDE
                        squared = (across + gap * gap) + depth[:, chunk * LANES : (chunk + 1) * LANES]
                        near.append(split(inverse_cube(squared)))
                    pieces[unit].append([jnp.concatenate(terms, axis=1) for terms in zip(*near)])
            left = terms_ref[q, :, pl.ds(part * HALF, HALF)]
            for unit in range(2):
                multiply_add(sums[2 * k + unit], left, pieces[unit], unit, part)

    def collect(sums, i, k):
        w = list_ref[i] % cell_blocks
        for unit in range(2):
            both = pltpu.matmul_pop(sums[2 * k + unit])
            total_ref[w, :, pl.ds(unit * TILE, TILE)] += both[: 2 * epochs] + both[2 * epochs :]

    def run(*sums):
        pipelined(count_ref[0], stage, functools.partial(issue, sums), functools.partial(collect, sums))

    pl.run_scoped(run, *accumulators(4 * epochs))

    zero = jnp.zeros((epochs, CBLOCK), F32)

    def combine(w, sums):
        at = pl.ds(pl.multiple_of(w * CBLOCK, CBLOCK), CBLOCK)
        total = total_ref[w] * cells_ref[pl.ds(1, 1), at]
        constant = total[:epochs] - DAMPING * model_ref[:, at]
        slope = total[epochs:] + DAMPING * direction_ref[:, at]
        constant_ref[:, at] = constant
        slope_ref[:, at] = slope
        return sums[0] + constant * slope, sums[1] + slope * slope

    cross, square = lax.fori_loop(0, cell_blocks, combine, (zero, zero), unroll=2)
    square = jnp.sum(square).reshape(1, 1)
    cross = jnp.sum(cross).reshape(1, 1)
    local_step = jnp.where(square > 0, cross / jnp.where(square > 0, square, 1.0), 0.0)

    def remainder(w, sums):
        at = pl.ds(pl.multiple_of(w * CBLOCK, CBLOCK), CBLOCK)
        slope = slope_ref[:, at]
        left = constant_ref[:, at] - local_step * slope
        return sums[0] + left * left, sums[1] + left * slope

    left_square, left_cross = lax.fori_loop(0, cell_blocks, remainder, (zero, zero), unroll=2)
    image = images[0][...]
    stats = [
        sums_ref[pl.ds(0, 1), pl.ds(0, 1)],
        sums_ref[pl.ds(1, 1), pl.ds(0, 1)],
        jnp.sum(image * image).reshape(1, 1),
        local_step,
        jnp.sum(left_square).reshape(1, 1),
        jnp.sum(left_cross).reshape(1, 1),
        jnp.sqrt(square),
        jnp.zeros((1, 1), F32),
    ]
    stats = jnp.concatenate([jnp.broadcast_to(value, (1, LANES)) for value in stats], axis=0)
    for i in range(stats_ref.shape[0]):
        stats_ref[i] = stats


def adjoint(sizes, ranks, pair_list, count, shift, messages, images, cell_rows, model_field, direction, sums):
    cell_blocks, station_blocks, pairs, epochs, slots = sizes
    return pl.pallas_call(
        functools.partial(adjoint_kernel, sizes),
        out_shape=(
            jax.ShapeDtypeStruct(model_field.shape, F32),
            jax.ShapeDtypeStruct(model_field.shape, F32),
            jax.ShapeDtypeStruct((ranks, 8, LANES), F32),
        ),
        in_specs=[SMEM] * 3 + [VMEM] * (2 * slots + 4),
        out_specs=(VMEM,) * 3,
        scratch_shapes=[
            pltpu.VMEM((slots + 1, LANES, LANES), F32),
            pltpu.VMEM((slots * station_blocks + 1, 4 * epochs, SBLOCK), BF16),
            pltpu.VMEM((cell_blocks, 2 * epochs, CBLOCK), F32),
            pltpu.VMEM((2, 1, CBLOCK), F32),
            pltpu.VMEM((2, SBLOCK, LANES), F32),
            pltpu.VMEM((2, SBLOCK, LANES), F32),
        ],
        compiler_params=params(),
        cost_estimate=pl.CostEstimate(flops=5 * 10**9, bytes_accessed=6 * 10**6, transcendentals=8 * 10**6),
        name="adjoint",
    )(pair_list, count, shift, *messages, *images, cell_rows, model_field, direction, sums)


def finish_kernel(
    stats_ref, constant_ref, slope_ref, model_ref, direction_ref, residual_ref, image_ref, model_out, residual_out, direction_out
):
    totals = jnp.sum(stats_ref[...], axis=0)[:, :1]
    gamma_old = totals[0:1]
    step = gamma_old / (totals[2:3] + DAMPING * totals[1:2] + GUARD)
    stats = stats_ref[...]
    ahead = step[None] - stats[:, 3:4, :]
    reach = ahead * stats[:, 6:7, :]
    gamma_new = jnp.sum(stats[:, 4:5, :] - 2.0 * ahead * stats[:, 5:6, :] + reach * reach, axis=0)[:, :1]
    ratio = gamma_new / (gamma_old + GUARD)
    blocks = model_ref.shape[1] // CBLOCK

    def block(w, unused):
        at = pl.ds(pl.multiple_of(w * CBLOCK, CBLOCK), CBLOCK)
        direction = direction_ref[:, at]
        model_out[:, at] = model_ref[:, at] + step * direction
        direction_out[:, at] = (constant_ref[:, at] - step * slope_ref[:, at]) + ratio * direction
        return 0

    lax.fori_loop(0, blocks, block, 0, unroll=2)
    for q in range(image_ref.shape[0]):
        at = pl.ds(q * SBLOCK, SBLOCK)
        residual_out[:, at] = residual_ref[:, at] - step * image_ref[q]


def finish(stats, constant, slope, model_field, direction, residual, image):
    return pl.pallas_call(
        finish_kernel,
        out_shape=(
            jax.ShapeDtypeStruct(model_field.shape, F32),
            jax.ShapeDtypeStruct(residual.shape, F32),
            jax.ShapeDtypeStruct(direction.shape, F32),
        ),
        in_specs=[VMEM] * 7,
        out_specs=(VMEM,) * 3,
        compiler_params=params(),
        name="finish",
    )(stats, constant, slope, model_field, direction, residual, image)


def shards(model_field, direction, old_grad, residual, block_pairs, depth_band, station_offsets):
    ranks = lax.axis_size("tile")
    tile_id = lax.axis_index("tile")
    epochs, cells = model_field.shape
    stations = residual.shape[1]
    station_blocks, pairs = block_pairs.shape
    cell_blocks = cells // CBLOCK
    sizes = (cell_blocks, station_blocks, pairs, epochs, SLOTS)
    side = 2 * (tile_id % 2) - 1

    def to_partner(array):
        return lax.ppermute(array, "tile", [(i, i ^ 1) for i in range(ranks)])

    def across(array):
        ends = [(i, i + 1) for i in range(1, ranks - 1, 2)]
        return lax.ppermute(array, "tile", ends + [(j, i) for i, j in ends])

    codes = jnp.pad(block_pairs.reshape(1, -1).astype(F32) + 1.0, ((0, 0), (0, stations - station_blocks * pairs)))
    own = jnp.concatenate([station_offsets, codes, jnp.zeros((5, stations), F32), residual], axis=0)
    partner = to_partner(own)
    arrived = across(jnp.stack([own, partner]))
    first_far, second_far = arrived[0], arrived[1]
    third_far = to_partner(first_far)
    messages = [own, partner, first_far, second_far, third_far]
    offsets = jnp.stack([0 * side, -side, side, 2 * side, -2 * side]).astype(jnp.int32)
    first_code = cell_blocks * (REACH - offsets) + 1
    shift = offsets.astype(F32)

    values, cell_rows, turned, sums = prepare(2.0 / math.sqrt(cells), depth_band, direction, old_grad)
    outs = forward(sizes, first_code, shift, messages, values, turned)
    partials, (pair_list, count) = outs[:SLOTS], outs[SLOTS:]

    near = partials[2] + to_partner(partials[4])
    given = across(jnp.stack([near, partials[3]]))
    image = partials[0] + given[0] + to_partner(partials[1] + given[1])

    partner_image = to_partner(image)
    arrived = across(jnp.stack([image, partner_image]))
    images = [image, partner_image, arrived[0], arrived[1], to_partner(arrived[0])]

    constant, slope, stats = adjoint(
        sizes, ranks, pair_list, count, shift, messages, images, cell_rows, model_field, direction, sums
    )
    stats = lax.all_to_all(stats, "tile", 0, 0)
    return finish(stats, constant, slope, model_field, direction, residual, image)


def solution(mesh):
    wide = P(None, ("groups", "tile"))
    mapped = jax.shard_map(
        shards,
        mesh=mesh,
        in_specs=(wide, wide, wide, wide, P(("groups", "tile"), None), P(("groups", "tile")), wide),
        out_specs=(wide, wide, wide),
        check_vma=False,
    )

    def step(*arrays):
        with jax.sharding.use_abstract_mesh(mesh.abstract_mesh):
            return mapped(*arrays)

    return step
```

```python
import functools
import math

import jax
import jax.numpy as jnp
from jax import lax
from jax.experimental import pallas as pl
from jax.experimental.pallas import tpu as pltpu
from jax.sharding import PartitionSpec as P

CBLOCK = 512
SBLOCK = 256
REACH = 2
BANDS = 16
COL_SIDE = 32
DEPTH_RANGE = 2.0
DEPTH_SHIFT = 0.25
DAMPING = 1.0
GUARD = 1e-06

F32 = jnp.float32
BF16 = jnp.bfloat16
LANES = 128
TILE = 256
HALF = TILE // 2

SMEM = pl.BlockSpec(memory_space=pltpu.SMEM)
VMEM = pl.BlockSpec(memory_space=pltpu.VMEM)


def params():
    return pltpu.CompilerParams(vmem_limit_bytes=48 * 2**20)


def split(values):
    high = values.astype(BF16)
    return high, (values - high.astype(F32)).astype(BF16)


def dot(left, right):
    return jnp.dot(left, right, preferred_element_type=F32)


def pack_kernel(offsets_ref, pairs_ref, message_ref):
    stations = offsets_ref.shape[1]
    message_ref[...] = jnp.zeros_like(message_ref)
    message_ref[pl.ds(0, 2), pl.ds(0, stations)] = offsets_ref[...]
    message_ref[:, pl.ds(stations, pairs_ref.shape[1])] = pairs_ref[...].astype(F32) + 1.0


def pack(station_offsets, block_pairs):
    rows, stations = block_pairs.shape[0], station_offsets.shape[1]
    return pl.pallas_call(
        pack_kernel,
        out_shape=jax.ShapeDtypeStruct((rows, stations + LANES), F32),
        in_specs=[VMEM] * 2,
        out_specs=VMEM,
        name="pack",
    )(station_offsets, block_pairs)


def prepare_kernel(scale, band_ref, band_row_ref, direction_ref, old_ref, values_ref, cells_ref, turned_ref, sums_ref):
    blocks = values_ref.shape[0]
    epochs = direction_ref.shape[0]
    depth = (band_ref[...].astype(F32) + 0.5) * (DEPTH_RANGE / BANDS)
    turned_ref[...] = (depth * depth).T

    def block(w, sums):
        at = pl.ds(pl.multiple_of(w * CBLOCK, CBLOCK), CBLOCK)
        row = (band_row_ref[:, at].astype(F32) + 0.5) * (DEPTH_RANGE / BANDS)
        shifted = row + DEPTH_SHIFT
        factor = row * scale * (shifted * jnp.sqrt(shifted))
        cells_ref[pl.ds(0, 1), at] = row * row
        cells_ref[pl.ds(1, 1), at] = factor
        values = direction_ref[:, at]
        old = old_ref[:, at]
        high, low = split(values * factor)
        values_ref[w, pl.ds(0, epochs), :] = high
        values_ref[w, pl.ds(epochs, epochs), :] = low
        return sums[0] + old * old, sums[1] + values * values

    zero = jnp.zeros((epochs, CBLOCK), F32)
    old_sum, direction_sum = lax.fori_loop(0, blocks, block, (zero, zero), unroll=2)
    sums_ref[pl.ds(0, 1), :] = jnp.broadcast_to(jnp.sum(old_sum).reshape(1, 1), (1, LANES))
    sums_ref[pl.ds(1, 1), :] = jnp.broadcast_to(jnp.sum(direction_sum).reshape(1, 1), (1, LANES))


def prepare(scale, depth_band, direction, old_grad):
    epochs, cells = direction.shape
    blocks = cells // CBLOCK
    return pl.pallas_call(
        functools.partial(prepare_kernel, scale),
        out_shape=(
            jax.ShapeDtypeStruct((blocks, 2 * epochs, CBLOCK), BF16),
            jax.ShapeDtypeStruct((2, cells), F32),
            jax.ShapeDtypeStruct((cells // LANES, LANES), F32),
            jax.ShapeDtypeStruct((2, LANES), F32),
        ),
        in_specs=[VMEM] * 4,
        out_specs=(VMEM,) * 4,
        compiler_params=params(),
        cost_estimate=pl.CostEstimate(flops=8 * epochs * cells, bytes_accessed=12 * epochs * cells, transcendentals=0),
        name="prepare",
    )(depth_band.reshape(cells // LANES, LANES), depth_band.reshape(1, cells), direction, old_grad)


def list_pairs(sizes, first_ref, codes, list_ref):
    cell_blocks, station_blocks, pairs = sizes[:3]
    count = jnp.int32(0)
    for slot, codes_ref in enumerate(codes):
        first = first_ref[slot]
        for q in range(station_blocks):
            for i in range(pairs):
                within = codes_ref[q, i].astype(jnp.int32) - first
                hit = jnp.logical_and(within >= 0, within < cell_blocks)
                list_ref[count] = (slot * station_blocks + q) * cell_blocks + within
                count = count + hit.astype(jnp.int32)
    for i in range(UNROLL + 4):
        list_ref[count + i] = len(codes) * station_blocks * cell_blocks
    return count


def pair_list(sizes):
    cell_blocks, station_blocks, pairs, epochs, slots = sizes
    return pltpu.SMEM((slots * station_blocks * pairs + UNROLL + 4,), jnp.int32)


def codes_spec(stations):
    return pl.BlockSpec((8, LANES), lambda i: (0, stations // LANES), memory_space=pltpu.SMEM)


UNROLL = 4


def pipelined(count, stage, issue, collect):
    stage(0, 0)
    stage(1, 1)
    issue(0, 0)

    def step(j, unused):
        for k in range(UNROLL):
            i, now, later = UNROLL * j + k, k % 2, 1 - k % 2
            issue(i + 1, later)
            stage(i + 2, now)
            collect(i, now)
        return 0

    rounds = (count + UNROLL - 2) // UNROLL
    lax.fori_loop(0, rounds, step, 0)
    collect(UNROLL * rounds, 0)


def multiply_add(sums_ref, left, pieces, unit, register):
    high, low = zip(*pieces)
    pltpu.matmul_push_rhs(jnp.concatenate(high + low, axis=0), register, unit)
    pltpu.matmul_acc_lhs(sums_ref, jnp.concatenate([left, left], axis=1), load_staged_rhs=register)


def accumulators(rows):
    return [pltpu.ACC(unit)((rows, TILE), F32) for unit in (0, 1)] * 2


def inverse_cube(squared):
    return lax.rsqrt(squared * squared * squared)


def forward_kernel(sizes, first_ref, shift_ref, *refs):
    cell_blocks, station_blocks, pairs, epochs, slots = sizes
    codes = refs[:slots]
    messages = refs[slots : 2 * slots]
    values_ref, turned_ref = refs[2 * slots : 2 * slots + 2]
    images = refs[2 * slots + 2 : 3 * slots + 2]
    list_ref, across_ref, along_ref, image_ref, gaps_ref, lines_ref, depths_ref = refs[3 * slots + 2 :]
    dummy = slots * station_blocks
    across_ref[pl.ds(dummy, 1), :] = jnp.zeros((1, SBLOCK), F32)
    along_ref[pl.ds(dummy, 1), :] = jnp.zeros((1, SBLOCK), F32)
    image_ref[...] = jnp.zeros_like(image_ref)
    for slot in range(slots):
        for q in range(station_blocks):
            at = pl.ds(q * SBLOCK, SBLOCK)
            row = pl.ds(slot * station_blocks + q, 1)
            across_ref[row, :] = messages[slot][pl.ds(0, 1), at] + shift_ref[slot]
            along_ref[row, :] = messages[slot][pl.ds(1, 1), at]
    count = list_pairs(sizes, first_ref, codes, list_ref)
    column = lax.broadcasted_iota(jnp.int32, (COL_SIDE, SBLOCK), 0).astype(F32)
    column = (column + 0.5) / COL_SIDE
    rows = CBLOCK // COL_SIDE

    def stage(i, k):
        code = list_ref[i]
        q, w = code // cell_blocks, code % cell_blocks
        across = across_ref[pl.ds(q, 1), :] - column
        gaps_ref[k] = across * across
        lines_ref[k] = along_ref[pl.ds(q, 1), :] - (w % 2).astype(F32) * (rows / COL_SIDE)
        turned = pltpu.roll(turned_ref[...], (LANES - w * (CBLOCK // LANES)) % LANES, 1)
        for part in range(CBLOCK // LANES):
            depths_ref[k, pl.ds(part * LANES, LANES), :] = jnp.broadcast_to(turned[:, part : part + 1], (LANES, LANES))

    def issue(sums, i, k):
        w = list_ref[i] % cell_blocks
        across = gaps_ref[k]
        along = lines_ref[k]
        for tile in range(CBLOCK // HALF):
            pieces = []
            for at in range(0, HALF, COL_SIDE):
                y = (tile * HALF + at) // COL_SIDE
                depth = depths_ref[k, pl.ds(y * COL_SIDE, COL_SIDE), :]
                depth = jnp.concatenate([depth] * (SBLOCK // LANES), axis=1)
                gap = along - (y + 0.5) / COL_SIDE
                pieces.append(split(inverse_cube((across + gap * gap) + depth)))
            left = values_ref[w, :, pl.ds(tile * HALF, HALF)]
            multiply_add(sums[2 * k + tile % 2], left, pieces, tile % 2, tile // 2)

    def collect(sums, i, k):
        q = list_ref[i] // cell_blocks
        both = pltpu.matmul_pop(sums[2 * k]) + pltpu.matmul_pop(sums[2 * k + 1])
        image_ref[q] += both[:epochs] + both[epochs:]

    def run(*sums):
        pipelined(count, stage, functools.partial(issue, sums), functools.partial(collect, sums))

    pl.run_scoped(run, *accumulators(2 * epochs))
    for slot in range(slots):
        images[slot][...] = image_ref[pl.ds(slot * station_blocks, station_blocks)]


def forward(sizes, first, shift, messages, values, turned):
    cell_blocks, station_blocks, pairs, epochs, slots = sizes
    stations = station_blocks * SBLOCK
    rows = (slots * station_blocks + 8) // 8 * 8
    return pl.pallas_call(
        functools.partial(forward_kernel, sizes),
        grid=(1,),
        out_shape=(jax.ShapeDtypeStruct((station_blocks, epochs, SBLOCK), F32),) * slots,
        in_specs=[SMEM, SMEM] + [codes_spec(stations)] * slots + [VMEM] * (slots + 2),
        out_specs=(VMEM,) * slots,
        scratch_shapes=[
            pair_list(sizes),
            pltpu.VMEM((rows, SBLOCK), F32),
            pltpu.VMEM((rows, SBLOCK), F32),
            pltpu.VMEM((slots * station_blocks + 1, epochs, SBLOCK), F32),
            pltpu.VMEM((2, COL_SIDE, SBLOCK), F32),
            pltpu.VMEM((2, 1, SBLOCK), F32),
            pltpu.VMEM((2, CBLOCK, LANES), F32),
        ],
        compiler_params=params(),
        cost_estimate=estimate(sizes),
        name="forward",
    )(first, shift, *messages, *messages, values, turned)


def estimate(sizes):
    cell_blocks, station_blocks, pairs, epochs, slots = sizes
    entries = station_blocks * pairs * slots // (2 * REACH + 1) * SBLOCK * CBLOCK
    return pl.CostEstimate(flops=2 * 1200 * entries, bytes_accessed=2**20, transcendentals=entries)


def adjoint_sums(sizes, first_ref, shift_ref, codes, messages, residuals, images, cells_ref, total_ref, scratch):
    cell_blocks, station_blocks, pairs, epochs, slots = sizes
    list_ref, stations_ref, terms_ref, depths_ref, gaps_ref, lines_ref = scratch
    dummy = slots * station_blocks
    terms_ref[dummy] = jnp.zeros(terms_ref.shape[1:], BF16)
    stations_ref[slots] = jnp.zeros(stations_ref.shape[1:], F32)
    total_ref[...] = jnp.zeros_like(total_ref)
    per_block = SBLOCK // LANES
    lane_rows = station_blocks * per_block
    for slot in range(slots):
        parts = [messages[slot][pl.ds(0, 1), pl.ds(i * LANES, LANES)] + shift_ref[slot] for i in range(lane_rows)]
        parts += [messages[slot][pl.ds(1, 1), pl.ds(i * LANES, LANES)] for i in range(lane_rows)]
        parts.append(jnp.zeros((LANES - 2 * lane_rows, LANES), F32))
        stations_ref[slot] = jnp.concatenate(parts, axis=0).T
        for q in range(station_blocks):
            stacked = jnp.concatenate([residuals[slot][:, pl.ds(q * SBLOCK, SBLOCK)], images[slot][q]], axis=0)
            high, low = split(stacked)
            terms_ref[slot * station_blocks + q, pl.ds(0, 2 * epochs), :] = high
            terms_ref[slot * station_blocks + q, pl.ds(2 * epochs, 2 * epochs), :] = low
    count = list_pairs(sizes, first_ref, codes, list_ref)
    lane = lax.broadcasted_iota(jnp.int32, (1, LANES), 1)
    column = ((lane % COL_SIDE).astype(F32) + 0.5) / COL_SIDE
    line = ((lane // COL_SIDE).astype(F32) + 0.5) / COL_SIDE
    rows = CBLOCK // COL_SIDE
    chunks = CBLOCK // LANES

    def stage(i, k):
        code = list_ref[i]
        q, w = code // cell_blocks, code % cell_blocks
        slot, within = q // station_blocks, q % station_blocks
        depths_ref[k] = cells_ref[pl.ds(0, 1), pl.ds(pl.multiple_of(w * CBLOCK, CBLOCK), CBLOCK)]
        lines = line + (w % 2).astype(F32) * (rows / COL_SIDE)
        places = pltpu.roll(stations_ref[slot], (LANES - within * per_block) % LANES, 1)
        for part in range(per_block):
            at = pl.ds(part * LANES, LANES)
            across = jnp.broadcast_to(places[:, part : part + 1], (LANES, LANES)) - column
            gaps_ref[k, at, :] = across * across
            along = jnp.broadcast_to(places[:, lane_rows + part : lane_rows + part + 1], (LANES, LANES))
            lines_ref[k, at, :] = along - lines

    def issue(sums, i, k):
        q = list_ref[i] // cell_blocks
        depth = depths_ref[k]
        for part in range(per_block):
            pieces = ([], [])
            for at in range(part * LANES, (part + 1) * LANES, 16):
                across = gaps_ref[k, pl.ds(at, 16), :]
                along = lines_ref[k, pl.ds(at, 16), :]
                for unit in range(2):
                    near = []
                    for chunk in range(unit * chunks // 2, (unit + 1) * chunks // 2):
                        gap = along - chunk * (LANES // COL_SIDE) / COL_SIDE
                        squared = (across + gap * gap) + depth[:, chunk * LANES : (chunk + 1) * LANES]
                        near.append(split(inverse_cube(squared)))
                    pieces[unit].append([jnp.concatenate(terms, axis=1) for terms in zip(*near)])
            left = terms_ref[q, :, pl.ds(part * HALF, HALF)]
            for unit in range(2):
                multiply_add(sums[2 * k + unit], left, pieces[unit], unit, part)

    def collect(sums, i, k):
        w = list_ref[i] % cell_blocks
        for unit in range(2):
            both = pltpu.matmul_pop(sums[2 * k + unit])
            total_ref[w, :, pl.ds(unit * TILE, TILE)] += both[: 2 * epochs] + both[2 * epochs :]

    def run(*sums):
        pipelined(count, stage, functools.partial(issue, sums), functools.partial(collect, sums))

    pl.run_scoped(run, *accumulators(4 * epochs))


def adjoint_refs(slots, refs):
    codes, messages, residuals, images = (refs[i * slots : (i + 1) * slots] for i in range(4))
    return codes, messages, residuals, images, refs[4 * slots :]


def near_kernel(sizes, first_ref, shift_ref, *refs):
    codes, messages, residuals, images, rest = adjoint_refs(sizes[-1], refs)
    cells_ref, total_ref, *scratch = rest
    adjoint_sums(sizes, first_ref, shift_ref, codes, messages, residuals, images, cells_ref, total_ref, scratch)


def far_kernel(sizes, first_ref, shift_ref, *refs):
    cell_blocks, station_blocks, pairs, epochs, slots = sizes
    codes, messages, residuals, images, rest = adjoint_refs(slots, refs)
    cells_ref, near_ref, model_ref, direction_ref, sums_ref, image_ref = rest[:6]
    constant_ref, slope_ref, stats_ref = rest[6:9]
    total_ref, *scratch = rest[9:]
    adjoint_sums(sizes, first_ref, shift_ref, codes, messages, residuals, images, cells_ref, total_ref, scratch)
    zero = jnp.zeros((epochs, CBLOCK), F32)

    def combine(w, sums):
        at = pl.ds(pl.multiple_of(w * CBLOCK, CBLOCK), CBLOCK)
        total = (near_ref[w] + total_ref[w]) * cells_ref[pl.ds(1, 1), at]
        constant = total[:epochs] - DAMPING * model_ref[:, at]
        slope = total[epochs:] + DAMPING * direction_ref[:, at]
        constant_ref[:, at] = constant
        slope_ref[:, at] = slope
        return sums[0] + constant * slope, sums[1] + slope * slope

    cross, square = lax.fori_loop(0, cell_blocks, combine, (zero, zero), unroll=2)
    square = jnp.sum(square).reshape(1, 1)
    cross = jnp.sum(cross).reshape(1, 1)
    local_step = jnp.where(square > 0, cross / jnp.where(square > 0, square, 1.0), 0.0)

    def remainder(w, sums):
        at = pl.ds(pl.multiple_of(w * CBLOCK, CBLOCK), CBLOCK)
        slope = slope_ref[:, at]
        left = constant_ref[:, at] - local_step * slope
        return sums[0] + left * left, sums[1] + left * slope

    left_square, left_cross = lax.fori_loop(0, cell_blocks, remainder, (zero, zero), unroll=2)
    image = image_ref[...]
    stats = [
        sums_ref[pl.ds(0, 1), pl.ds(0, 1)],
        sums_ref[pl.ds(1, 1), pl.ds(0, 1)],
        jnp.sum(image * image).reshape(1, 1),
        local_step,
        jnp.sum(left_square).reshape(1, 1),
        jnp.sum(left_cross).reshape(1, 1),
        jnp.sqrt(square),
    ]
    lane = lax.broadcasted_iota(jnp.int32, (1, LANES), 1)
    row = jnp.zeros((1, LANES), F32)
    for i, value in enumerate(stats):
        row = jnp.where(lane == i, value, row)
    for i in range(stats_ref.shape[0]):
        stats_ref[i] = row


def adjoint(sizes, first, shift, messages, residuals, images, cell_rows, last=()):
    cell_blocks, station_blocks, pairs, epochs, slots = sizes
    total = (cell_blocks, 2 * epochs, CBLOCK)
    scratch = [
        pair_list(sizes),
        pltpu.VMEM((slots + 1, LANES, LANES), F32),
        pltpu.VMEM((slots * station_blocks + 1, 4 * epochs, SBLOCK), BF16),
        pltpu.VMEM((2, 1, CBLOCK), F32),
        pltpu.VMEM((2, SBLOCK, LANES), F32),
        pltpu.VMEM((2, SBLOCK, LANES), F32),
    ]
    if last:
        ranks, *last = last
        kernel, cells = far_kernel, (epochs, cell_blocks * CBLOCK)
        shapes = [cells, cells, (ranks, 1, LANES)]
        scratch = [pltpu.VMEM(total, F32)] + scratch
    else:
        kernel, shapes = near_kernel, [total]
    return pl.pallas_call(
        functools.partial(kernel, sizes),
        grid=(1,),
        out_shape=tuple(jax.ShapeDtypeStruct(shape, F32) for shape in shapes),
        in_specs=[SMEM, SMEM]
        + [codes_spec(station_blocks * SBLOCK)] * slots
        + [VMEM] * (3 * slots + 1 + len(last)),
        out_specs=(VMEM,) * len(shapes),
        scratch_shapes=scratch,
        compiler_params=params(),
        cost_estimate=estimate(sizes),
        name="far" if last else "near",
    )(first, shift, *messages, *messages, *residuals, *images, cell_rows, *last)


def finish_kernel(
    stats_ref, constant_ref, slope_ref, model_ref, direction_ref, residual_ref, image_ref, model_out, residual_out, direction_out
):
    stats = stats_ref[...][:, 0, :]
    gamma_old, direction_square, image_square = (
        jnp.sum(stats[:, i : i + 1], axis=0, keepdims=True) for i in range(3)
    )
    step = gamma_old / (image_square + DAMPING * direction_square + GUARD)
    ahead = step - stats[:, 3:4]
    reach = ahead * stats[:, 6:7]
    gamma_new = jnp.sum(stats[:, 4:5] - 2.0 * ahead * stats[:, 5:6] + reach * reach, axis=0, keepdims=True)
    ratio = gamma_new / (gamma_old + GUARD)
    blocks = model_ref.shape[1] // CBLOCK

    def block(w, unused):
        at = pl.ds(pl.multiple_of(w * CBLOCK, CBLOCK), CBLOCK)
        direction = direction_ref[:, at]
        model_out[:, at] = model_ref[:, at] + step * direction
        direction_out[:, at] = (constant_ref[:, at] - step * slope_ref[:, at]) + ratio * direction
        return 0

    lax.fori_loop(0, blocks, block, 0, unroll=2)
    for q in range(image_ref.shape[0]):
        at = pl.ds(q * SBLOCK, SBLOCK)
        residual_out[:, at] = residual_ref[:, at] - step * image_ref[q]


def finish(stats, constant, slope, model_field, direction, residual, image):
    return pl.pallas_call(
        finish_kernel,
        out_shape=(
            jax.ShapeDtypeStruct(model_field.shape, F32),
            jax.ShapeDtypeStruct(residual.shape, F32),
            jax.ShapeDtypeStruct(direction.shape, F32),
        ),
        in_specs=[VMEM] * 7,
        out_specs=(VMEM,) * 3,
        compiler_params=params(),
        name="finish",
    )(stats, constant, slope, model_field, direction, residual, image)


def after(arrays, others):
    return lax.optimization_barrier((arrays, others))[0]


def shards(model_field, direction, old_grad, residual, block_pairs, depth_band, station_offsets):
    ranks = lax.axis_size("tile")
    tile_id = lax.axis_index("tile")
    epochs, cells = model_field.shape
    station_blocks, pairs = block_pairs.shape
    cell_blocks = cells // CBLOCK
    side = 2 * (tile_id % 2) - 1

    def to_partner(array):
        return lax.ppermute(array, "tile", [(i, i ^ 1) for i in range(ranks)])

    def across(first, second):
        ends = [(i, i + 1) for i in range(1, ranks - 1, 2)]
        both = lax.ppermute(jnp.stack([first, second]), "tile", ends + [(j, i) for i, j in ends])
        return both[0], both[1]

    def slots(*places):
        offsets = jnp.stack([multiple * side for multiple in places]).astype(jnp.int32)
        sizes = (cell_blocks, station_blocks, pairs, epochs, len(places))
        return sizes, cell_blocks * (REACH - offsets) + 1, offsets.astype(F32)

    own_slot, partner_slot, near_slots, far_slots = slots(0), slots(-1), slots(0, -1), slots(1, 2, -2)

    own = pack(station_offsets, block_pairs)
    values, cell_rows, turned, sums = prepare(2.0 / math.sqrt(cells), depth_band, direction, old_grad)
    partner = to_partner(own)
    first_far, second_far = across(own, partner)
    (to_return,) = forward(*partner_slot, [partner], values, turned)
    third_far = to_partner(first_far)

    own_residual = after(residual, third_far)
    partner_residual = to_partner(own_residual)
    far_residuals = across(own_residual, partner_residual)
    far_residuals = [*far_residuals, to_partner(far_residuals[0])]

    far = [first_far, second_far, third_far]
    to_first, to_second, to_third = forward(*far_slots, far, values, turned)
    to_first = to_first + to_partner(to_third)
    (image,) = forward(*own_slot, [after(own, to_first)], values, turned)
    given, to_pass = across(to_first, to_second)
    image = image + given + to_partner(to_return + to_pass)

    partner_image = to_partner(image)
    first_image, second_image = across(image, partner_image)
    (near_total,) = adjoint(
        *near_slots, [own, partner], [residual, partner_residual], [image, partner_image], cell_rows
    )
    far_images = [first_image, second_image, to_partner(first_image)]
    constant, slope, stats = adjoint(
        *far_slots, far, far_residuals, far_images, cell_rows,
        (ranks, near_total, model_field, direction, sums, image),
    )
    stats = lax.all_to_all(stats, "tile", 0, 0)
    return finish(stats, constant, slope, model_field, direction, residual, image)


def solution(mesh):
    wide = P(None, ("groups", "tile"))
    mapped = jax.shard_map(
        shards,
        mesh=mesh,
        in_specs=(wide, wide, wide, wide, P(("groups", "tile"), None), P(("groups", "tile")), wide),
        out_specs=(wide, wide, wide),
        check_vma=False,
    )

    def step(*arrays):
        with jax.sharding.use_abstract_mesh(mesh.abstract_mesh):
            return mapped(*arrays)

    return step
```

```python
import functools
import math

import jax
import jax.numpy as jnp
from jax import lax
from jax.experimental import pallas as pl
from jax.experimental.pallas import tpu as pltpu
from jax.sharding import PartitionSpec as P

CBLOCK = 512
SBLOCK = 256
REACH = 2
BANDS = 16
COL_SIDE = 32
DEPTH_RANGE = 2.0
DEPTH_SHIFT = 0.25
DAMPING = 1.0
GUARD = 1e-06

F32 = jnp.float32
BF16 = jnp.bfloat16
LANES = 128
TILE = 256
HALF = TILE // 2

SMEM = pl.BlockSpec(memory_space=pltpu.SMEM)
VMEM = pl.BlockSpec(memory_space=pltpu.VMEM)


def params():
    return pltpu.CompilerParams(vmem_limit_bytes=24 * 2**20)


def split(values):
    high = values.astype(BF16)
    return high, (values - high.astype(F32)).astype(BF16)


def dot(left, right):
    return jnp.dot(left, right, preferred_element_type=F32)


def pack_kernel(offsets_ref, pairs_ref, message_ref):
    stations = offsets_ref.shape[1]
    message_ref[...] = jnp.zeros_like(message_ref)
    message_ref[pl.ds(0, 2), pl.ds(0, stations)] = offsets_ref[...]
    message_ref[:, pl.ds(stations, pairs_ref.shape[1])] = pairs_ref[...].astype(F32) + 1.0


def pack(station_offsets, block_pairs):
    rows, stations = block_pairs.shape[0], station_offsets.shape[1]
    return pl.pallas_call(
        pack_kernel,
        out_shape=jax.ShapeDtypeStruct((rows, stations + LANES), F32),
        in_specs=[VMEM] * 2,
        out_specs=VMEM,
        name="pack",
    )(station_offsets, block_pairs)


def pair_kernel(*refs):
    first_ref, second_ref, *added_refs, message_ref = refs
    first = first_ref[...]
    for added_ref in added_refs:
        first = first + added_ref[...]
    message_ref[0] = first
    message_ref[1] = second_ref[...]


def pair_up(first, second, *added):
    return pl.pallas_call(
        pair_kernel,
        out_shape=jax.ShapeDtypeStruct((2, *first.shape), F32),
        in_specs=[VMEM] * (2 + len(added)),
        out_specs=VMEM,
        name="pair",
    )(first, second, *added)


def prepare_kernel(scale, band_ref, band_row_ref, direction_ref, old_ref, values_ref, cells_ref, turned_ref, sums_ref):
    blocks = values_ref.shape[0]
    epochs = direction_ref.shape[0]

    @pl.when(pl.program_id(0) == 0)
    def first():
        depth = (band_ref[...].astype(F32) + 0.5) * (DEPTH_RANGE / BANDS)
        turned_ref[...] = (depth * depth).T
        sums_ref[...] = jnp.zeros_like(sums_ref)

    def block(w, sums):
        at = pl.ds(pl.multiple_of(w * CBLOCK, CBLOCK), CBLOCK)
        row = (band_row_ref[:, at].astype(F32) + 0.5) * (DEPTH_RANGE / BANDS)
        shifted = row + DEPTH_SHIFT
        factor = row * scale * (shifted * jnp.sqrt(shifted))
        cells_ref[pl.ds(0, 1), at] = row * row
        cells_ref[pl.ds(1, 1), at] = factor
        values = direction_ref[:, at]
        old = old_ref[:, at]
        high, low = split(values * factor)
        values_ref[w, pl.ds(0, epochs), :] = high
        values_ref[w, pl.ds(epochs, epochs), :] = low
        return sums[0] + old * old, sums[1] + values * values

    zero = jnp.zeros((epochs, CBLOCK), F32)
    old_sum, direction_sum = lax.fori_loop(0, blocks, block, (zero, zero), unroll=2)
    sums_ref[pl.ds(0, 1), :] += jnp.broadcast_to(jnp.sum(old_sum).reshape(1, 1), (1, LANES))
    sums_ref[pl.ds(1, 1), :] += jnp.broadcast_to(jnp.sum(direction_sum).reshape(1, 1), (1, LANES))


PARTS = 4


def prepare(scale, depth_band, direction, old_grad):
    epochs, cells = direction.shape
    blocks = cells // CBLOCK
    direction, old_grad = (pltpu.with_memory_space_constraint(array, pltpu.HBM) for array in (direction, old_grad))
    wide = pl.BlockSpec((epochs, cells // PARTS), lambda i: (0, i))
    return pl.pallas_call(
        functools.partial(prepare_kernel, scale),
        grid=(PARTS,),
        out_shape=(
            jax.ShapeDtypeStruct((blocks, 2 * epochs, CBLOCK), BF16),
            jax.ShapeDtypeStruct((2, cells), F32),
            jax.ShapeDtypeStruct((cells // LANES, LANES), F32),
            jax.ShapeDtypeStruct((2, LANES), F32),
        ),
        in_specs=[VMEM, pl.BlockSpec((1, cells // PARTS), lambda i: (0, i)), wide, wide],
        out_specs=(
            pl.BlockSpec((blocks // PARTS, 2 * epochs, CBLOCK), lambda i: (i, 0, 0)),
            pl.BlockSpec((2, cells // PARTS), lambda i: (0, i)),
            VMEM,
            VMEM,
        ),
        compiler_params=params(),
        cost_estimate=pl.CostEstimate(flops=8 * epochs * cells, bytes_accessed=12 * epochs * cells, transcendentals=0),
        name="prepare",
    )(depth_band.reshape(cells // LANES, LANES), depth_band.reshape(1, cells), direction, old_grad)


def list_pairs(sizes, first_ref, codes, list_ref):
    cell_blocks, station_blocks, pairs = sizes[:3]
    count = jnp.int32(0)
    for slot, codes_ref in enumerate(codes):
        first = first_ref[slot]
        for q in range(station_blocks):
            for i in range(pairs):
                within = codes_ref[q, i].astype(jnp.int32) - first
                hit = jnp.logical_and(within >= 0, within < cell_blocks)
                list_ref[count] = (slot * station_blocks + q) * cell_blocks + within
                count = count + hit.astype(jnp.int32)
    for i in range(UNROLL + 4):
        list_ref[count + i] = len(codes) * station_blocks * cell_blocks
    return count


def pair_list(sizes):
    cell_blocks, station_blocks, pairs, epochs, slots = sizes
    return pltpu.SMEM((slots * station_blocks * pairs + UNROLL + 4,), jnp.int32)


def codes_spec(stations):
    return pl.BlockSpec((8, LANES), lambda i: (0, stations // LANES), memory_space=pltpu.SMEM)


UNROLL = 4


def pipelined(count, stage, issue, collect):
    stage(0, 0)
    stage(1, 1)
    issue(0, 0)

    def step(j, unused):
        for k in range(UNROLL):
            i, now, later = UNROLL * j + k, k % 2, 1 - k % 2
            issue(i + 1, later)
            stage(i + 2, now)
            collect(i, now)
        return 0

    rounds = (count + UNROLL - 2) // UNROLL
    lax.fori_loop(0, rounds, step, 0)
    collect(UNROLL * rounds, 0)


def multiply_add(sums_ref, left, pieces, unit, register):
    high, low = zip(*pieces)
    pltpu.matmul_push_rhs(jnp.concatenate(high + low, axis=0), register, unit)
    pltpu.matmul_acc_lhs(sums_ref, jnp.concatenate([left, left], axis=1), load_staged_rhs=register)


def accumulators(rows):
    return [pltpu.ACC(unit)((rows, TILE), F32) for unit in (0, 1)] * 2


def inverse_cube(squared):
    return lax.rsqrt(squared * squared * squared)


def forward_kernel(sizes, first_ref, shift_ref, *refs):
    cell_blocks, station_blocks, pairs, epochs, slots = sizes
    codes = refs[:slots]
    messages = refs[slots : 2 * slots]
    values_ref, turned_ref = refs[2 * slots : 2 * slots + 2]
    images = refs[2 * slots + 2 : 3 * slots + 2]
    list_ref, across_ref, along_ref, image_ref, gaps_ref, lines_ref, depths_ref = refs[3 * slots + 2 :]
    dummy = slots * station_blocks
    across_ref[pl.ds(dummy, 1), :] = jnp.zeros((1, SBLOCK), F32)
    along_ref[pl.ds(dummy, 1), :] = jnp.zeros((1, SBLOCK), F32)
    image_ref[...] = jnp.zeros_like(image_ref)
    for slot in range(slots):
        for q in range(station_blocks):
            at = pl.ds(q * SBLOCK, SBLOCK)
            row = pl.ds(slot * station_blocks + q, 1)
            across_ref[row, :] = messages[slot][pl.ds(0, 1), at] + shift_ref[slot]
            along_ref[row, :] = messages[slot][pl.ds(1, 1), at]
    count = list_pairs(sizes, first_ref, codes, list_ref)
    column = lax.broadcasted_iota(jnp.int32, (COL_SIDE, SBLOCK), 0).astype(F32)
    column = (column + 0.5) / COL_SIDE
    rows = CBLOCK // COL_SIDE

    def stage(i, k):
        code = list_ref[i]
        q, w = code // cell_blocks, code % cell_blocks
        across = across_ref[pl.ds(q, 1), :] - column
        gaps_ref[k] = across * across
        lines_ref[k] = along_ref[pl.ds(q, 1), :] - (w % 2).astype(F32) * (rows / COL_SIDE)
        turned = pltpu.roll(turned_ref[...], (LANES - w * (CBLOCK // LANES)) % LANES, 1)
        for part in range(CBLOCK // LANES):
            depths_ref[k, pl.ds(part * LANES, LANES), :] = jnp.broadcast_to(turned[:, part : part + 1], (LANES, LANES))

    def issue(sums, i, k):
        w = list_ref[i] % cell_blocks
        across = gaps_ref[k]
        along = lines_ref[k]
        for tile in range(CBLOCK // HALF):
            pieces = []
            for at in range(0, HALF, COL_SIDE):
                y = (tile * HALF + at) // COL_SIDE
                depth = depths_ref[k, pl.ds(y * COL_SIDE, COL_SIDE), :]
                depth = jnp.concatenate([depth] * (SBLOCK // LANES), axis=1)
                gap = along - (y + 0.5) / COL_SIDE
                pieces.append(split(inverse_cube((across + gap * gap) + depth)))
            left = values_ref[w, :, pl.ds(tile * HALF, HALF)]
            multiply_add(sums[2 * k + tile % 2], left, pieces, tile % 2, tile // 2)

    def collect(sums, i, k):
        q = list_ref[i] // cell_blocks
        both = pltpu.matmul_pop(sums[2 * k]) + pltpu.matmul_pop(sums[2 * k + 1])
        image_ref[q] += both[:epochs] + both[epochs:]

    def run(*sums):
        pipelined(count, stage, functools.partial(issue, sums), functools.partial(collect, sums))

    pl.run_scoped(run, *accumulators(2 * epochs))
    for slot in range(slots):
        images[slot][...] = image_ref[pl.ds(slot * station_blocks, station_blocks)]


def forward(sizes, first, shift, messages, values, turned):
    cell_blocks, station_blocks, pairs, epochs, slots = sizes
    stations = station_blocks * SBLOCK
    rows = (slots * station_blocks + 8) // 8 * 8
    return pl.pallas_call(
        functools.partial(forward_kernel, sizes),
        grid=(1,),
        out_shape=(jax.ShapeDtypeStruct((station_blocks, epochs, SBLOCK), F32),) * slots,
        in_specs=[SMEM, SMEM] + [codes_spec(stations)] * slots + [VMEM] * (slots + 2),
        out_specs=(VMEM,) * slots,
        scratch_shapes=[
            pair_list(sizes),
            pltpu.VMEM((rows, SBLOCK), F32),
            pltpu.VMEM((rows, SBLOCK), F32),
            pltpu.VMEM((slots * station_blocks + 1, epochs, SBLOCK), F32),
            pltpu.VMEM((2, COL_SIDE, SBLOCK), F32),
            pltpu.VMEM((2, 1, SBLOCK), F32),
            pltpu.VMEM((2, CBLOCK, LANES), F32),
        ],
        compiler_params=params(),
        cost_estimate=estimate(sizes),
        name="forward",
    )(first, shift, *messages, *messages, values, turned)


def estimate(sizes):
    cell_blocks, station_blocks, pairs, epochs, slots = sizes
    entries = station_blocks * pairs * slots // (2 * REACH + 1) * SBLOCK * CBLOCK
    return pl.CostEstimate(flops=2 * 1200 * entries, bytes_accessed=2**20, transcendentals=entries)


def adjoint_sums(sizes, first_ref, shift_ref, codes, messages, residuals, images, cells_ref, total_ref, scratch):
    cell_blocks, station_blocks, pairs, epochs, slots = sizes
    list_ref, stations_ref, terms_ref, depths_ref, gaps_ref, lines_ref = scratch
    dummy = slots * station_blocks
    terms_ref[dummy] = jnp.zeros(terms_ref.shape[1:], BF16)
    stations_ref[slots] = jnp.zeros(stations_ref.shape[1:], F32)
    total_ref[...] = jnp.zeros_like(total_ref)
    per_block = SBLOCK // LANES
    lane_rows = station_blocks * per_block
    for slot in range(slots):
        parts = [messages[slot][pl.ds(0, 1), pl.ds(i * LANES, LANES)] + shift_ref[slot] for i in range(lane_rows)]
        parts += [messages[slot][pl.ds(1, 1), pl.ds(i * LANES, LANES)] for i in range(lane_rows)]
        parts.append(jnp.zeros((LANES - 2 * lane_rows, LANES), F32))
        stations_ref[slot] = jnp.concatenate(parts, axis=0).T
        for q in range(station_blocks):
            stacked = jnp.concatenate([residuals[slot][:, pl.ds(q * SBLOCK, SBLOCK)], images[slot][q]], axis=0)
            high, low = split(stacked)
            terms_ref[slot * station_blocks + q, pl.ds(0, 2 * epochs), :] = high
            terms_ref[slot * station_blocks + q, pl.ds(2 * epochs, 2 * epochs), :] = low
    count = list_pairs(sizes, first_ref, codes, list_ref)
    lane = lax.broadcasted_iota(jnp.int32, (1, LANES), 1)
    column = ((lane % COL_SIDE).astype(F32) + 0.5) / COL_SIDE
    line = ((lane // COL_SIDE).astype(F32) + 0.5) / COL_SIDE
    rows = CBLOCK // COL_SIDE
    chunks = CBLOCK // LANES

    def stage(i, k):
        code = list_ref[i]
        q, w = code // cell_blocks, code % cell_blocks
        slot, within = q // station_blocks, q % station_blocks
        depths_ref[k] = cells_ref[pl.ds(0, 1), pl.ds(pl.multiple_of(w * CBLOCK, CBLOCK), CBLOCK)]
        lines = line + (w % 2).astype(F32) * (rows / COL_SIDE)
        places = pltpu.roll(stations_ref[slot], (LANES - within * per_block) % LANES, 1)
        for part in range(per_block):
            at = pl.ds(part * LANES, LANES)
            across = jnp.broadcast_to(places[:, part : part + 1], (LANES, LANES)) - column
            gaps_ref[k, at, :] = across * across
            along = jnp.broadcast_to(places[:, lane_rows + part : lane_rows + part + 1], (LANES, LANES))
            lines_ref[k, at, :] = along - lines

    def issue(sums, i, k):
        q = list_ref[i] // cell_blocks
        depth = depths_ref[k]
        for part in range(per_block):
            pieces = ([], [])
            for at in range(part * LANES, (part + 1) * LANES, 16):
                across = gaps_ref[k, pl.ds(at, 16), :]
                along = lines_ref[k, pl.ds(at, 16), :]
                for unit in range(2):
                    near = []
                    for chunk in range(unit * chunks // 2, (unit + 1) * chunks // 2):
                        gap = along - chunk * (LANES // COL_SIDE) / COL_SIDE
                        squared = (across + gap * gap) + depth[:, chunk * LANES : (chunk + 1) * LANES]
                        near.append(split(inverse_cube(squared)))
                    pieces[unit].append([jnp.concatenate(terms, axis=1) for terms in zip(*near)])
            left = terms_ref[q, :, pl.ds(part * HALF, HALF)]
            for unit in range(2):
                multiply_add(sums[2 * k + unit], left, pieces[unit], unit, part)

    def collect(sums, i, k):
        w = list_ref[i] % cell_blocks
        for unit in range(2):
            both = pltpu.matmul_pop(sums[2 * k + unit])
            total_ref[w, :, pl.ds(unit * TILE, TILE)] += both[: 2 * epochs] + both[2 * epochs :]

    def run(*sums):
        pipelined(count, stage, functools.partial(issue, sums), functools.partial(collect, sums))

    pl.run_scoped(run, *accumulators(4 * epochs))


def adjoint_refs(slots, refs):
    codes, messages, residuals, images = (refs[i * slots : (i + 1) * slots] for i in range(4))
    return codes, messages, residuals, images, refs[4 * slots :]


def near_kernel(sizes, first_ref, shift_ref, *refs):
    codes, messages, residuals, images, rest = adjoint_refs(sizes[-1], refs)
    cells_ref, total_ref, *scratch = rest
    adjoint_sums(sizes, first_ref, shift_ref, codes, messages, residuals, images, cells_ref, total_ref, scratch)


def far_kernel(sizes, first_ref, shift_ref, *refs):
    cell_blocks, station_blocks, pairs, epochs, slots = sizes
    codes, messages, residuals, images, rest = adjoint_refs(slots, refs)
    cells_ref, near_ref, model_ref, direction_ref, sums_ref, image_ref = rest[:6]
    constant_ref, slope_ref, stats_ref = rest[6:9]
    total_ref, *scratch = rest[9:]
    adjoint_sums(sizes, first_ref, shift_ref, codes, messages, residuals, images, cells_ref, total_ref, scratch)
    zero = jnp.zeros((epochs, CBLOCK), F32)

    def combine(w, sums):
        at = pl.ds(pl.multiple_of(w * CBLOCK, CBLOCK), CBLOCK)
        total = (near_ref[w] + total_ref[w]) * cells_ref[pl.ds(1, 1), at]
        constant = total[:epochs] - DAMPING * model_ref[:, at]
        slope = total[epochs:] + DAMPING * direction_ref[:, at]
        constant_ref[:, at] = constant
        slope_ref[:, at] = slope
        return sums[0] + constant * slope, sums[1] + slope * slope

    cross, square = lax.fori_loop(0, cell_blocks, combine, (zero, zero), unroll=2)
    square = jnp.sum(square).reshape(1, 1)
    cross = jnp.sum(cross).reshape(1, 1)
    local_step = jnp.where(square > 0, cross / jnp.where(square > 0, square, 1.0), 0.0)

    def remainder(w, sums):
        at = pl.ds(pl.multiple_of(w * CBLOCK, CBLOCK), CBLOCK)
        slope = slope_ref[:, at]
        left = constant_ref[:, at] - local_step * slope
        return sums[0] + left * left, sums[1] + left * slope

    left_square, left_cross = lax.fori_loop(0, cell_blocks, remainder, (zero, zero), unroll=2)
    image = image_ref[...]
    stats = [
        sums_ref[pl.ds(0, 1), pl.ds(0, 1)],
        sums_ref[pl.ds(1, 1), pl.ds(0, 1)],
        jnp.sum(image * image).reshape(1, 1),
        local_step,
        jnp.sum(left_square).reshape(1, 1),
        jnp.sum(left_cross).reshape(1, 1),
        jnp.sqrt(square),
    ]
    lane = lax.broadcasted_iota(jnp.int32, (1, LANES), 1)
    row = jnp.zeros((1, LANES), F32)
    for i, value in enumerate(stats):
        row = jnp.where(lane == i, value, row)
    for i in range(stats_ref.shape[0]):
        stats_ref[i] = row


def adjoint(sizes, first, shift, messages, residuals, images, cell_rows, last=()):
    cell_blocks, station_blocks, pairs, epochs, slots = sizes
    total = (cell_blocks, 2 * epochs, CBLOCK)
    scratch = [
        pair_list(sizes),
        pltpu.VMEM((slots + 1, LANES, LANES), F32),
        pltpu.VMEM((slots * station_blocks + 1, 4 * epochs, SBLOCK), BF16),
        pltpu.VMEM((2, 1, CBLOCK), F32),
        pltpu.VMEM((2, SBLOCK, LANES), F32),
        pltpu.VMEM((2, SBLOCK, LANES), F32),
    ]
    if last:
        ranks, *last = last
        kernel, cells = far_kernel, (epochs, cell_blocks * CBLOCK)
        shapes = [cells, cells, (ranks, 1, LANES)]
        scratch = [pltpu.VMEM(total, F32)] + scratch
    else:
        kernel, shapes = near_kernel, [total]
    return pl.pallas_call(
        functools.partial(kernel, sizes),
        grid=(1,),
        out_shape=tuple(jax.ShapeDtypeStruct(shape, F32) for shape in shapes),
        in_specs=[SMEM, SMEM]
        + [codes_spec(station_blocks * SBLOCK)] * slots
        + [VMEM] * (3 * slots + 1 + len(last)),
        out_specs=(VMEM,) * len(shapes),
        scratch_shapes=scratch,
        compiler_params=params(),
        cost_estimate=estimate(sizes),
        name="far" if last else "near",
    )(first, shift, *messages, *messages, *residuals, *images, cell_rows, *last)


def finish_kernel(
    stats_ref, constant_ref, slope_ref, model_ref, direction_ref, residual_ref, image_ref, model_out, residual_out, direction_out
):
    stats = stats_ref[...][:, 0, :]
    gamma_old, direction_square, image_square = (
        jnp.sum(stats[:, i : i + 1], axis=0, keepdims=True) for i in range(3)
    )
    step = gamma_old / (image_square + DAMPING * direction_square + GUARD)
    ahead = step - stats[:, 3:4]
    reach = ahead * stats[:, 6:7]
    gamma_new = jnp.sum(stats[:, 4:5] - 2.0 * ahead * stats[:, 5:6] + reach * reach, axis=0, keepdims=True)
    ratio = gamma_new / (gamma_old + GUARD)
    blocks = model_ref.shape[1] // CBLOCK

    def block(w, unused):
        at = pl.ds(pl.multiple_of(w * CBLOCK, CBLOCK), CBLOCK)
        direction = direction_ref[:, at]
        model_out[:, at] = model_ref[:, at] + step * direction
        direction_out[:, at] = (constant_ref[:, at] - step * slope_ref[:, at]) + ratio * direction
        return 0

    lax.fori_loop(0, blocks, block, 0, unroll=2)
    for q in range(image_ref.shape[0]):
        at = pl.ds(q * SBLOCK, SBLOCK)
        residual_out[:, at] = residual_ref[:, at] - step * image_ref[q]


def finish(stats, constant, slope, model_field, direction, residual, image):
    return pl.pallas_call(
        finish_kernel,
        out_shape=(
            jax.ShapeDtypeStruct(model_field.shape, F32),
            jax.ShapeDtypeStruct(residual.shape, F32),
            jax.ShapeDtypeStruct(direction.shape, F32),
        ),
        in_specs=[VMEM] * 7,
        out_specs=(VMEM,) * 3,
        compiler_params=params(),
        name="finish",
    )(stats, constant, slope, model_field, direction, residual, image)


def after(arrays, others):
    return lax.optimization_barrier((arrays, others))[0]


def shards(model_field, direction, old_grad, residual, block_pairs, depth_band, station_offsets):
    ranks = lax.axis_size("tile")
    tile_id = lax.axis_index("tile")
    epochs, cells = model_field.shape
    station_blocks, pairs = block_pairs.shape
    cell_blocks = cells // CBLOCK
    side = 2 * (tile_id % 2) - 1

    def to_partner(array):
        return lax.ppermute(array, "tile", [(i, i ^ 1) for i in range(ranks)])

    def across(message):
        ends = [(i, i + 1) for i in range(1, ranks - 1, 2)]
        return lax.ppermute(message, "tile", ends + [(j, i) for i, j in ends])

    def slots(*places):
        offsets = jnp.stack([multiple * side for multiple in places]).astype(jnp.int32)
        sizes = (cell_blocks, station_blocks, pairs, epochs, len(places))
        return sizes, cell_blocks * (REACH - offsets) + 1, offsets.astype(F32)

    own_slot, partner_slot, near_slots, far_slots = slots(0), slots(-1), slots(0, -1), slots(1, 2, -2)

    own = pack(station_offsets, block_pairs)
    partner = to_partner(own)
    arrived = across(pair_up(own, partner))
    partner_residual = to_partner(after(residual, partner))
    values, cell_rows, turned, sums = prepare(
        2.0 / math.sqrt(cells), after(depth_band, partner), direction, old_grad
    )
    (to_return,) = forward(*partner_slot, [partner], values, turned)
    arrived = after(arrived, (to_return, partner_residual))
    first_far, second_far = arrived[0], arrived[1]
    third_far = to_partner(first_far)
    far = [first_far, second_far, third_far]

    arrived = across(pair_up(after(residual, first_far), partner_residual))
    to_first, to_second, to_third = forward(*far_slots, far, values, turned)
    to_third, arrived = after((to_third, arrived), (arrived, to_third))
    far_residuals = [arrived[0], arrived[1], to_partner(arrived[0])]
    returned = to_partner(to_third)
    given = across(pair_up(to_first, to_second, returned))
    (image,) = forward(*own_slot, [after(own, (far_residuals[2], returned))], values, turned)
    given = after(given, image)
    image = image + given[0] + to_partner(to_return + given[1])

    partner_image = to_partner(image)
    arrived = across(pair_up(image, partner_image))
    (near_total,) = adjoint(
        *near_slots, [own, partner], [residual, partner_residual], [image, partner_image], cell_rows
    )
    arrived = after(arrived, near_total)
    far_images = [arrived[0], arrived[1], to_partner(arrived[0])]
    constant, slope, stats = adjoint(
        *far_slots, far, far_residuals, far_images, cell_rows,
        (ranks, near_total, model_field, direction, sums, image),
    )
    stats = lax.all_to_all(stats, "tile", 0, 0)
    return finish(stats, constant, slope, model_field, direction, residual, image)


def solution(mesh):
    wide = P(None, ("groups", "tile"))
    mapped = jax.shard_map(
        shards,
        mesh=mesh,
        in_specs=(wide, wide, wide, wide, P(("groups", "tile"), None), P(("groups", "tile")), wide),
        out_specs=(wide, wide, wide),
        check_vma=False,
    )

    def step(*arrays):
        with jax.sharding.use_abstract_mesh(mesh.abstract_mesh):
            return mapped(*arrays)

    return step
```

```python
import functools
import math

import jax
import jax.numpy as jnp
from jax import lax
from jax.experimental import pallas as pl
from jax.experimental.pallas import tpu as pltpu
from jax.sharding import PartitionSpec as P

CBLOCK = 512
SBLOCK = 256
REACH = 2
BANDS = 16
COL_SIDE = 32
DEPTH_RANGE = 2.0
DEPTH_SHIFT = 0.25
DAMPING = 1.0
GUARD = 1e-06

F32 = jnp.float32
BF16 = jnp.bfloat16
LANES = 128
TILE = 256
HALF = TILE // 2

SMEM = pl.BlockSpec(memory_space=pltpu.SMEM)
VMEM = pl.BlockSpec(memory_space=pltpu.VMEM)


def params(mebibytes=16):
    return pltpu.CompilerParams(vmem_limit_bytes=mebibytes * 2**20)


def split(values):
    high = values.astype(BF16)
    return high, (values - high.astype(F32)).astype(BF16)


def dot(left, right):
    return jnp.dot(left, right, preferred_element_type=F32)


def pack_kernel(offsets_ref, pairs_ref, message_ref):
    lines = offsets_ref.shape[1] // LANES
    message_ref[...] = jnp.zeros_like(message_ref)
    for i in range(lines):
        at = pl.ds(i * LANES, LANES)
        message_ref[pl.ds(i, 1), :] = offsets_ref[pl.ds(0, 1), at]
        message_ref[pl.ds(lines + i, 1), :] = offsets_ref[pl.ds(1, 1), at]
    rows, pairs = pairs_ref.shape
    message_ref[pl.ds(2 * lines, rows), pl.ds(0, pairs)] = pairs_ref[...].astype(F32) + 1.0


def pack(station_offsets, block_pairs):
    rows = 2 * station_offsets.shape[1] // LANES + block_pairs.shape[0]
    return pl.pallas_call(
        pack_kernel,
        out_shape=jax.ShapeDtypeStruct((rows, LANES), F32),
        in_specs=[VMEM] * 2,
        out_specs=VMEM,
        compiler_params=params(2),
        name="pack",
    )(station_offsets, block_pairs)


def pair_kernel(*refs):
    first_ref, second_ref, *added_refs, message_ref = refs
    first = first_ref[...]
    for added_ref in added_refs:
        first = first + added_ref[...]
    message_ref[0] = first
    message_ref[1] = second_ref[...]


def pair_up(first, second, *added):
    return pl.pallas_call(
        pair_kernel,
        out_shape=jax.ShapeDtypeStruct((2, *first.shape), F32),
        in_specs=[VMEM] * (2 + len(added)),
        out_specs=VMEM,
        compiler_params=params(2),
        name="pair",
    )(first, second, *added)


def prepare_kernel(scale, band_ref, band_row_ref, direction_ref, values_ref, cells_ref, turned_ref):
    blocks = values_ref.shape[0]
    epochs = direction_ref.shape[0]

    @pl.when(pl.program_id(0) == 0)
    def first():
        depth = (band_ref[...].astype(F32) + 0.5) * (DEPTH_RANGE / BANDS)
        turned_ref[...] = (depth * depth).T

    def block(w, unused):
        at = pl.ds(pl.multiple_of(w * CBLOCK, CBLOCK), CBLOCK)
        row = (band_row_ref[:, at].astype(F32) + 0.5) * (DEPTH_RANGE / BANDS)
        shifted = row + DEPTH_SHIFT
        factor = row * scale * (shifted * jnp.sqrt(shifted))
        cells_ref[pl.ds(0, 1), at] = row * row
        cells_ref[pl.ds(1, 1), at] = factor
        high, low = split(direction_ref[:, at] * factor)
        values_ref[w, pl.ds(0, epochs), :] = high
        values_ref[w, pl.ds(epochs, epochs), :] = low
        return 0

    lax.fori_loop(0, blocks, block, 0, unroll=4)


PARTS = 2


def prepare(scale, depth_band, direction):
    epochs, cells = direction.shape
    blocks = cells // CBLOCK
    return pl.pallas_call(
        functools.partial(prepare_kernel, scale),
        grid=(PARTS,),
        out_shape=(
            jax.ShapeDtypeStruct((blocks, 2 * epochs, CBLOCK), BF16),
            jax.ShapeDtypeStruct((2, cells), F32),
            jax.ShapeDtypeStruct((cells // LANES, LANES), F32),
        ),
        in_specs=[
            VMEM,
            pl.BlockSpec((1, cells // PARTS), lambda i: (0, i)),
            pl.BlockSpec((epochs, cells // PARTS), lambda i: (0, i)),
        ],
        out_specs=(
            pl.BlockSpec((blocks // PARTS, 2 * epochs, CBLOCK), lambda i: (i, 0, 0)),
            pl.BlockSpec((2, cells // PARTS), lambda i: (0, i)),
            VMEM,
        ),
        compiler_params=params(8),
        cost_estimate=pl.CostEstimate(flops=8 * epochs * cells, bytes_accessed=12 * epochs * cells, transcendentals=0),
        name="prepare",
    )(
        depth_band.reshape(cells // LANES, LANES),
        depth_band.reshape(1, cells),
        pltpu.with_memory_space_constraint(direction, pltpu.HBM),
    )


def send_codes(sizes, first_ref, messages, codes_ref, scalars_ref, sent):
    cell_blocks, station_blocks, pairs, epochs, slots = sizes
    q = lax.broadcasted_iota(jnp.int32, (station_blocks, LANES), 0)
    for slot, message_ref in enumerate(messages):
        codes = message_ref[pl.ds(message_ref.shape[0] - station_blocks, station_blocks), :]
        within = codes.astype(jnp.int32) - first_ref[slot]
        hit = jnp.logical_and(within >= 0, within < cell_blocks)
        code = (slot * station_blocks + q) * cell_blocks + within
        codes_ref[pl.ds(slot * station_blocks, station_blocks), :] = jnp.where(hit, code, -1)
    copy = pltpu.make_async_copy(codes_ref, scalars_ref, sent)
    copy.start()
    return copy


def list_pairs(sizes, copy, scalars_ref, list_ref):
    cell_blocks, station_blocks, pairs, epochs, slots = sizes
    copy.wait()
    count = jnp.int32(0)
    for row in range(slots * station_blocks):
        for i in range(pairs):
            code = scalars_ref[row, i]
            list_ref[count] = code
            count = count + (code >= 0).astype(jnp.int32)
    for i in range(UNROLL + 4):
        list_ref[count + i] = slots * station_blocks * cell_blocks
    return count


def list_scratch(sizes):
    cell_blocks, station_blocks, pairs, epochs, slots = sizes
    return [
        pltpu.SMEM((slots * station_blocks * pairs + UNROLL + 4,), jnp.int32),
        pltpu.VMEM((slots * station_blocks, LANES), jnp.int32),
        pltpu.SMEM((slots * station_blocks, LANES), jnp.int32),
        pltpu.SemaphoreType.DMA(()),
    ]


UNROLL = 4


def pipelined(count, stage, issue, collect):
    stage(0, 0)
    stage(1, 1)
    issue(0, 0)

    def step(j, unused):
        for k in range(UNROLL):
            i, now, later = UNROLL * j + k, k % 2, 1 - k % 2
            issue(i + 1, later)
            stage(i + 2, now)
            collect(i, now)
        return 0

    rounds = (count + UNROLL - 2) // UNROLL
    lax.fori_loop(0, rounds, step, 0)
    collect(UNROLL * rounds, 0)


def multiply_add(sums_ref, left, pieces, unit, register):
    high, low = zip(*pieces)
    pltpu.matmul_push_rhs(jnp.concatenate(high + low, axis=0), register, unit)
    pltpu.matmul_acc_lhs(sums_ref, jnp.concatenate([left, left], axis=1), load_staged_rhs=register)


def accumulators(rows):
    return [pltpu.ACC(unit)((rows, TILE), F32) for unit in (0, 1)] * 2


def inverse_cube(squared):
    return lax.rsqrt(squared * squared * squared)


def forward_kernel(sizes, first_ref, shift_ref, *refs):
    cell_blocks, station_blocks, pairs, epochs, slots = sizes
    messages = refs[:slots]
    values_ref, turned_ref = refs[slots : slots + 2]
    images = refs[slots + 2 : 2 * slots + 2]
    list_ref, codes_ref, scalars_ref, sent, *scratch = refs[2 * slots + 2 :]
    across_ref, along_ref, image_ref, gaps_ref, lines_ref, depths_ref = scratch
    copy = send_codes(sizes, first_ref, messages, codes_ref, scalars_ref, sent)
    dummy = slots * station_blocks
    per_block = SBLOCK // LANES
    lines = station_blocks * per_block
    across_ref[pl.ds(dummy, 1), :] = jnp.zeros((1, SBLOCK), F32)
    along_ref[pl.ds(dummy, 1), :] = jnp.zeros((1, SBLOCK), F32)
    image_ref[...] = jnp.zeros_like(image_ref)
    for slot in range(slots):
        for i in range(lines):
            place = (pl.ds(slot * station_blocks + i // per_block, 1), pl.ds(i % per_block * LANES, LANES))
            across_ref[place] = messages[slot][pl.ds(i, 1), :] + shift_ref[slot]
            along_ref[place] = messages[slot][pl.ds(lines + i, 1), :]
    count = list_pairs(sizes, copy, scalars_ref, list_ref)
    column = lax.broadcasted_iota(jnp.int32, (COL_SIDE, SBLOCK), 0).astype(F32)
    column = (column + 0.5) / COL_SIDE
    rows = CBLOCK // COL_SIDE

    def stage(i, k):
        code = list_ref[i]
        q, w = code // cell_blocks, code % cell_blocks
        across = across_ref[pl.ds(q, 1), :] - column
        gaps_ref[k] = across * across
        lines_ref[k] = along_ref[pl.ds(q, 1), :] - (w % 2).astype(F32) * (rows / COL_SIDE)
        turned = pltpu.roll(turned_ref[...], (LANES - w * (CBLOCK // LANES)) % LANES, 1)
        for part in range(CBLOCK // LANES):
            depths_ref[k, pl.ds(part * LANES, LANES), :] = jnp.broadcast_to(turned[:, part : part + 1], (LANES, LANES))

    def issue(sums, i, k):
        w = list_ref[i] % cell_blocks
        across = gaps_ref[k]
        along = lines_ref[k]
        for tile in range(CBLOCK // HALF):
            pieces = []
            for at in range(0, HALF, COL_SIDE):
                y = (tile * HALF + at) // COL_SIDE
                depth = depths_ref[k, pl.ds(y * COL_SIDE, COL_SIDE), :]
                depth = jnp.concatenate([depth] * (SBLOCK // LANES), axis=1)
                gap = along - (y + 0.5) / COL_SIDE
                pieces.append(split(inverse_cube((across + gap * gap) + depth)))
            left = values_ref[w, :, pl.ds(tile * HALF, HALF)]
            multiply_add(sums[2 * k + tile % 2], left, pieces, tile % 2, tile // 2)

    def collect(sums, i, k):
        q = list_ref[i] // cell_blocks
        both = pltpu.matmul_pop(sums[2 * k]) + pltpu.matmul_pop(sums[2 * k + 1])
        image_ref[q] += both[:epochs] + both[epochs:]

    def run(*sums):
        pipelined(count, stage, functools.partial(issue, sums), functools.partial(collect, sums))

    pl.run_scoped(run, *accumulators(2 * epochs))
    for slot in range(slots):
        images[slot][...] = image_ref[pl.ds(slot * station_blocks, station_blocks)]


def forward(sizes, first, shift, messages, values, turned):
    cell_blocks, station_blocks, pairs, epochs, slots = sizes
    rows = (slots * station_blocks + 8) // 8 * 8
    return pl.pallas_call(
        functools.partial(forward_kernel, sizes),
        out_shape=(jax.ShapeDtypeStruct((station_blocks, epochs, SBLOCK), F32),) * slots,
        in_specs=[SMEM, SMEM] + [VMEM] * (slots + 2),
        out_specs=(VMEM,) * slots,
        scratch_shapes=list_scratch(sizes)
        + [
            pltpu.VMEM((rows, SBLOCK), F32),
            pltpu.VMEM((rows, SBLOCK), F32),
            pltpu.VMEM((slots * station_blocks + 1, epochs, SBLOCK), F32),
            pltpu.VMEM((2, COL_SIDE, SBLOCK), F32),
            pltpu.VMEM((2, 1, SBLOCK), F32),
            pltpu.VMEM((2, CBLOCK, LANES), F32),
        ],
        compiler_params=params(),
        cost_estimate=estimate(sizes),
        name="forward",
    )(first, shift, *messages, values, turned)


def estimate(sizes):
    cell_blocks, station_blocks, pairs, epochs, slots = sizes
    entries = station_blocks * pairs * slots // (2 * REACH + 1) * SBLOCK * CBLOCK
    return pl.CostEstimate(flops=2 * 1200 * entries, bytes_accessed=2**20, transcendentals=entries)


def adjoint_sums(sizes, first_ref, shift_ref, messages, residuals, images, cells_ref, total_ref, scratch):
    cell_blocks, station_blocks, pairs, epochs, slots = sizes
    list_ref, codes_ref, scalars_ref, sent, stations_ref, terms_ref, depths_ref, gaps_ref, lines_ref = scratch
    copy = send_codes(sizes, first_ref, messages, codes_ref, scalars_ref, sent)
    dummy = slots * station_blocks
    terms_ref[dummy] = jnp.zeros(terms_ref.shape[1:], BF16)
    stations_ref[slots] = jnp.zeros(stations_ref.shape[1:], F32)
    total_ref[...] = jnp.zeros_like(total_ref)
    per_block = SBLOCK // LANES
    lane_rows = station_blocks * per_block
    for slot in range(slots):
        places = [messages[slot][pl.ds(0, lane_rows), :] + shift_ref[slot], messages[slot][pl.ds(lane_rows, lane_rows), :]]
        places.append(jnp.zeros((LANES - 2 * lane_rows, LANES), F32))
        stations_ref[slot] = jnp.concatenate(places, axis=0).T
        for q in range(station_blocks):
            stacked = jnp.concatenate([residuals[slot][:, pl.ds(q * SBLOCK, SBLOCK)], images[slot][q]], axis=0)
            high, low = split(stacked)
            terms_ref[slot * station_blocks + q, pl.ds(0, 2 * epochs), :] = high
            terms_ref[slot * station_blocks + q, pl.ds(2 * epochs, 2 * epochs), :] = low
    count = list_pairs(sizes, copy, scalars_ref, list_ref)
    lane = lax.broadcasted_iota(jnp.int32, (1, LANES), 1)
    column = ((lane % COL_SIDE).astype(F32) + 0.5) / COL_SIDE
    line = ((lane // COL_SIDE).astype(F32) + 0.5) / COL_SIDE
    rows = CBLOCK // COL_SIDE
    chunks = CBLOCK // LANES

    def stage(i, k):
        code = list_ref[i]
        q, w = code // cell_blocks, code % cell_blocks
        slot, within = q // station_blocks, q % station_blocks
        depths_ref[k] = cells_ref[pl.ds(0, 1), pl.ds(pl.multiple_of(w * CBLOCK, CBLOCK), CBLOCK)]
        lines = line + (w % 2).astype(F32) * (rows / COL_SIDE)
        places = pltpu.roll(stations_ref[slot], (LANES - within * per_block) % LANES, 1)
        for part in range(per_block):
            at = pl.ds(part * LANES, LANES)
            across = jnp.broadcast_to(places[:, part : part + 1], (LANES, LANES)) - column
            gaps_ref[k, at, :] = across * across
            along = jnp.broadcast_to(places[:, lane_rows + part : lane_rows + part + 1], (LANES, LANES))
            lines_ref[k, at, :] = along - lines

    def issue(sums, i, k):
        q = list_ref[i] // cell_blocks
        depth = depths_ref[k]
        for part in range(per_block):
            pieces = ([], [])
            for at in range(part * LANES, (part + 1) * LANES, 16):
                across = gaps_ref[k, pl.ds(at, 16), :]
                along = lines_ref[k, pl.ds(at, 16), :]
                for unit in range(2):
                    near = []
                    for chunk in range(unit * chunks // 2, (unit + 1) * chunks // 2):
                        gap = along - chunk * (LANES // COL_SIDE) / COL_SIDE
                        squared = (across + gap * gap) + depth[:, chunk * LANES : (chunk + 1) * LANES]
                        near.append(split(inverse_cube(squared)))
                    pieces[unit].append([jnp.concatenate(terms, axis=1) for terms in zip(*near)])
            left = terms_ref[q, :, pl.ds(part * HALF, HALF)]
            for unit in range(2):
                multiply_add(sums[2 * k + unit], left, pieces[unit], unit, part)

    def collect(sums, i, k):
        w = list_ref[i] % cell_blocks
        for unit in range(2):
            both = pltpu.matmul_pop(sums[2 * k + unit])
            total_ref[w, :, pl.ds(unit * TILE, TILE)] += both[: 2 * epochs] + both[2 * epochs :]

    def run(*sums):
        pipelined(count, stage, functools.partial(issue, sums), functools.partial(collect, sums))

    pl.run_scoped(run, *accumulators(4 * epochs))


def near_kernel(sizes, first_ref, shift_ref, *refs):
    cell_blocks, station_blocks, pairs, epochs, slots = sizes
    messages, residuals, images = (refs[i * slots : (i + 1) * slots] for i in range(3))
    cells_ref, direction_ref, old_ref, total_ref, sums_ref, *scratch = refs[3 * slots :]
    adjoint_sums(sizes, first_ref, shift_ref, messages, residuals, images, cells_ref, total_ref, scratch)

    def add(w, sums):
        at = pl.ds(pl.multiple_of(w * CBLOCK, CBLOCK), CBLOCK)
        direction, old = direction_ref[:, at], old_ref[:, at]
        return sums[0] + old * old, sums[1] + direction * direction

    zero = jnp.zeros((epochs, CBLOCK), F32)
    for i, total in enumerate(lax.fori_loop(0, cell_blocks, add, (zero, zero), unroll=4)):
        sums_ref[pl.ds(i, 1), :] = jnp.broadcast_to(jnp.sum(total).reshape(1, 1), (1, LANES))


def far_kernel(sizes, first_ref, shift_ref, *refs):
    cell_blocks, station_blocks, pairs, epochs, slots = sizes
    messages, residuals, images = (refs[i * slots : (i + 1) * slots] for i in range(3))
    rest = refs[3 * slots :]
    cells_ref, near_ref, sums_ref, model_ref, direction_ref, image_ref = rest[:6]
    constant_ref, slope_ref, stats_ref = rest[6:9]
    total_ref, *scratch = rest[9:]
    adjoint_sums(sizes, first_ref, shift_ref, messages, residuals, images, cells_ref, total_ref, scratch)
    zero = jnp.zeros((epochs, CBLOCK), F32)

    def combine(w, sums):
        at = pl.ds(pl.multiple_of(w * CBLOCK, CBLOCK), CBLOCK)
        total = (near_ref[w] + total_ref[w]) * cells_ref[pl.ds(1, 1), at]
        constant = total[:epochs] - DAMPING * model_ref[:, at]
        slope = total[epochs:] + DAMPING * direction_ref[:, at]
        constant_ref[:, at] = constant
        slope_ref[:, at] = slope
        return sums[0] + constant * slope, sums[1] + slope * slope

    cross, square = lax.fori_loop(0, cell_blocks, combine, (zero, zero), unroll=2)
    square = jnp.sum(square).reshape(1, 1)
    cross = jnp.sum(cross).reshape(1, 1)
    local_step = jnp.where(square > 0, cross / jnp.where(square > 0, square, 1.0), 0.0)

    def remainder(w, sums):
        at = pl.ds(pl.multiple_of(w * CBLOCK, CBLOCK), CBLOCK)
        slope = slope_ref[:, at]
        left = constant_ref[:, at] - local_step * slope
        return sums[0] + left * left, sums[1] + left * slope

    left_square, left_cross = lax.fori_loop(0, cell_blocks, remainder, (zero, zero), unroll=2)
    image = image_ref[...]
    stats = [
        sums_ref[pl.ds(0, 1), pl.ds(0, 1)],
        sums_ref[pl.ds(1, 1), pl.ds(0, 1)],
        jnp.sum(image * image).reshape(1, 1),
        local_step,
        jnp.sum(left_square).reshape(1, 1),
        jnp.sum(left_cross).reshape(1, 1),
        jnp.sqrt(square),
    ]
    lane = lax.broadcasted_iota(jnp.int32, (1, LANES), 1)
    row = jnp.zeros((1, LANES), F32)
    for i, value in enumerate(stats):
        row = jnp.where(lane == i, value, row)
    for i in range(stats_ref.shape[0]):
        stats_ref[i] = row


def adjoint(sizes, first, shift, messages, residuals, images, cell_rows, *others, ranks=None):
    cell_blocks, station_blocks, pairs, epochs, slots = sizes
    total = (cell_blocks, 2 * epochs, CBLOCK)
    scratch = list_scratch(sizes) + [
        pltpu.VMEM((slots + 1, LANES, LANES), F32),
        pltpu.VMEM((slots * station_blocks + 1, 4 * epochs, SBLOCK), BF16),
        pltpu.VMEM((2, 1, CBLOCK), F32),
        pltpu.VMEM((2, SBLOCK, LANES), F32),
        pltpu.VMEM((2, SBLOCK, LANES), F32),
    ]
    if ranks is None:
        kernel, shapes = near_kernel, [total, (2, LANES)]
    else:
        kernel, cells = far_kernel, (epochs, cell_blocks * CBLOCK)
        shapes = [cells, cells, (ranks, 1, LANES)]
        scratch = [pltpu.VMEM(total, F32)] + scratch
    return pl.pallas_call(
        functools.partial(kernel, sizes),
        out_shape=tuple(jax.ShapeDtypeStruct(shape, F32) for shape in shapes),
        in_specs=[SMEM, SMEM] + [VMEM] * (3 * slots + 1 + len(others)),
        out_specs=(VMEM,) * len(shapes),
        scratch_shapes=scratch,
        compiler_params=params(),
        cost_estimate=estimate(sizes),
        name="near" if ranks is None else "far",
    )(first, shift, *messages, *residuals, *images, cell_rows, *others)


def finish_kernel(
    stats_ref, constant_ref, slope_ref, model_ref, direction_ref, residual_ref, image_ref,
    model_out, residual_out, direction_out, new_model, new_residual, new_direction, sent,
):
    stats = stats_ref[...][:, 0, :]
    gamma_old, direction_square, image_square = (
        jnp.sum(stats[:, i : i + 1], axis=0, keepdims=True) for i in range(3)
    )
    step = gamma_old / (image_square + DAMPING * direction_square + GUARD)
    ahead = step - stats[:, 3:4]
    reach = ahead * stats[:, 6:7]
    gamma_new = jnp.sum(stats[:, 4:5] - 2.0 * ahead * stats[:, 5:6] + reach * reach, axis=0, keepdims=True)
    ratio = gamma_new / (gamma_old + GUARD)
    copies = []

    def send(i, source, target, at):
        copies.append(pltpu.make_async_copy(source.at[:, at], target.at[:, at], sent.at[i]))
        copies[-1].start()

    for q in range(image_ref.shape[0]):
        at = pl.ds(q * SBLOCK, SBLOCK)
        new_residual[:, at] = residual_ref[:, at] - step * image_ref[q]
    send(0, new_residual, residual_out, pl.ds(0, residual_ref.shape[1]))
    cells = model_ref.shape[1] // FINISH_PARTS
    for part in range(FINISH_PARTS):

        def block(w, unused):
            at = pl.ds(pl.multiple_of(part * cells + w * CBLOCK, CBLOCK), CBLOCK)
            direction = direction_ref[:, at]
            new_model[:, at] = model_ref[:, at] + step * direction
            new_direction[:, at] = (constant_ref[:, at] - step * slope_ref[:, at]) + ratio * direction
            return 0

        lax.fori_loop(0, cells // CBLOCK, block, 0, unroll=2)
        send(1 + 2 * part, new_model, model_out, pl.ds(part * cells, cells))
        send(2 + 2 * part, new_direction, direction_out, pl.ds(part * cells, cells))
    for copy in copies:
        copy.wait()


FINISH_PARTS = 4


def finish(stats, constant, slope, model_field, direction, residual, image):
    outs = (model_field.shape, residual.shape, direction.shape)
    return pl.pallas_call(
        finish_kernel,
        out_shape=tuple(jax.ShapeDtypeStruct(shape, F32) for shape in outs),
        in_specs=[VMEM] * 7,
        out_specs=(pl.BlockSpec(memory_space=pl.ANY),) * 3,
        scratch_shapes=[pltpu.VMEM(shape, F32) for shape in outs]
        + [pltpu.SemaphoreType.DMA((1 + 2 * FINISH_PARTS,))],
        compiler_params=params(),
        name="finish",
    )(stats, constant, slope, model_field, direction, residual, image)


def after(arrays, others):
    return lax.optimization_barrier((arrays, others))[0]


def shards(model_field, direction, old_grad, residual, block_pairs, depth_band, station_offsets):
    ranks = lax.axis_size("tile")
    tile_id = lax.axis_index("tile")
    epochs, cells = model_field.shape
    station_blocks, pairs = block_pairs.shape
    cell_blocks = cells // CBLOCK
    side = 2 * (tile_id % 2) - 1

    def to_partner(array):
        return lax.ppermute(array, "tile", [(i, i ^ 1) for i in range(ranks)])

    def across(message):
        ends = [(i, i + 1) for i in range(1, ranks - 1, 2)]
        return lax.ppermute(message, "tile", ends + [(j, i) for i, j in ends])

    def slots(*places):
        offsets = jnp.stack([multiple * side for multiple in places]).astype(jnp.int32)
        sizes = (cell_blocks, station_blocks, pairs, epochs, len(places))
        return sizes, cell_blocks * (REACH - offsets) + 1, offsets.astype(F32)

    near_slots, far_slots = slots(0, -1), slots(1, 2, -2)

    own = pack(station_offsets, block_pairs)
    partner = to_partner(own)
    near = [own, partner]
    partner_residual = to_partner(after(residual, own))
    arrived = across(pair_up(*near))
    values, cell_rows, turned = prepare(2.0 / math.sqrt(cells), after(depth_band, partner), direction)
    arrived = after(arrived, (values, partner_residual))
    far = [arrived[0], arrived[1], to_partner(arrived[0])]

    arrived = across(pair_up(residual, partner_residual))
    to_first, to_second, to_third = forward(*far_slots, far, values, turned)
    to_third, arrived = after((to_third, arrived), (arrived, to_third))
    far_residuals = [arrived[0], arrived[1], to_partner(arrived[0])]
    returned = to_partner(to_third)
    given = across(pair_up(to_first, to_second, returned))
    image, to_return = forward(*near_slots, after(near, (far_residuals[2], returned)), values, turned)
    given = after(given, image)
    image = image + given[0] + to_partner(to_return + given[1])

    near_images = [image, to_partner(image)]
    arrived = across(pair_up(*near_images))
    near_total, sums = adjoint(
        *near_slots, near, [residual, partner_residual], near_images, cell_rows, direction, old_grad
    )
    arrived = after(arrived, near_total)
    far_images = [arrived[0], arrived[1], to_partner(arrived[0])]
    constant, slope, stats = adjoint(
        *far_slots, far, far_residuals, far_images, cell_rows, near_total, sums, model_field, direction, image, ranks=ranks
    )
    stats = lax.all_to_all(stats, "tile", 0, 0)
    return finish(stats, constant, slope, model_field, direction, residual, image)


def solution(mesh):
    wide = P(None, ("groups", "tile"))
    mapped = jax.shard_map(
        shards,
        mesh=mesh,
        in_specs=(wide, wide, wide, wide, P(("groups", "tile"), None), P(("groups", "tile")), wide),
        out_specs=(wide, wide, wide),
        check_vma=False,
    )

    def step(*arrays):
        with jax.sharding.use_abstract_mesh(mesh.abstract_mesh):
            return mapped(*arrays)

    return step
```

```python
import functools
import math

import jax
import jax.numpy as jnp
from jax import lax
from jax.experimental import pallas as pl
from jax.experimental.pallas import tpu as pltpu
from jax.sharding import PartitionSpec as P

CBLOCK = 512
SBLOCK = 256
REACH = 2
BANDS = 16
COL_SIDE = 32
DEPTH_RANGE = 2.0
DEPTH_SHIFT = 0.25
DAMPING = 1.0
GUARD = 1e-06

F32 = jnp.float32
BF16 = jnp.bfloat16
LANES = 128
TILE = 256
HALF = TILE // 2

SMEM = pl.BlockSpec(memory_space=pltpu.SMEM)
VMEM = pl.BlockSpec(memory_space=pltpu.VMEM)


def params(mebibytes=16):
    return pltpu.CompilerParams(vmem_limit_bytes=mebibytes * 2**20)


def split(values):
    high = values.astype(BF16)
    return high, (values - high.astype(F32)).astype(BF16)


def dot(left, right):
    return jnp.dot(left, right, preferred_element_type=F32)


def pack_kernel(offsets_any, pairs_any, residual_any, message_ref, residual_ref, offsets_ref, pairs_ref, sent):
    copies = [
        pltpu.make_async_copy(offsets_any, offsets_ref, sent.at[0]),
        pltpu.make_async_copy(pairs_any, pairs_ref, sent.at[1]),
        pltpu.make_async_copy(residual_any, residual_ref, sent.at[2]),
    ]
    for copy in copies:
        copy.start()
    lines = offsets_ref.shape[1] // LANES
    rows, pairs = pairs_ref.shape
    message_ref[pl.ds(2 * lines, rows), :] = jnp.zeros((rows, LANES), F32)
    for copy in copies:
        copy.wait()
    for i in range(lines):
        at = pl.ds(i * LANES, LANES)
        message_ref[pl.ds(i, 1), :] = offsets_ref[pl.ds(0, 1), at]
        message_ref[pl.ds(lines + i, 1), :] = offsets_ref[pl.ds(1, 1), at]
    message_ref[pl.ds(2 * lines, rows), pl.ds(0, pairs)] = pairs_ref[...].astype(F32) + 1.0


def in_hbm(array):
    return pltpu.with_memory_space_constraint(array, pltpu.HBM)


def pack(station_offsets, block_pairs, residual):
    rows = 2 * station_offsets.shape[1] // LANES + block_pairs.shape[0]
    return pl.pallas_call(
        pack_kernel,
        out_shape=(jax.ShapeDtypeStruct((rows, LANES), F32), jax.ShapeDtypeStruct(residual.shape, F32)),
        in_specs=[pl.BlockSpec(memory_space=pl.ANY)] * 3,
        out_specs=(VMEM, VMEM),
        scratch_shapes=[
            pltpu.VMEM(station_offsets.shape, F32),
            pltpu.VMEM(block_pairs.shape, jnp.int32),
            pltpu.SemaphoreType.DMA((3,)),
        ],
        compiler_params=params(2),
        name="pack",
    )(in_hbm(station_offsets), in_hbm(block_pairs), in_hbm(residual))


def far_parts_kernel(parts_ref, third_ref, message_ref):
    message_ref[0] = parts_ref[0] + third_ref[...]
    message_ref[1] = parts_ref[1]


def far_parts(parts, third):
    return small_call(far_parts_kernel, (2, *third.shape), "far_parts", parts, third)


def both_images_kernel(mine_ref, theirs_ref, images_ref):
    images_ref[0] = mine_ref[0] + theirs_ref[1]
    images_ref[1] = mine_ref[1] + theirs_ref[0]


def both_images(mine, theirs):
    return small_call(both_images_kernel, mine.shape, "both_images", mine, theirs)


def add_kernel(left_ref, right_ref, sum_ref):
    sum_ref[...] = left_ref[...] + right_ref[...]


def pair_kernel(first_ref, second_ref, message_ref):
    message_ref[0] = first_ref[...]
    message_ref[1] = second_ref[...]


def pair_up(first, second):
    return small_call(pair_kernel, (2, *first.shape), "pair", first, second)


def small_call(kernel, shape, name, *arrays):
    return pl.pallas_call(
        kernel,
        out_shape=jax.ShapeDtypeStruct(shape, F32),
        in_specs=[VMEM] * len(arrays),
        out_specs=VMEM,
        compiler_params=params(2),
        name=name,
    )(*arrays)


def prepare_kernel(scale, band_ref, band_row_ref, direction_ref, values_ref, cells_ref, turned_ref):
    blocks = values_ref.shape[0]
    epochs = direction_ref.shape[0]

    @pl.when(pl.program_id(0) == 0)
    def first():
        depth = (band_ref[...].astype(F32) + 0.5) * (DEPTH_RANGE / BANDS)
        turned_ref[...] = (depth * depth).T

    def block(w, unused):
        at = pl.ds(pl.multiple_of(w * CBLOCK, CBLOCK), CBLOCK)
        row = (band_row_ref[:, at].astype(F32) + 0.5) * (DEPTH_RANGE / BANDS)
        shifted = row + DEPTH_SHIFT
        factor = row * scale * (shifted * jnp.sqrt(shifted))
        cells_ref[pl.ds(0, 1), at] = row * row
        cells_ref[pl.ds(1, 1), at] = factor
        high, low = split(direction_ref[:, at] * factor)
        values_ref[w, pl.ds(0, epochs), :] = high
        values_ref[w, pl.ds(epochs, epochs), :] = low
        return 0

    lax.fori_loop(0, blocks, block, 0, unroll=4)


PARTS = 2


def prepare(scale, depth_band, direction):
    epochs, cells = direction.shape
    blocks = cells // CBLOCK
    return pl.pallas_call(
        functools.partial(prepare_kernel, scale),
        grid=(PARTS,),
        out_shape=(
            jax.ShapeDtypeStruct((blocks, 2 * epochs, CBLOCK), BF16),
            jax.ShapeDtypeStruct((2, cells), F32),
            jax.ShapeDtypeStruct((cells // LANES, LANES), F32),
        ),
        in_specs=[
            pl.BlockSpec((cells // LANES, LANES), lambda i: (0, 0)),
            pl.BlockSpec((1, cells // PARTS), lambda i: (0, i)),
            pl.BlockSpec((epochs, cells // PARTS), lambda i: (0, i)),
        ],
        out_specs=(
            pl.BlockSpec((blocks // PARTS, 2 * epochs, CBLOCK), lambda i: (i, 0, 0)),
            pl.BlockSpec((2, cells // PARTS), lambda i: (0, i)),
            VMEM,
        ),
        compiler_params=params(8),
        cost_estimate=pl.CostEstimate(flops=8 * epochs * cells, bytes_accessed=12 * epochs * cells, transcendentals=0),
        name="prepare",
    )(
        in_hbm(depth_band.reshape(cells // LANES, LANES)),
        in_hbm(depth_band.reshape(1, cells)),
        in_hbm(direction),
    )


def send_codes(sizes, first_ref, messages, codes_ref, scalars_ref, sent):
    cell_blocks, station_blocks, pairs, epochs, slots = sizes
    q = lax.broadcasted_iota(jnp.int32, (station_blocks, LANES), 0)
    for slot, message_ref in enumerate(messages):
        codes = message_ref[pl.ds(message_ref.shape[0] - station_blocks, station_blocks), :]
        within = codes.astype(jnp.int32) - first_ref[slot]
        hit = jnp.logical_and(within >= 0, within < cell_blocks)
        code = (slot * station_blocks + q) * cell_blocks + within
        codes_ref[pl.ds(slot * station_blocks, station_blocks), :] = jnp.where(hit, code, -1)
    copy = pltpu.make_async_copy(codes_ref, scalars_ref, sent)
    copy.start()
    return copy


def list_pairs(sizes, copy, scalars_ref, list_ref):
    cell_blocks, station_blocks, pairs, epochs, slots = sizes
    copy.wait()
    count = jnp.int32(0)
    for row in range(slots * station_blocks):
        for i in range(pairs):
            code = scalars_ref[row, i]
            list_ref[count] = code
            count = count + (code >= 0).astype(jnp.int32)
    for i in range(UNROLL + 4):
        list_ref[count + i] = slots * station_blocks * cell_blocks
    return count


def list_scratch(sizes):
    cell_blocks, station_blocks, pairs, epochs, slots = sizes
    return [
        pltpu.SMEM((slots * station_blocks * pairs + UNROLL + 4,), jnp.int32),
        pltpu.VMEM((slots * station_blocks, LANES), jnp.int32),
        pltpu.SMEM((slots * station_blocks, LANES), jnp.int32),
        pltpu.SemaphoreType.DMA(()),
    ]


UNROLL = 4


def pipelined(count, stage, issue, collect):
    stage(0, 0)
    stage(1, 1)
    issue(0, 0)

    def step(j, unused):
        for k in range(UNROLL):
            i, now, later = UNROLL * j + k, k % 2, 1 - k % 2
            issue(i + 1, later)
            stage(i + 2, now)
            collect(i, now)
        return 0

    rounds = (count + UNROLL - 2) // UNROLL
    lax.fori_loop(0, rounds, step, 0)
    collect(UNROLL * rounds, 0)


def multiply_add(sums_ref, left, pieces, unit, register):
    high, low = zip(*pieces)
    pltpu.matmul_push_rhs(jnp.concatenate(high + low, axis=0), register, unit)
    pltpu.matmul_acc_lhs(sums_ref, jnp.concatenate([left, left], axis=1), load_staged_rhs=register)


def accumulators(rows):
    return [pltpu.ACC(unit)((rows, TILE), F32) for unit in (0, 1)] * 2


def inverse_cube(squared):
    return lax.rsqrt(squared * squared * squared)


def forward_kernel(sizes, first_ref, shift_ref, *refs):
    cell_blocks, station_blocks, pairs, epochs, slots = sizes
    messages = refs[:slots]
    values_ref, turned_ref = refs[slots : slots + 2]
    images_ref, list_ref, codes_ref, scalars_ref, sent, *scratch = refs[slots + 2 :]
    across_ref, along_ref, image_ref, gaps_ref, lines_ref, depths_ref = scratch
    copy = send_codes(sizes, first_ref, messages, codes_ref, scalars_ref, sent)
    dummy = slots * station_blocks
    per_block = SBLOCK // LANES
    lines = station_blocks * per_block
    across_ref[pl.ds(dummy, 1), :] = jnp.zeros((1, SBLOCK), F32)
    along_ref[pl.ds(dummy, 1), :] = jnp.zeros((1, SBLOCK), F32)
    image_ref[...] = jnp.zeros_like(image_ref)
    for slot in range(slots):
        for i in range(lines):
            place = (pl.ds(slot * station_blocks + i // per_block, 1), pl.ds(i % per_block * LANES, LANES))
            across_ref[place] = messages[slot][pl.ds(i, 1), :] + shift_ref[slot]
            along_ref[place] = messages[slot][pl.ds(lines + i, 1), :]
    count = list_pairs(sizes, copy, scalars_ref, list_ref)
    column = lax.broadcasted_iota(jnp.int32, (COL_SIDE, SBLOCK), 0).astype(F32)
    column = (column + 0.5) / COL_SIDE
    rows = CBLOCK // COL_SIDE

    def stage(i, k):
        code = list_ref[i]
        q, w = code // cell_blocks, code % cell_blocks
        across = across_ref[pl.ds(q, 1), :] - column
        gaps_ref[k] = across * across
        lines_ref[k] = along_ref[pl.ds(q, 1), :] - (w % 2).astype(F32) * (rows / COL_SIDE)
        turned = pltpu.roll(turned_ref[...], (LANES - w * (CBLOCK // LANES)) % LANES, 1)
        for part in range(CBLOCK // LANES):
            depths_ref[k, pl.ds(part * LANES, LANES), :] = jnp.broadcast_to(turned[:, part : part + 1], (LANES, LANES))

    def issue(sums, i, k):
        w = list_ref[i] % cell_blocks
        across = gaps_ref[k]
        along = lines_ref[k]
        for tile in range(CBLOCK // HALF):
            pieces = []
            for at in range(0, HALF, COL_SIDE):
                y = (tile * HALF + at) // COL_SIDE
                depth = depths_ref[k, pl.ds(y * COL_SIDE, COL_SIDE), :]
                depth = jnp.concatenate([depth] * (SBLOCK // LANES), axis=1)
                gap = along - (y + 0.5) / COL_SIDE
                pieces.append(split(inverse_cube((across + gap * gap) + depth)))
            left = values_ref[w, :, pl.ds(tile * HALF, HALF)]
            multiply_add(sums[2 * k + tile % 2], left, pieces, tile % 2, tile // 2)

    def collect(sums, i, k):
        q = list_ref[i] // cell_blocks
        both = pltpu.matmul_pop(sums[2 * k]) + pltpu.matmul_pop(sums[2 * k + 1])
        image_ref[q] += both[:epochs] + both[epochs:]

    def run(*sums):
        pipelined(count, stage, functools.partial(issue, sums), functools.partial(collect, sums))

    pl.run_scoped(run, *accumulators(2 * epochs))
    for slot in range(slots):
        images_ref[slot] = image_ref[pl.ds(slot * station_blocks, station_blocks)]


def forward(sizes, first, shift, messages, values, turned):
    cell_blocks, station_blocks, pairs, epochs, slots = sizes
    rows = (slots * station_blocks + 8) // 8 * 8
    return pl.pallas_call(
        functools.partial(forward_kernel, sizes),
        out_shape=jax.ShapeDtypeStruct((slots, station_blocks, epochs, SBLOCK), F32),
        in_specs=[SMEM, SMEM] + [VMEM] * (slots + 2),
        out_specs=VMEM,
        scratch_shapes=list_scratch(sizes)
        + [
            pltpu.VMEM((rows, SBLOCK), F32),
            pltpu.VMEM((rows, SBLOCK), F32),
            pltpu.VMEM((slots * station_blocks + 1, epochs, SBLOCK), F32),
            pltpu.VMEM((2, COL_SIDE, SBLOCK), F32),
            pltpu.VMEM((2, 1, SBLOCK), F32),
            pltpu.VMEM((2, CBLOCK, LANES), F32),
        ],
        compiler_params=params(),
        cost_estimate=estimate(sizes, 0.1 if slots > 2 else 1),
        name="forward",
    )(first, shift, *messages, values, turned)


def estimate(sizes, part=1):
    cell_blocks, station_blocks, pairs, epochs, slots = sizes
    entries = station_blocks * pairs * slots // (2 * REACH + 1) * SBLOCK * CBLOCK
    return pl.CostEstimate(flops=int(2 * 1200 * entries * part), bytes_accessed=2**20, transcendentals=entries)


def adjoint_sums(sizes, first_ref, shift_ref, messages, residuals, images, cells_ref, total_ref, scratch):
    cell_blocks, station_blocks, pairs, epochs, slots = sizes
    list_ref, codes_ref, scalars_ref, sent, stations_ref, terms_ref, depths_ref, gaps_ref, lines_ref = scratch
    copy = send_codes(sizes, first_ref, messages, codes_ref, scalars_ref, sent)
    dummy = slots * station_blocks
    terms_ref[dummy] = jnp.zeros(terms_ref.shape[1:], BF16)
    stations_ref[slots] = jnp.zeros(stations_ref.shape[1:], F32)
    total_ref[...] = jnp.zeros_like(total_ref)
    per_block = SBLOCK // LANES
    lane_rows = station_blocks * per_block
    for slot in range(slots):
        places = [messages[slot][pl.ds(0, lane_rows), :] + shift_ref[slot], messages[slot][pl.ds(lane_rows, lane_rows), :]]
        places.append(jnp.zeros((LANES - 2 * lane_rows, LANES), F32))
        stations_ref[slot] = jnp.concatenate(places, axis=0).T
        for q in range(station_blocks):
            stacked = jnp.concatenate([residuals[slot][:, pl.ds(q * SBLOCK, SBLOCK)], images[slot][q]], axis=0)
            high, low = split(stacked)
            terms_ref[slot * station_blocks + q, pl.ds(0, 2 * epochs), :] = high
            terms_ref[slot * station_blocks + q, pl.ds(2 * epochs, 2 * epochs), :] = low
    count = list_pairs(sizes, copy, scalars_ref, list_ref)
    lane = lax.broadcasted_iota(jnp.int32, (1, LANES), 1)
    column = ((lane % COL_SIDE).astype(F32) + 0.5) / COL_SIDE
    line = ((lane // COL_SIDE).astype(F32) + 0.5) / COL_SIDE
    rows = CBLOCK // COL_SIDE
    chunks = CBLOCK // LANES

    def stage(i, k):
        code = list_ref[i]
        q, w = code // cell_blocks, code % cell_blocks
        slot, within = q // station_blocks, q % station_blocks
        depths_ref[k] = cells_ref[pl.ds(0, 1), pl.ds(pl.multiple_of(w * CBLOCK, CBLOCK), CBLOCK)]
        lines = line + (w % 2).astype(F32) * (rows / COL_SIDE)
        places = pltpu.roll(stations_ref[slot], (LANES - within * per_block) % LANES, 1)
        for part in range(per_block):
            at = pl.ds(part * LANES, LANES)
            across = jnp.broadcast_to(places[:, part : part + 1], (LANES, LANES)) - column
            gaps_ref[k, at, :] = across * across
            along = jnp.broadcast_to(places[:, lane_rows + part : lane_rows + part + 1], (LANES, LANES))
            lines_ref[k, at, :] = along - lines

    def issue(sums, i, k):
        q = list_ref[i] // cell_blocks
        depth = depths_ref[k]
        for part in range(per_block):
            pieces = ([], [])
            for at in range(part * LANES, (part + 1) * LANES, 16):
                across = gaps_ref[k, pl.ds(at, 16), :]
                along = lines_ref[k, pl.ds(at, 16), :]
                for unit in range(2):
                    near = []
                    for chunk in range(unit * chunks // 2, (unit + 1) * chunks // 2):
                        gap = along - chunk * (LANES // COL_SIDE) / COL_SIDE
                        squared = (across + gap * gap) + depth[:, chunk * LANES : (chunk + 1) * LANES]
                        near.append(split(inverse_cube(squared)))
                    pieces[unit].append([jnp.concatenate(terms, axis=1) for terms in zip(*near)])
            left = terms_ref[q, :, pl.ds(part * HALF, HALF)]
            for unit in range(2):
                multiply_add(sums[2 * k + unit], left, pieces[unit], unit, part)

    def collect(sums, i, k):
        w = list_ref[i] % cell_blocks
        for unit in range(2):
            both = pltpu.matmul_pop(sums[2 * k + unit])
            total_ref[w, :, pl.ds(unit * TILE, TILE)] += both[: 2 * epochs] + both[2 * epochs :]

    def run(*sums):
        pipelined(count, stage, functools.partial(issue, sums), functools.partial(collect, sums))

    pl.run_scoped(run, *accumulators(4 * epochs))


def slot_refs(slots, refs):
    messages, refs = refs[:slots], refs[slots:]
    arrays = slots - 1
    residuals, images, rest = refs[:arrays], refs[arrays : 2 * arrays], refs[2 * arrays :]
    return messages, *([pair.at[0], pair.at[1], *single] for pair, *single in (residuals, images)), rest


def near_kernel(sizes, first_ref, shift_ref, *refs):
    cell_blocks, station_blocks, pairs, epochs, slots = sizes
    messages, residuals, images, rest = slot_refs(slots, refs)
    cells_ref, direction_ref, old_ref, total_ref, sums_ref, *scratch = rest
    adjoint_sums(sizes, first_ref, shift_ref, messages, residuals, images, cells_ref, total_ref, scratch)

    def add(w, sums):
        at = pl.ds(pl.multiple_of(w * CBLOCK, CBLOCK), CBLOCK)
        direction, old = direction_ref[:, at], old_ref[:, at]
        return sums[0] + old * old, sums[1] + direction * direction

    zero = jnp.zeros((epochs, CBLOCK), F32)
    for i, total in enumerate(lax.fori_loop(0, cell_blocks, add, (zero, zero), unroll=4)):
        sums_ref[pl.ds(i, 1), :] = jnp.broadcast_to(jnp.sum(total).reshape(1, 1), (1, LANES))


def far_kernel(sizes, first_ref, shift_ref, *refs):
    cell_blocks, station_blocks, pairs, epochs, slots = sizes
    messages, residuals, images, rest = slot_refs(slots, refs)
    cells_ref, near_ref, sums_ref, model_ref, direction_ref, image_ref = rest[:6]
    constant_ref, slope_ref, stats_ref = rest[6:9]
    total_ref, *scratch = rest[9:]
    adjoint_sums(sizes, first_ref, shift_ref, messages, residuals, images, cells_ref, total_ref, scratch)
    zero = jnp.zeros((epochs, CBLOCK), F32)

    def combine(w, sums):
        at = pl.ds(pl.multiple_of(w * CBLOCK, CBLOCK), CBLOCK)
        total = (near_ref[w] + total_ref[w]) * cells_ref[pl.ds(1, 1), at]
        constant = total[:epochs] - DAMPING * model_ref[:, at]
        slope = total[epochs:] + DAMPING * direction_ref[:, at]
        constant_ref[:, at] = constant
        slope_ref[:, at] = slope
        return sums[0] + constant * slope, sums[1] + slope * slope

    cross, square = lax.fori_loop(0, cell_blocks, combine, (zero, zero), unroll=2)
    square = jnp.sum(square).reshape(1, 1)
    cross = jnp.sum(cross).reshape(1, 1)
    local_step = jnp.where(square > 0, cross / jnp.where(square > 0, square, 1.0), 0.0)

    def remainder(w, sums):
        at = pl.ds(pl.multiple_of(w * CBLOCK, CBLOCK), CBLOCK)
        slope = slope_ref[:, at]
        left = constant_ref[:, at] - local_step * slope
        return sums[0] + left * left, sums[1] + left * slope

    left_square, left_cross = lax.fori_loop(0, cell_blocks, remainder, (zero, zero), unroll=2)
    image = image_ref[0]
    stats = [
        sums_ref[pl.ds(0, 1), pl.ds(0, 1)],
        sums_ref[pl.ds(1, 1), pl.ds(0, 1)],
        jnp.sum(image * image).reshape(1, 1),
        local_step,
        jnp.sum(left_square).reshape(1, 1),
        jnp.sum(left_cross).reshape(1, 1),
        jnp.sqrt(square),
    ]
    lane = lax.broadcasted_iota(jnp.int32, (1, LANES), 1)
    row = jnp.zeros((1, LANES), F32)
    for i, value in enumerate(stats):
        row = jnp.where(lane == i, value, row)
    for i in range(stats_ref.shape[0]):
        stats_ref[i] = row


def adjoint(sizes, first, shift, messages, residuals, images, cell_rows, *others, ranks=None):
    cell_blocks, station_blocks, pairs, epochs, slots = sizes
    total = (cell_blocks, 2 * epochs, CBLOCK)
    scratch = list_scratch(sizes) + [
        pltpu.VMEM((slots + 1, LANES, LANES), F32),
        pltpu.VMEM((slots * station_blocks + 1, 4 * epochs, SBLOCK), BF16),
        pltpu.VMEM((2, 1, CBLOCK), F32),
        pltpu.VMEM((2, SBLOCK, LANES), F32),
        pltpu.VMEM((2, SBLOCK, LANES), F32),
    ]
    if ranks is None:
        kernel, shapes = near_kernel, [total, (2, LANES)]
    else:
        kernel, cells = far_kernel, (epochs, cell_blocks * CBLOCK)
        shapes = [cells, cells, (ranks, 1, LANES)]
        scratch = [pltpu.VMEM(total, F32)] + scratch
    return pl.pallas_call(
        functools.partial(kernel, sizes),
        out_shape=tuple(jax.ShapeDtypeStruct(shape, F32) for shape in shapes),
        in_specs=[SMEM, SMEM] + [VMEM] * (3 * slots - 1 + len(others)),
        out_specs=(VMEM,) * len(shapes),
        scratch_shapes=scratch,
        compiler_params=params(),
        cost_estimate=estimate(sizes),
        name="near" if ranks is None else "far",
    )(first, shift, *messages, *residuals, *images, cell_rows, *others)


def finish_kernel(
    stats_ref, constant_ref, slope_ref, model_ref, direction_ref, residual_ref, image_ref,
    model_out, residual_out, direction_out, new_model, new_residual, new_direction, sent,
):
    stats = stats_ref[...][:, 0, :]
    gamma_old, direction_square, image_square = (
        jnp.sum(stats[:, i : i + 1], axis=0, keepdims=True) for i in range(3)
    )
    step = gamma_old / (image_square + DAMPING * direction_square + GUARD)
    ahead = step - stats[:, 3:4]
    reach = ahead * stats[:, 6:7]
    gamma_new = jnp.sum(stats[:, 4:5] - 2.0 * ahead * stats[:, 5:6] + reach * reach, axis=0, keepdims=True)
    ratio = gamma_new / (gamma_old + GUARD)
    copies = []

    def send(i, source, target, at):
        copies.append(pltpu.make_async_copy(source.at[:, at], target.at[:, at], sent.at[i]))
        copies[-1].start()

    for q in range(image_ref.shape[1]):
        at = pl.ds(q * SBLOCK, SBLOCK)
        new_residual[:, at] = residual_ref[:, at] - step * image_ref[0, q]
    send(0, new_residual, residual_out, pl.ds(0, residual_ref.shape[1]))
    cells = model_ref.shape[1] // FINISH_PARTS
    for part in range(FINISH_PARTS):

        def block(w, unused):
            at = pl.ds(pl.multiple_of(part * cells + w * CBLOCK, CBLOCK), CBLOCK)
            direction = direction_ref[:, at]
            new_model[:, at] = model_ref[:, at] + step * direction
            new_direction[:, at] = (constant_ref[:, at] - step * slope_ref[:, at]) + ratio * direction
            return 0

        lax.fori_loop(0, cells // CBLOCK, block, 0, unroll=2)
        send(1 + 2 * part, new_model, model_out, pl.ds(part * cells, cells))
        send(2 + 2 * part, new_direction, direction_out, pl.ds(part * cells, cells))
    for copy in copies:
        copy.wait()


FINISH_PARTS = 4


def finish(stats, constant, slope, model_field, direction, residual, image):
    outs = (model_field.shape, residual.shape, direction.shape)
    return pl.pallas_call(
        finish_kernel,
        out_shape=tuple(jax.ShapeDtypeStruct(shape, F32) for shape in outs),
        in_specs=[VMEM] * 7,
        out_specs=(pl.BlockSpec(memory_space=pl.ANY),) * 3,
        scratch_shapes=[pltpu.VMEM(shape, F32) for shape in outs]
        + [pltpu.SemaphoreType.DMA((1 + 2 * FINISH_PARTS,))],
        compiler_params=params(),
        name="finish",
    )(stats, constant, slope, model_field, direction, residual, image)


def after(arrays, others):
    return lax.optimization_barrier((arrays, others))[0]


def shards(model_field, direction, old_grad, residual, block_pairs, depth_band, station_offsets):
    ranks = lax.axis_size("tile")
    tile_id = lax.axis_index("tile")
    epochs, cells = model_field.shape
    station_blocks, pairs = block_pairs.shape
    cell_blocks = cells // CBLOCK
    side = 2 * (tile_id % 2) - 1

    def to_partner(array):
        return lax.ppermute(array, "tile", [(i, i ^ 1) for i in range(ranks)])

    def across(message):
        ends = [(i, i + 1) for i in range(1, ranks - 1, 2)]
        return lax.ppermute(message, "tile", ends + [(j, i) for i, j in ends])

    def slots(*places):
        offsets = jnp.stack([multiple * side for multiple in places]).astype(jnp.int32)
        sizes = (cell_blocks, station_blocks, pairs, epochs, len(places))
        return sizes, cell_blocks * (REACH - offsets) + 1, offsets.astype(F32)

    near_slots, far_slots = slots(0, -1), slots(1, 2, -2)

    own, residual = pack(station_offsets, block_pairs, residual)
    partner = to_partner(own)
    near = [own, partner]
    partner_residual = to_partner(residual)
    arrived = across(pair_up(*near))
    values, cell_rows, turned = prepare(2.0 / math.sqrt(cells), after(depth_band, partner), direction)
    residuals = pair_up(residual, partner_residual)
    arrived = after(arrived, (values, residuals))
    far = [arrived[0], arrived[1], to_partner(arrived[0])]

    far_residuals = across(residuals)
    parts = forward(*far_slots, far, values, turned)
    parts, far_residuals = after((parts, far_residuals), (far_residuals, parts))
    returned = to_partner(parts[2])
    given = across(far_parts(parts, returned))
    mine = forward(*near_slots, after(near, returned), values, turned)
    given = after(given, mine)
    mine = small_call(add_kernel, mine.shape, "add", mine, given)
    images = both_images(mine, to_partner(mine))

    far_images = across(images)
    third_residual = to_partner(after(far_residuals[0], images))
    near_total, sums = adjoint(*near_slots, near, [residuals], [images], cell_rows, direction, old_grad)
    far_images, third_residual = after((far_images, third_residual), near_total)
    third_image = to_partner(far_images[0])
    constant, slope, stats = adjoint(
        *far_slots, far, [far_residuals, third_residual], [far_images, third_image], cell_rows,
        near_total, sums, model_field, direction, images, ranks=ranks,
    )
    stats = lax.all_to_all(stats, "tile", 0, 0)
    return finish(stats, constant, slope, model_field, direction, residual, images)


def solution(mesh):
    wide = P(None, ("groups", "tile"))
    mapped = jax.shard_map(
        shards,
        mesh=mesh,
        in_specs=(wide, wide, wide, wide, P(("groups", "tile"), None), P(("groups", "tile")), wide),
        out_specs=(wide, wide, wide),
        check_vma=False,
    )

    def step(*arrays):
        with jax.sharding.use_abstract_mesh(mesh.abstract_mesh):
            return mapped(*arrays)

    return step
```

```python
import functools
import math

import jax
import jax.numpy as jnp
from jax import lax
from jax.experimental import pallas as pl
from jax.experimental.pallas import tpu as pltpu
from jax.sharding import PartitionSpec as P

CBLOCK = 512
SBLOCK = 256
REACH = 2
BANDS = 16
COL_SIDE = 32
DEPTH_RANGE = 2.0
DEPTH_SHIFT = 0.25
DAMPING = 1.0
GUARD = 1e-06

F32 = jnp.float32
BF16 = jnp.bfloat16
LANES = 128
TILE = 256
HALF = TILE // 2

SMEM = pl.BlockSpec(memory_space=pltpu.SMEM)
VMEM = pl.BlockSpec(memory_space=pltpu.VMEM)


def params(mebibytes=16):
    return pltpu.CompilerParams(vmem_limit_bytes=mebibytes * 2**20)


def split(values):
    high = values.astype(BF16)
    return high, (values - high.astype(F32)).astype(BF16)


def dot(left, right):
    return jnp.dot(left, right, preferred_element_type=F32)


def pack_kernel(offsets_any, pairs_any, residual_any, message_ref, residual_ref, offsets_ref, pairs_ref, rows_ref, sent):
    copies = [
        pltpu.make_async_copy(offsets_any, offsets_ref, sent.at[0]),
        pltpu.make_async_copy(pairs_any, pairs_ref, sent.at[1]),
        pltpu.make_async_copy(residual_any, rows_ref, sent.at[2]),
    ]
    for copy in copies:
        copy.start()
    lines = offsets_ref.shape[1] // LANES
    rows, pairs = pairs_ref.shape
    message_ref[pl.ds(2 * lines, rows), :] = jnp.zeros((rows, LANES), F32)
    for copy in copies:
        copy.wait()
    for i in range(lines):
        at = pl.ds(i * LANES, LANES)
        message_ref[pl.ds(i, 1), :] = offsets_ref[pl.ds(0, 1), at]
        message_ref[pl.ds(lines + i, 1), :] = offsets_ref[pl.ds(1, 1), at]
    message_ref[pl.ds(2 * lines, rows), pl.ds(0, pairs)] = pairs_ref[...].astype(F32) + 1.0
    for q in range(rows):
        residual_ref[q] = rows_ref[:, pl.ds(q * SBLOCK, SBLOCK)]


def in_hbm(array):
    return pltpu.with_memory_space_constraint(array, pltpu.HBM)


def pack(station_offsets, block_pairs, residual):
    rows = 2 * station_offsets.shape[1] // LANES + block_pairs.shape[0]
    return pl.pallas_call(
        pack_kernel,
        out_shape=(jax.ShapeDtypeStruct((rows, LANES), F32), jax.ShapeDtypeStruct((block_pairs.shape[0], residual.shape[0], SBLOCK), F32)),
        in_specs=[pl.BlockSpec(memory_space=pl.ANY)] * 3,
        out_specs=(VMEM, VMEM),
        scratch_shapes=[
            pltpu.VMEM(station_offsets.shape, F32),
            pltpu.VMEM(block_pairs.shape, jnp.int32),
            pltpu.VMEM(residual.shape, F32),
            pltpu.SemaphoreType.DMA((3,)),
        ],
        compiler_params=params(2),
        name="pack",
    )(in_hbm(station_offsets), in_hbm(block_pairs), in_hbm(residual))


def far_parts_kernel(parts_ref, third_ref, message_ref):
    message_ref[0] = parts_ref[0] + third_ref[...]
    message_ref[1] = parts_ref[1]


def far_parts(parts, third):
    return small_call(far_parts_kernel, (2, *third.shape), "far_parts", parts, third)


def both_images_kernel(mine_ref, theirs_ref, images_ref):
    images_ref[0] = mine_ref[0] + theirs_ref[1]
    images_ref[1] = mine_ref[1] + theirs_ref[0]


def both_images(mine, theirs):
    return small_call(both_images_kernel, mine.shape, "both_images", mine, theirs)


def add_kernel(left_ref, right_ref, sum_ref):
    sum_ref[...] = left_ref[...] + right_ref[...]


def pair_kernel(first_ref, second_ref, message_ref):
    message_ref[0] = first_ref[...]
    message_ref[1] = second_ref[...]


def pair_up(first, second):
    return small_call(pair_kernel, (2, *first.shape), "pair", first, second)


def small_call(kernel, shape, name, *arrays):
    return pl.pallas_call(
        kernel,
        out_shape=jax.ShapeDtypeStruct(shape, F32),
        in_specs=[VMEM] * len(arrays),
        out_specs=VMEM,
        compiler_params=params(2),
        name=name,
    )(*arrays)


def prepare_kernel(scale, band_ref, band_row_ref, direction_ref, values_ref, cells_ref, turned_ref):
    blocks = values_ref.shape[0]
    epochs = direction_ref.shape[0]

    @pl.when(pl.program_id(0) == 0)
    def first():
        depth = (band_ref[...].astype(F32) + 0.5) * (DEPTH_RANGE / BANDS)
        turned_ref[...] = (depth * depth).T

    def block(w, unused):
        at = pl.ds(pl.multiple_of(w * CBLOCK, CBLOCK), CBLOCK)
        row = (band_row_ref[:, at].astype(F32) + 0.5) * (DEPTH_RANGE / BANDS)
        shifted = row + DEPTH_SHIFT
        factor = row * scale * (shifted * jnp.sqrt(shifted))
        cells_ref[pl.ds(0, 1), at] = row * row
        cells_ref[pl.ds(1, 1), at] = factor
        high, low = split(direction_ref[:, at] * factor)
        values_ref[w, pl.ds(0, epochs), :] = high
        values_ref[w, pl.ds(epochs, epochs), :] = low
        return 0

    lax.fori_loop(0, blocks, block, 0, unroll=4)


PARTS = 2


def prepare(scale, depth_band, direction):
    epochs, cells = direction.shape
    blocks = cells // CBLOCK
    return pl.pallas_call(
        functools.partial(prepare_kernel, scale),
        grid=(PARTS,),
        out_shape=(
            jax.ShapeDtypeStruct((blocks, 2 * epochs, CBLOCK), BF16),
            jax.ShapeDtypeStruct((2, cells), F32),
            jax.ShapeDtypeStruct((cells // LANES, LANES), F32),
        ),
        in_specs=[
            pl.BlockSpec((cells // LANES, LANES), lambda i: (0, 0)),
            pl.BlockSpec((1, cells // PARTS), lambda i: (0, i)),
            pl.BlockSpec((epochs, cells // PARTS), lambda i: (0, i)),
        ],
        out_specs=(
            pl.BlockSpec((blocks // PARTS, 2 * epochs, CBLOCK), lambda i: (i, 0, 0)),
            pl.BlockSpec((2, cells // PARTS), lambda i: (0, i)),
            VMEM,
        ),
        compiler_params=params(8),
        cost_estimate=pl.CostEstimate(flops=8 * epochs * cells, bytes_accessed=12 * epochs * cells, transcendentals=0),
        name="prepare",
    )(
        in_hbm(depth_band.reshape(cells // LANES, LANES)),
        in_hbm(depth_band.reshape(1, cells)),
        in_hbm(direction),
    )


def tile_offset(place):
    return place * (2 * (lax.axis_index("tile") % 2) - 1)


def send_codes(sizes, messages, codes_ref, scalars_ref, sent):
    cell_blocks, station_blocks, pairs, epochs, places = sizes
    q = lax.broadcasted_iota(jnp.int32, (station_blocks, LANES), 0)
    for slot, message_ref in enumerate(messages):
        codes = message_ref[pl.ds(message_ref.shape[0] - station_blocks, station_blocks), :]
        within = codes.astype(jnp.int32) - (cell_blocks * (REACH - tile_offset(places[slot])) + 1)
        hit = jnp.logical_and(within >= 0, within < cell_blocks)
        code = (slot * station_blocks + q) * cell_blocks + within
        codes_ref[pl.ds(slot * station_blocks, station_blocks), :] = jnp.where(hit, code, -1)
    copy = pltpu.make_async_copy(codes_ref, scalars_ref, sent)
    copy.start()
    return copy


def list_pairs(sizes, copy, scalars_ref, list_ref):
    cell_blocks, station_blocks, pairs, epochs, places = sizes
    slots = len(places)
    copy.wait()
    count = jnp.int32(0)
    for row in range(slots * station_blocks):
        for i in range(pairs):
            code = scalars_ref[row, i]
            list_ref[count] = code
            count = count + (code >= 0).astype(jnp.int32)
    for i in range(UNROLL + 4):
        list_ref[count + i] = slots * station_blocks * cell_blocks
    return count


def list_scratch(sizes):
    cell_blocks, station_blocks, pairs, epochs, places = sizes
    slots = len(places)
    return [
        pltpu.SMEM((slots * station_blocks * pairs + UNROLL + 4,), jnp.int32),
        pltpu.VMEM((slots * station_blocks, LANES), jnp.int32),
        pltpu.SMEM((slots * station_blocks, LANES), jnp.int32),
        pltpu.SemaphoreType.DMA(()),
    ]


UNROLL = 4


def pipelined(count, stage, issue, collect):
    stage(0, 0)
    stage(1, 1)
    issue(0, 0)

    def step(j, unused):
        for k in range(UNROLL):
            i, now, later = UNROLL * j + k, k % 2, 1 - k % 2
            issue(i + 1, later)
            stage(i + 2, now)
            collect(i, now)
        return 0

    rounds = (count + UNROLL - 2) // UNROLL
    lax.fori_loop(0, rounds, step, 0)
    collect(UNROLL * rounds, 0)


def multiply_add(sums_ref, left, pieces, unit, register):
    high, low = zip(*pieces)
    pltpu.matmul_push_rhs(jnp.concatenate(high + low, axis=0), register, unit)
    pltpu.matmul_acc_lhs(sums_ref, jnp.concatenate([left, left], axis=1), load_staged_rhs=register)


def accumulators(rows):
    return [pltpu.ACC(unit)((rows, TILE), F32) for unit in (0, 1)] * 2


def inverse_cube(squared):
    return lax.rsqrt(squared * squared * squared)


def forward_kernel(sizes, *refs):
    cell_blocks, station_blocks, pairs, epochs, places = sizes
    slots = len(places)
    messages = refs[:slots]
    values_ref, turned_ref = refs[slots : slots + 2]
    images_ref, list_ref, codes_ref, scalars_ref, sent, *scratch = refs[slots + 2 :]
    across_ref, along_ref, image_ref, gaps_ref, lines_ref, depths_ref = scratch
    copy = send_codes(sizes, messages, codes_ref, scalars_ref, sent)
    dummy = slots * station_blocks
    per_block = SBLOCK // LANES
    lines = station_blocks * per_block
    across_ref[pl.ds(dummy, 1), :] = jnp.zeros((1, SBLOCK), F32)
    along_ref[pl.ds(dummy, 1), :] = jnp.zeros((1, SBLOCK), F32)
    image_ref[...] = jnp.zeros_like(image_ref)
    for slot in range(slots):
        for i in range(lines):
            place = (pl.ds(slot * station_blocks + i // per_block, 1), pl.ds(i % per_block * LANES, LANES))
            across_ref[place] = messages[slot][pl.ds(i, 1), :] + tile_offset(places[slot]).astype(F32)
            along_ref[place] = messages[slot][pl.ds(lines + i, 1), :]
    count = list_pairs(sizes, copy, scalars_ref, list_ref)
    column = lax.broadcasted_iota(jnp.int32, (COL_SIDE, SBLOCK), 0).astype(F32)
    column = (column + 0.5) / COL_SIDE
    rows = CBLOCK // COL_SIDE
    line = (lax.broadcasted_iota(jnp.int32, (rows, SBLOCK), 0).astype(F32) + 0.5) / COL_SIDE

    def stage(i, k):
        code = list_ref[i]
        q, w = code // cell_blocks, code % cell_blocks
        across = across_ref[pl.ds(q, 1), :] - column
        gaps_ref[k] = across * across
        along = along_ref[pl.ds(q, 1), :] - (w % 2).astype(F32) * (rows / COL_SIDE) - line
        lines_ref[k] = along * along
        turned = pltpu.roll(turned_ref[...], (LANES - w * (CBLOCK // LANES)) % LANES, 1)
        for part in range(CBLOCK // LANES):
            depths_ref[k, pl.ds(part * LANES, LANES), :] = jnp.broadcast_to(turned[:, part : part + 1], (LANES, LANES))

    def issue(sums, i, k):
        w = list_ref[i] % cell_blocks
        across = gaps_ref[k]
        for tile in range(CBLOCK // HALF):
            pieces = []
            for at in range(0, HALF, COL_SIDE):
                y = (tile * HALF + at) // COL_SIDE
                depth = depths_ref[k, pl.ds(y * COL_SIDE, COL_SIDE), :]
                depth = jnp.concatenate([depth] * (SBLOCK // LANES), axis=1)
                along = lines_ref[k, pl.ds(y, 1), :]
                pieces.append(split(inverse_cube((across + along) + depth)))
            left = values_ref[w, :, pl.ds(tile * HALF, HALF)]
            multiply_add(sums[2 * k + tile % 2], left, pieces, tile % 2, tile // 2)

    def collect(sums, i, k):
        q = list_ref[i] // cell_blocks
        both = pltpu.matmul_pop(sums[2 * k]) + pltpu.matmul_pop(sums[2 * k + 1])
        image_ref[q] += both[:epochs] + both[epochs:]

    def run(*sums):
        pipelined(count, stage, functools.partial(issue, sums), functools.partial(collect, sums))

    pl.run_scoped(run, *accumulators(2 * epochs))
    for slot in range(slots):
        images_ref[slot] = image_ref[pl.ds(slot * station_blocks, station_blocks)]


def forward(sizes, messages, values, turned):
    cell_blocks, station_blocks, pairs, epochs, places = sizes
    slots = len(places)
    rows = (slots * station_blocks + 8) // 8 * 8
    return pl.pallas_call(
        functools.partial(forward_kernel, sizes),
        out_shape=jax.ShapeDtypeStruct((slots, station_blocks, epochs, SBLOCK), F32),
        in_specs=[VMEM] * (slots + 2),
        out_specs=VMEM,
        scratch_shapes=list_scratch(sizes)
        + [
            pltpu.VMEM((rows, SBLOCK), F32),
            pltpu.VMEM((rows, SBLOCK), F32),
            pltpu.VMEM((slots * station_blocks + 1, epochs, SBLOCK), F32),
            pltpu.VMEM((2, COL_SIDE, SBLOCK), F32),
            pltpu.VMEM((2, CBLOCK // COL_SIDE, SBLOCK), F32),
            pltpu.VMEM((2, CBLOCK, LANES), F32),
        ],
        compiler_params=params(),
        cost_estimate=estimate(sizes, 0.1 if slots > 2 else 1),
        name="forward",
    )(*messages, values, turned)


def estimate(sizes, part=1):
    cell_blocks, station_blocks, pairs, epochs, places = sizes
    slots = len(places)
    entries = station_blocks * pairs * slots // (2 * REACH + 1) * SBLOCK * CBLOCK
    return pl.CostEstimate(flops=int(2 * 1200 * entries * part), bytes_accessed=2**20, transcendentals=entries)


def adjoint_sums(sizes, messages, residuals, images, cells_ref, total_ref, scratch):
    cell_blocks, station_blocks, pairs, epochs, places = sizes
    slots = len(places)
    list_ref, codes_ref, scalars_ref, sent, stations_ref, terms_ref, depths_ref, gaps_ref, lines_ref = scratch
    copy = send_codes(sizes, messages, codes_ref, scalars_ref, sent)
    dummy = slots * station_blocks
    terms_ref[dummy] = jnp.zeros(terms_ref.shape[1:], BF16)
    stations_ref[slots] = jnp.zeros(stations_ref.shape[1:], F32)
    total_ref[...] = jnp.zeros_like(total_ref)
    per_block = SBLOCK // LANES
    lane_rows = station_blocks * per_block
    for slot in range(slots):
        shift = tile_offset(places[slot]).astype(F32)
        rows = [messages[slot][pl.ds(0, lane_rows), :] + shift, messages[slot][pl.ds(lane_rows, lane_rows), :]]
        rows.append(jnp.zeros((LANES - 2 * lane_rows, LANES), F32))
        stations_ref[slot] = jnp.concatenate(rows, axis=0).T
        for q in range(station_blocks):
            stacked = jnp.concatenate([residuals[slot][q], images[slot][q]], axis=0)
            high, low = split(stacked)
            terms_ref[slot * station_blocks + q, pl.ds(0, 2 * epochs), :] = high
            terms_ref[slot * station_blocks + q, pl.ds(2 * epochs, 2 * epochs), :] = low
    count = list_pairs(sizes, copy, scalars_ref, list_ref)
    lane = lax.broadcasted_iota(jnp.int32, (1, LANES), 1)
    column = ((lane % COL_SIDE).astype(F32) + 0.5) / COL_SIDE
    line = ((lane // COL_SIDE).astype(F32) + 0.5) / COL_SIDE
    rows = CBLOCK // COL_SIDE
    chunks = CBLOCK // LANES
    stride = LANES / COL_SIDE / COL_SIDE

    def stage(i, k):
        code = list_ref[i]
        q, w = code // cell_blocks, code % cell_blocks
        slot, within = q // station_blocks, q % station_blocks
        depths_ref[k] = cells_ref[pl.ds(0, 1), pl.ds(pl.multiple_of(w * CBLOCK, CBLOCK), CBLOCK)]
        lines = line + (w % 2).astype(F32) * (rows / COL_SIDE)
        places = pltpu.roll(stations_ref[slot], (LANES - within * per_block) % LANES, 1)
        for part in range(per_block):
            at = pl.ds(part * LANES, LANES)
            across = jnp.broadcast_to(places[:, part : part + 1], (LANES, LANES)) - column
            gaps_ref[k, at, :] = across * across
            along = jnp.broadcast_to(places[:, lane_rows + part : lane_rows + part + 1], (LANES, LANES))
            lines_ref[k, at, :] = along - lines

    def issue(sums, i, k):
        q = list_ref[i] // cell_blocks
        depth = depths_ref[k]
        for part in range(per_block):
            pieces = ([], [])
            for at in range(part * LANES, (part + 1) * LANES, 16):
                across = gaps_ref[k, pl.ds(at, 16), :]
                along = lines_ref[k, pl.ds(at, 16), :]
                level = across + along * along
                slope = stride * stride - 2 * stride * along
                for unit in range(2):
                    near = []
                    for chunk in range(unit * chunks // 2, (unit + 1) * chunks // 2):
                        squared = level + depth[:, chunk * LANES : (chunk + 1) * LANES]
                        near.append(split(inverse_cube(squared)))
                        if chunk < chunks - 1:
                            level = level + slope
                            slope = slope + 2 * stride * stride
                    pieces[unit].append([jnp.concatenate(terms, axis=1) for terms in zip(*near)])
            left = terms_ref[q, :, pl.ds(part * HALF, HALF)]
            for unit in range(2):
                multiply_add(sums[2 * k + unit], left, pieces[unit], unit, part)

    def collect(sums, i, k):
        w = list_ref[i] % cell_blocks
        for unit in range(2):
            both = pltpu.matmul_pop(sums[2 * k + unit])
            total_ref[w, :, pl.ds(unit * TILE, TILE)] += both[: 2 * epochs] + both[2 * epochs :]

    def run(*sums):
        pipelined(count, stage, functools.partial(issue, sums), functools.partial(collect, sums))

    pl.run_scoped(run, *accumulators(4 * epochs))


def slot_refs(slots, refs):
    messages, (residuals, images), rest = refs[:slots], refs[slots : slots + 2], refs[slots + 2 :]
    residuals, images = [residuals.at[0], residuals.at[1]], [images.at[0], images.at[1]]
    if slots == 3:
        third, *rest = rest
        residuals.append(third.at[0])
        images.append(third.at[1])
    return messages, residuals, images, rest


def near_kernel(sizes, *refs):
    cell_blocks, station_blocks, pairs, epochs, places = sizes
    slots = len(places)
    messages, residuals, images, rest = slot_refs(slots, refs)
    cells_ref, direction_ref, old_ref, total_ref, sums_ref, *scratch = rest
    adjoint_sums(sizes, messages, residuals, images, cells_ref, total_ref, scratch)

    def add(w, sums):
        at = pl.ds(pl.multiple_of(w * CBLOCK, CBLOCK), CBLOCK)
        direction, old = direction_ref[:, at], old_ref[:, at]
        return sums[0] + old * old, sums[1] + direction * direction

    zero = jnp.zeros((epochs, CBLOCK), F32)
    for i, total in enumerate(lax.fori_loop(0, cell_blocks, add, (zero, zero), unroll=4)):
        sums_ref[pl.ds(i, 1), :] = jnp.broadcast_to(jnp.sum(total).reshape(1, 1), (1, LANES))


def far_kernel(sizes, *refs):
    cell_blocks, station_blocks, pairs, epochs, places = sizes
    slots = len(places)
    messages, residuals, images, rest = slot_refs(slots, refs)
    cells_ref, near_ref, sums_ref, model_ref, direction_ref, image_ref = rest[:6]
    constant_ref, slope_ref, stats_ref = rest[6:9]
    total_ref, *scratch = rest[9:]
    adjoint_sums(sizes, messages, residuals, images, cells_ref, total_ref, scratch)
    zero = jnp.zeros((epochs, CBLOCK), F32)

    def combine(w, sums):
        at = pl.ds(pl.multiple_of(w * CBLOCK, CBLOCK), CBLOCK)
        total = (near_ref[w] + total_ref[w]) * cells_ref[pl.ds(1, 1), at]
        constant = total[:epochs] - DAMPING * model_ref[:, at]
        slope = total[epochs:] + DAMPING * direction_ref[:, at]
        constant_ref[:, at] = constant
        slope_ref[:, at] = slope
        return sums[0] + constant * slope, sums[1] + slope * slope

    cross, square = lax.fori_loop(0, cell_blocks, combine, (zero, zero), unroll=2)
    square = jnp.sum(square).reshape(1, 1)
    cross = jnp.sum(cross).reshape(1, 1)
    local_step = jnp.where(square > 0, cross / jnp.where(square > 0, square, 1.0), 0.0)

    def remainder(w, sums):
        at = pl.ds(pl.multiple_of(w * CBLOCK, CBLOCK), CBLOCK)
        slope = slope_ref[:, at]
        left = constant_ref[:, at] - local_step * slope
        return sums[0] + left * left, sums[1] + left * slope

    left_square, left_cross = lax.fori_loop(0, cell_blocks, remainder, (zero, zero), unroll=2)
    image = image_ref[0]
    stats = [
        sums_ref[pl.ds(0, 1), pl.ds(0, 1)],
        sums_ref[pl.ds(1, 1), pl.ds(0, 1)],
        jnp.sum(image * image).reshape(1, 1),
        local_step,
        jnp.sum(left_square).reshape(1, 1),
        jnp.sum(left_cross).reshape(1, 1),
        jnp.sqrt(square),
    ]
    lane = lax.broadcasted_iota(jnp.int32, (1, LANES), 1)
    row = jnp.zeros((1, LANES), F32)
    for i, value in enumerate(stats):
        row = jnp.where(lane == i, value, row)
    for i in range(stats_ref.shape[0]):
        stats_ref[i] = row


def adjoint(sizes, messages, terms, cell_rows, *others, ranks=None):
    cell_blocks, station_blocks, pairs, epochs, places = sizes
    slots = len(places)
    total = (cell_blocks, 2 * epochs, CBLOCK)
    scratch = list_scratch(sizes) + [
        pltpu.VMEM((slots + 1, LANES, LANES), F32),
        pltpu.VMEM((slots * station_blocks + 1, 4 * epochs, SBLOCK), BF16),
        pltpu.VMEM((2, 1, CBLOCK), F32),
        pltpu.VMEM((2, SBLOCK, LANES), F32),
        pltpu.VMEM((2, SBLOCK, LANES), F32),
    ]
    if ranks is None:
        kernel, shapes = near_kernel, [total, (2, LANES)]
    else:
        kernel, cells = far_kernel, (epochs, cell_blocks * CBLOCK)
        shapes = [cells, cells, (ranks, 1, LANES)]
        scratch = [pltpu.VMEM(total, F32)] + scratch
    return pl.pallas_call(
        functools.partial(kernel, sizes),
        out_shape=tuple(jax.ShapeDtypeStruct(shape, F32) for shape in shapes),
        in_specs=[VMEM] * (slots + len(terms) + 1 + len(others)),
        out_specs=(VMEM,) * len(shapes),
        scratch_shapes=scratch,
        compiler_params=params(),
        cost_estimate=estimate(sizes),
        name="near" if ranks is None else "far",
    )(*messages, *terms, cell_rows, *others)


def finish_kernel(
    stats_ref, constant_ref, slope_ref, model_ref, direction_ref, residual_ref, image_ref,
    model_out, residual_out, direction_out, new_model, new_residual, new_direction, sent,
):
    stats = stats_ref[...][:, 0, :]
    gamma_old, direction_square, image_square = (
        jnp.sum(stats[:, i : i + 1], axis=0, keepdims=True) for i in range(3)
    )
    step = gamma_old / (image_square + DAMPING * direction_square + GUARD)
    ahead = step - stats[:, 3:4]
    reach = ahead * stats[:, 6:7]
    gamma_new = jnp.sum(stats[:, 4:5] - 2.0 * ahead * stats[:, 5:6] + reach * reach, axis=0, keepdims=True)
    ratio = gamma_new / (gamma_old + GUARD)
    copies = []

    def send(i, source, target, at):
        copies.append(pltpu.make_async_copy(source.at[:, at], target.at[:, at], sent.at[i]))
        copies[-1].start()

    for q in range(image_ref.shape[1]):
        at = pl.ds(q * SBLOCK, SBLOCK)
        new_residual[:, at] = residual_ref[q] - step * image_ref[0, q]
    send(0, new_residual, residual_out, pl.ds(0, new_residual.shape[1]))
    cells = model_ref.shape[1] // FINISH_PARTS
    for part in range(FINISH_PARTS):

        def block(w, unused):
            at = pl.ds(pl.multiple_of(part * cells + w * CBLOCK, CBLOCK), CBLOCK)
            direction = direction_ref[:, at]
            new_model[:, at] = model_ref[:, at] + step * direction
            new_direction[:, at] = (constant_ref[:, at] - step * slope_ref[:, at]) + ratio * direction
            return 0

        lax.fori_loop(0, cells // CBLOCK, block, 0, unroll=2)
        send(1 + 2 * part, new_model, model_out, pl.ds(part * cells, cells))
        send(2 + 2 * part, new_direction, direction_out, pl.ds(part * cells, cells))
    for copy in copies:
        copy.wait()


FINISH_PARTS = 4


def finish(stats, constant, slope, model_field, direction, residual, image):
    blocks, epochs, _ = residual.shape
    outs = (model_field.shape, (epochs, blocks * SBLOCK), direction.shape)
    return pl.pallas_call(
        finish_kernel,
        out_shape=tuple(jax.ShapeDtypeStruct(shape, F32) for shape in outs),
        in_specs=[VMEM] * 7,
        out_specs=(pl.BlockSpec(memory_space=pl.ANY),) * 3,
        scratch_shapes=[pltpu.VMEM(shape, F32) for shape in outs]
        + [pltpu.SemaphoreType.DMA((1 + 2 * FINISH_PARTS,))],
        compiler_params=params(),
        name="finish",
    )(stats, constant, slope, model_field, direction, residual, image)


def after(arrays, others):
    return lax.optimization_barrier((arrays, others))[0]


def shards(model_field, direction, old_grad, residual, block_pairs, depth_band, station_offsets):
    ranks = lax.axis_size("tile")
    epochs, cells = model_field.shape
    station_blocks, pairs = block_pairs.shape
    cell_blocks = cells // CBLOCK

    def to_partner(array):
        return lax.ppermute(array, "tile", [(i, i ^ 1) for i in range(ranks)])

    def across(message):
        ends = [(i, i + 1) for i in range(1, ranks - 1, 2)]
        return lax.ppermute(message, "tile", ends + [(j, i) for i, j in ends])

    sizes = (cell_blocks, station_blocks, pairs, epochs)
    near_slots, far_slots = (*sizes, (0, -1)), (*sizes, (1, 2, -2))

    own, residual = pack(station_offsets, block_pairs, residual)
    partner = to_partner(own)
    near = [own, partner]
    partner_residual = to_partner(residual)
    arrived = across(pair_up(*near))
    values, cell_rows, turned = prepare(2.0 / math.sqrt(cells), after(depth_band, partner), direction)
    residuals = pair_up(residual, partner_residual)
    arrived = after(arrived, (values, residuals))
    far = [arrived[0], arrived[1], to_partner(arrived[0])]

    far_residuals = across(residuals)
    parts = forward(far_slots, far, values, turned)
    parts, far_residuals = after((parts, far_residuals), (far_residuals, parts))
    returned = to_partner(parts[2])
    given = across(far_parts(parts, returned))
    mine = forward(near_slots, after(near, returned), values, turned)
    given = after(given, mine)
    mine = small_call(add_kernel, mine.shape, "add", mine, given)
    images = both_images(mine, to_partner(mine))

    far_images = across(images)
    near_total, sums = adjoint(near_slots, near, [residuals, images], cell_rows, direction, old_grad)
    far_images = after(far_images, near_total)
    thirds = to_partner(pair_up(far_residuals[0], far_images[0]))
    constant, slope, stats = adjoint(
        far_slots, far, [far_residuals, far_images, thirds], cell_rows,
        near_total, sums, model_field, direction, images, ranks=ranks,
    )
    stats = lax.all_to_all(stats, "tile", 0, 0)
    return finish(stats, constant, slope, model_field, direction, residual, images)


def solution(mesh):
    wide = P(None, ("groups", "tile"))
    mapped = jax.shard_map(
        shards,
        mesh=mesh,
        in_specs=(wide, wide, wide, wide, P(("groups", "tile"), None), P(("groups", "tile")), wide),
        out_specs=(wide, wide, wide),
        check_vma=False,
    )

    def step(*arrays):
        with jax.sharding.use_abstract_mesh(mesh.abstract_mesh):
            return mapped(*arrays)

    return step
```

```python
import functools
import math

import jax
import jax.numpy as jnp
from jax import lax
from jax.experimental import pallas as pl
from jax.experimental.pallas import tpu as pltpu
from jax.sharding import PartitionSpec as P

CBLOCK = 512
SBLOCK = 256
REACH = 2
BANDS = 16
COL_SIDE = 32
DEPTH_RANGE = 2.0
DEPTH_SHIFT = 0.25
DAMPING = 1.0
GUARD = 1e-06

F32 = jnp.float32
BF16 = jnp.bfloat16
LANES = 128
TILE = 256
HALF = TILE // 2

SMEM = pl.BlockSpec(memory_space=pltpu.SMEM)
VMEM = pl.BlockSpec(memory_space=pltpu.VMEM)


def params(mebibytes=16):
    return pltpu.CompilerParams(vmem_limit_bytes=mebibytes * 2**20)


def parts_of(number, size):
    assert size & (size - 1) == 0
    return number >> (size.bit_length() - 1), number & (size - 1)


def split(values):
    high = values.astype(BF16)
    return high, (values - high.astype(F32)).astype(BF16)


def dot(left, right):
    return jnp.dot(left, right, preferred_element_type=F32)


def pack_kernel(offsets_any, pairs_any, residual_any, message_ref, residual_ref, offsets_ref, pairs_ref, rows_ref, sent):
    copies = [
        pltpu.make_async_copy(offsets_any, offsets_ref, sent.at[0]),
        pltpu.make_async_copy(pairs_any, pairs_ref, sent.at[1]),
        pltpu.make_async_copy(residual_any, rows_ref, sent.at[2]),
    ]
    for copy in copies:
        copy.start()
    lines = offsets_ref.shape[1] // LANES
    rows, pairs = pairs_ref.shape
    message_ref[pl.ds(2 * lines, rows), :] = jnp.zeros((rows, LANES), F32)
    for copy in copies:
        copy.wait()
    for i in range(lines):
        at = pl.ds(i * LANES, LANES)
        message_ref[pl.ds(i, 1), :] = offsets_ref[pl.ds(0, 1), at]
        message_ref[pl.ds(lines + i, 1), :] = offsets_ref[pl.ds(1, 1), at]
    message_ref[pl.ds(2 * lines, rows), pl.ds(0, pairs)] = pairs_ref[...].astype(F32) + 1.0
    for q in range(rows):
        residual_ref[q] = rows_ref[:, pl.ds(q * SBLOCK, SBLOCK)]


def in_hbm(array):
    return pltpu.with_memory_space_constraint(array, pltpu.HBM)


def pack(station_offsets, block_pairs, residual):
    rows = 2 * station_offsets.shape[1] // LANES + block_pairs.shape[0]
    return pl.pallas_call(
        pack_kernel,
        out_shape=(jax.ShapeDtypeStruct((rows, LANES), F32), jax.ShapeDtypeStruct((block_pairs.shape[0], residual.shape[0], SBLOCK), F32)),
        in_specs=[pl.BlockSpec(memory_space=pl.ANY)] * 3,
        out_specs=(VMEM, VMEM),
        scratch_shapes=[
            pltpu.VMEM(station_offsets.shape, F32),
            pltpu.VMEM(block_pairs.shape, jnp.int32),
            pltpu.VMEM(residual.shape, F32),
            pltpu.SemaphoreType.DMA((3,)),
        ],
        compiler_params=params(2),
        name="pack",
    )(in_hbm(station_offsets), in_hbm(block_pairs), in_hbm(residual))


def far_parts_kernel(parts_ref, third_ref, message_ref):
    message_ref[0] = parts_ref[0] + third_ref[...]
    message_ref[1] = parts_ref[1]


def far_parts(parts, third):
    return small_call(far_parts_kernel, (2, *third.shape), "far_parts", parts, third)


def both_images_kernel(mine_ref, theirs_ref, images_ref):
    images_ref[0] = mine_ref[0] + theirs_ref[1]
    images_ref[1] = mine_ref[1] + theirs_ref[0]


def both_images(mine, theirs):
    return small_call(both_images_kernel, mine.shape, "both_images", mine, theirs)


def add_kernel(left_ref, right_ref, sum_ref):
    sum_ref[...] = left_ref[...] + right_ref[...]


def pair_kernel(first_ref, second_ref, message_ref):
    message_ref[0] = first_ref[...]
    message_ref[1] = second_ref[...]


def pair_up(first, second):
    return small_call(pair_kernel, (2, *first.shape), "pair", first, second)


def small_call(kernel, shape, name, *arrays):
    return pl.pallas_call(
        kernel,
        out_shape=jax.ShapeDtypeStruct(shape, F32),
        in_specs=[VMEM] * len(arrays),
        out_specs=VMEM,
        compiler_params=params(2),
        name=name,
    )(*arrays)


def prepare_kernel(scale, band_ref, band_row_ref, direction_ref, values_ref, cells_ref, turned_ref):
    blocks = values_ref.shape[0]
    epochs = direction_ref.shape[0]

    @pl.when(pl.program_id(0) == 0)
    def first():
        depth = (band_ref[...].astype(F32) + 0.5) * (DEPTH_RANGE / BANDS)
        turned_ref[...] = (depth * depth).T

    def block(w, unused):
        at = pl.ds(pl.multiple_of(w * CBLOCK, CBLOCK), CBLOCK)
        row = (band_row_ref[:, at].astype(F32) + 0.5) * (DEPTH_RANGE / BANDS)
        shifted = row + DEPTH_SHIFT
        factor = row * scale * (shifted * jnp.sqrt(shifted))
        cells_ref[pl.ds(0, 1), at] = row * row
        cells_ref[pl.ds(1, 1), at] = factor
        high, low = split(direction_ref[:, at] * factor)
        values_ref[w, pl.ds(0, epochs), :] = high
        values_ref[w, pl.ds(epochs, epochs), :] = low
        return 0

    lax.fori_loop(0, blocks, block, 0, unroll=4)


PARTS = 2


def prepare(scale, depth_band, direction):
    epochs, cells = direction.shape
    blocks = cells // CBLOCK
    return pl.pallas_call(
        functools.partial(prepare_kernel, scale),
        grid=(PARTS,),
        out_shape=(
            jax.ShapeDtypeStruct((blocks, 2 * epochs, CBLOCK), BF16),
            jax.ShapeDtypeStruct((2, cells), F32),
            jax.ShapeDtypeStruct((cells // LANES, LANES), F32),
        ),
        in_specs=[
            pl.BlockSpec((cells // LANES, LANES), lambda i: (0, 0)),
            pl.BlockSpec((1, cells // PARTS), lambda i: (0, i)),
            pl.BlockSpec((epochs, cells // PARTS), lambda i: (0, i)),
        ],
        out_specs=(
            pl.BlockSpec((blocks // PARTS, 2 * epochs, CBLOCK), lambda i: (i, 0, 0)),
            pl.BlockSpec((2, cells // PARTS), lambda i: (0, i)),
            VMEM,
        ),
        compiler_params=params(8),
        cost_estimate=pl.CostEstimate(flops=8 * epochs * cells, bytes_accessed=12 * epochs * cells, transcendentals=0),
        name="prepare",
    )(
        in_hbm(depth_band.reshape(cells // LANES, LANES)),
        in_hbm(depth_band.reshape(1, cells)),
        in_hbm(direction),
    )


def tile_offset(place):
    return place * (2 * (lax.axis_index("tile") & 1) - 1)


def send_codes(sizes, messages, codes_ref, scalars_ref, sent):
    cell_blocks, station_blocks, pairs, epochs, places = sizes
    q = lax.broadcasted_iota(jnp.int32, (station_blocks, LANES), 0)
    for slot, message_ref in enumerate(messages):
        codes = message_ref[pl.ds(message_ref.shape[0] - station_blocks, station_blocks), :]
        within = codes.astype(jnp.int32) - (cell_blocks * (REACH - tile_offset(places[slot])) + 1)
        hit = jnp.logical_and(within >= 0, within < cell_blocks)
        code = (slot * station_blocks + q) * cell_blocks + within
        codes_ref[pl.ds(slot * station_blocks, station_blocks), :] = jnp.where(hit, code, -1)
    copy = pltpu.make_async_copy(codes_ref, scalars_ref, sent)
    copy.start()
    return copy


def list_pairs(sizes, copy, scalars_ref, list_ref):
    cell_blocks, station_blocks, pairs, epochs, places = sizes
    slots = len(places)
    copy.wait()
    count = jnp.int32(0)
    for row in range(slots * station_blocks):
        for i in range(pairs):
            code = scalars_ref[row, i]
            list_ref[count] = code
            count = count + (code >= 0).astype(jnp.int32)
    for i in range(2 * UNROLL):
        list_ref[count + i] = slots * station_blocks * cell_blocks
    return count


def list_scratch(sizes):
    cell_blocks, station_blocks, pairs, epochs, places = sizes
    slots = len(places)
    return [
        pltpu.SMEM((slots * station_blocks * pairs + 2 * UNROLL,), jnp.int32),
        pltpu.VMEM((slots * station_blocks, LANES), jnp.int32),
        pltpu.SMEM((slots * station_blocks, LANES), jnp.int32),
        pltpu.SemaphoreType.DMA(()),
    ]


UNROLL = 4


def pipelined(count, stage, issue, collect):
    stage(0, 0)
    stage(1, 1)
    issue(0, 0)

    def step(j, unused):
        for k in range(UNROLL):
            i = UNROLL * j + k
            issue(i + 1, (k + 1) % 2)
            stage(i + 2, k % 2)
            collect(i, k % 2)
        return 0

    rounds = (count + UNROLL - 2) // UNROLL
    lax.fori_loop(0, rounds, step, 0)
    collect(UNROLL * rounds, 0)


def multiply_add(sums_ref, left, pieces, unit, register):
    high, low = zip(*pieces)
    pltpu.matmul_push_rhs(jnp.concatenate(high + low, axis=0), register, unit)
    pltpu.matmul_acc_lhs(sums_ref, jnp.concatenate([left, left], axis=1), load_staged_rhs=register)


def accumulators(rows):
    return [pltpu.ACC(unit)((rows, TILE), F32) for unit in (0, 1)] * 2


def inverse_cube(squared):
    return lax.rsqrt(squared * squared * squared)


def forward_kernel(sizes, *refs):
    cell_blocks, station_blocks, pairs, epochs, places = sizes
    slots = len(places)
    messages = refs[:slots]
    values_ref, turned_ref = refs[slots : slots + 2]
    images_ref, list_ref, codes_ref, scalars_ref, sent, *scratch = refs[slots + 2 :]
    across_ref, along_ref, image_ref, gaps_ref, lines_ref, depths_ref = scratch
    copy = send_codes(sizes, messages, codes_ref, scalars_ref, sent)
    dummy = slots * station_blocks
    per_block = SBLOCK // LANES
    lines = station_blocks * per_block
    across_ref[pl.ds(dummy, 1), :] = jnp.zeros((1, SBLOCK), F32)
    along_ref[pl.ds(dummy, 1), :] = jnp.zeros((1, SBLOCK), F32)
    image_ref[...] = jnp.zeros_like(image_ref)
    for slot in range(slots):
        for i in range(lines):
            place = (pl.ds(slot * station_blocks + i // per_block, 1), pl.ds(i % per_block * LANES, LANES))
            across_ref[place] = messages[slot][pl.ds(i, 1), :] + tile_offset(places[slot]).astype(F32)
            along_ref[place] = messages[slot][pl.ds(lines + i, 1), :]
    count = list_pairs(sizes, copy, scalars_ref, list_ref)
    column = lax.broadcasted_iota(jnp.int32, (COL_SIDE, SBLOCK), 0).astype(F32)
    column = (column + 0.5) / COL_SIDE
    rows = CBLOCK // COL_SIDE
    line = (lax.broadcasted_iota(jnp.int32, (rows, SBLOCK), 0).astype(F32) + 0.5) / COL_SIDE

    def stage(i, k):
        code = list_ref[i]
        q, w = parts_of(code, cell_blocks)
        across = across_ref[pl.ds(q, 1), :] - column
        gaps_ref[k] = across * across
        along = along_ref[pl.ds(q, 1), :] - (w & 1).astype(F32) * (rows / COL_SIDE) - line
        lines_ref[k] = along * along
        turned = pltpu.roll(turned_ref[...], (LANES - w * (CBLOCK // LANES)) & (LANES - 1), 1)
        for part in range(CBLOCK // LANES):
            depths_ref[k, pl.ds(part * LANES, LANES), :] = jnp.broadcast_to(turned[:, part : part + 1], (LANES, LANES))

    def issue(sums, i, k):
        w = list_ref[i] & (cell_blocks - 1)
        across = gaps_ref[k]
        for tile in range(CBLOCK // HALF):
            pieces = []
            for at in range(0, HALF, COL_SIDE):
                y = (tile * HALF + at) // COL_SIDE
                depth = depths_ref[k, pl.ds(y * COL_SIDE, COL_SIDE), :]
                depth = jnp.concatenate([depth] * (SBLOCK // LANES), axis=1)
                along = lines_ref[k, pl.ds(y, 1), :]
                pieces.append(split(inverse_cube((across + along) + depth)))
            left = values_ref[w, :, pl.ds(tile * HALF, HALF)]
            multiply_add(sums[2 * k + tile % 2], left, pieces, tile % 2, tile // 2)

    def collect(sums, i, k):
        q, _ = parts_of(list_ref[i], cell_blocks)
        both = pltpu.matmul_pop(sums[2 * k]) + pltpu.matmul_pop(sums[2 * k + 1])
        image_ref[q] += both[:epochs] + both[epochs:]

    def run(*sums):
        pipelined(count, stage, functools.partial(issue, sums), functools.partial(collect, sums))

    pl.run_scoped(run, *accumulators(2 * epochs))
    for slot in range(slots):
        images_ref[slot] = image_ref[pl.ds(slot * station_blocks, station_blocks)]


def forward(sizes, messages, values, turned):
    cell_blocks, station_blocks, pairs, epochs, places = sizes
    slots = len(places)
    rows = (slots * station_blocks + 8) // 8 * 8
    return pl.pallas_call(
        functools.partial(forward_kernel, sizes),
        out_shape=jax.ShapeDtypeStruct((slots, station_blocks, epochs, SBLOCK), F32),
        in_specs=[VMEM] * (slots + 2),
        out_specs=VMEM,
        scratch_shapes=list_scratch(sizes)
        + [
            pltpu.VMEM((rows, SBLOCK), F32),
            pltpu.VMEM((rows, SBLOCK), F32),
            pltpu.VMEM((slots * station_blocks + 1, epochs, SBLOCK), F32),
            pltpu.VMEM((2, COL_SIDE, SBLOCK), F32),
            pltpu.VMEM((2, CBLOCK // COL_SIDE, SBLOCK), F32),
            pltpu.VMEM((2, CBLOCK, LANES), F32),
        ],
        compiler_params=params(),
        cost_estimate=estimate(sizes, 0.1 if slots > 2 else 1),
        name="forward",
    )(*messages, values, turned)


def estimate(sizes, part=1):
    cell_blocks, station_blocks, pairs, epochs, places = sizes
    slots = len(places)
    entries = station_blocks * pairs * slots // (2 * REACH + 1) * SBLOCK * CBLOCK
    return pl.CostEstimate(flops=int(2 * 1200 * entries * part), bytes_accessed=2**20, transcendentals=entries)


def adjoint_sums(sizes, messages, residuals, images, cells_ref, total_ref, scratch, clear):
    cell_blocks, station_blocks, pairs, epochs, places = sizes
    slots = len(places)
    list_ref, codes_ref, scalars_ref, sent, stations_ref, terms_ref, depths_ref, gaps_ref, lines_ref = scratch
    copy = send_codes(sizes, messages, codes_ref, scalars_ref, sent)
    dummy = slots * station_blocks
    stations_ref[slots] = jnp.zeros(stations_ref.shape[1:], F32)
    per_block = SBLOCK // LANES
    lane_rows = station_blocks * per_block
    for slot in range(slots):
        shift = tile_offset(places[slot]).astype(F32)
        rows = [messages[slot][pl.ds(0, lane_rows), :] + shift, messages[slot][pl.ds(lane_rows, lane_rows), :]]
        rows.append(jnp.zeros((LANES - 2 * lane_rows, LANES), F32))
        stations_ref[slot] = jnp.concatenate(rows, axis=0).T
    if clear:
        total_ref[...] = jnp.zeros_like(total_ref)
    count = list_pairs(sizes, copy, scalars_ref, list_ref)
    terms_ref[dummy] = jnp.zeros(terms_ref.shape[1:], BF16)
    for slot in range(slots):
        for q in range(station_blocks):
            stacked = jnp.concatenate([residuals[slot][q], images[slot][q]], axis=0)
            high, low = split(stacked)
            terms_ref[slot * station_blocks + q, pl.ds(0, 2 * epochs), :] = high
            terms_ref[slot * station_blocks + q, pl.ds(2 * epochs, 2 * epochs), :] = low
    lane = lax.broadcasted_iota(jnp.int32, (1, LANES), 1)
    column = ((lane % COL_SIDE).astype(F32) + 0.5) / COL_SIDE
    line = ((lane // COL_SIDE).astype(F32) + 0.5) / COL_SIDE
    rows = CBLOCK // COL_SIDE
    chunks = CBLOCK // LANES
    stride = LANES / COL_SIDE / COL_SIDE

    def stage(i, k):
        code = list_ref[i]
        q, w = parts_of(code, cell_blocks)
        slot, within = parts_of(q, station_blocks)
        depths_ref[k] = cells_ref[pl.ds(0, 1), pl.ds(pl.multiple_of(w * CBLOCK, CBLOCK), CBLOCK)]
        lines = line + (w & 1).astype(F32) * (rows / COL_SIDE)
        places = pltpu.roll(stations_ref[slot], (LANES - within * per_block) & (LANES - 1), 1)
        for part in range(per_block):
            at = pl.ds(part * LANES, LANES)
            across = jnp.broadcast_to(places[:, part : part + 1], (LANES, LANES)) - column
            gaps_ref[k, at, :] = across * across
            along = jnp.broadcast_to(places[:, lane_rows + part : lane_rows + part + 1], (LANES, LANES))
            lines_ref[k, at, :] = along - lines

    def issue(sums, i, k):
        q, _ = parts_of(list_ref[i], cell_blocks)
        depth = depths_ref[k]
        for part in range(per_block):
            pieces = ([], [])
            for at in range(part * LANES, (part + 1) * LANES, 16):
                across = gaps_ref[k, pl.ds(at, 16), :]
                along = lines_ref[k, pl.ds(at, 16), :]
                level = across + along * along
                slope = stride * stride - 2 * stride * along
                for unit in range(2):
                    near = []
                    for chunk in range(unit * chunks // 2, (unit + 1) * chunks // 2):
                        squared = level + depth[:, chunk * LANES : (chunk + 1) * LANES]
                        near.append(split(inverse_cube(squared)))
                        if chunk < chunks - 1:
                            level = level + slope
                            slope = slope + 2 * stride * stride
                    pieces[unit].append([jnp.concatenate(terms, axis=1) for terms in zip(*near)])
            left = terms_ref[q, :, pl.ds(part * HALF, HALF)]
            for unit in range(2):
                multiply_add(sums[2 * k + unit], left, pieces[unit], unit, part)

    def collect(sums, i, k):
        w = list_ref[i] & (cell_blocks - 1)
        for unit in range(2):
            both = pltpu.matmul_pop(sums[2 * k + unit])
            total_ref[w, :, pl.ds(unit * TILE, TILE)] += both[: 2 * epochs] + both[2 * epochs :]

    def run(*sums):
        pipelined(count, stage, functools.partial(issue, sums), functools.partial(collect, sums))

    pl.run_scoped(run, *accumulators(4 * epochs))


def slot_refs(slots, refs):
    messages, (residuals, images), rest = refs[:slots], refs[slots : slots + 2], refs[slots + 2 :]
    residuals, images = [residuals.at[0], residuals.at[1]], [images.at[0], images.at[1]]
    if slots == 3:
        third, *rest = rest
        residuals.append(third.at[0])
        images.append(third.at[1])
    return messages, residuals, images, rest


def near_kernel(sizes, *refs):
    cell_blocks, station_blocks, pairs, epochs, places = sizes
    slots = len(places)
    messages, residuals, images, rest = slot_refs(slots, refs)
    cells_ref, direction_ref, old_ref, total_ref, sums_ref, *scratch = rest
    adjoint_sums(sizes, messages, residuals, images, cells_ref, total_ref, scratch, True)

    def add(w, sums):
        at = pl.ds(pl.multiple_of(w * CBLOCK, CBLOCK), CBLOCK)
        direction, old = direction_ref[:, at], old_ref[:, at]
        return sums[0] + old * old, sums[1] + direction * direction

    zero = jnp.zeros((epochs, CBLOCK), F32)
    for i, total in enumerate(lax.fori_loop(0, cell_blocks, add, (zero, zero), unroll=4)):
        sums_ref[pl.ds(i, 1), :] = jnp.broadcast_to(jnp.sum(total).reshape(1, 1), (1, LANES))


def far_kernel(sizes, *refs):
    cell_blocks, station_blocks, pairs, epochs, places = sizes
    slots = len(places)
    messages, residuals, images, rest = slot_refs(slots, refs)
    cells_ref, _, sums_ref, model_ref, direction_ref, image_ref = rest[:6]
    constant_ref, slope_ref, stats_ref, total_ref, *scratch = rest[6:]
    adjoint_sums(sizes, messages, residuals, images, cells_ref, total_ref, scratch, False)
    zero = jnp.zeros((epochs, CBLOCK), F32)

    def combine(w, sums):
        at = pl.ds(pl.multiple_of(w * CBLOCK, CBLOCK), CBLOCK)
        total = total_ref[w] * cells_ref[pl.ds(1, 1), at]
        constant = total[:epochs] - DAMPING * model_ref[:, at]
        slope = total[epochs:] + DAMPING * direction_ref[:, at]
        constant_ref[:, at] = constant
        slope_ref[:, at] = slope
        return sums[0] + constant * slope, sums[1] + slope * slope

    cross, square = lax.fori_loop(0, cell_blocks, combine, (zero, zero), unroll=2)
    square = jnp.sum(square).reshape(1, 1)
    cross = jnp.sum(cross).reshape(1, 1)
    local_step = jnp.where(square > 0, cross / jnp.where(square > 0, square, 1.0), 0.0)

    def remainder(w, sums):
        at = pl.ds(pl.multiple_of(w * CBLOCK, CBLOCK), CBLOCK)
        slope = slope_ref[:, at]
        left = constant_ref[:, at] - local_step * slope
        return sums[0] + left * left, sums[1] + left * slope

    left_square, left_cross = lax.fori_loop(0, cell_blocks, remainder, (zero, zero), unroll=2)
    image = image_ref[0]
    stats = [
        sums_ref[pl.ds(0, 1), pl.ds(0, 1)],
        sums_ref[pl.ds(1, 1), pl.ds(0, 1)],
        jnp.sum(image * image).reshape(1, 1),
        local_step,
        jnp.sum(left_square).reshape(1, 1),
        jnp.sum(left_cross).reshape(1, 1),
        jnp.sqrt(square),
    ]
    lane = lax.broadcasted_iota(jnp.int32, (1, LANES), 1)
    row = jnp.zeros((1, LANES), F32)
    for i, value in enumerate(stats):
        row = jnp.where(lane == i, value, row)
    for i in range(stats_ref.shape[0]):
        stats_ref[i] = row


def adjoint(sizes, messages, terms, cell_rows, *others, ranks=None):
    cell_blocks, station_blocks, pairs, epochs, places = sizes
    slots = len(places)
    total = (cell_blocks, 2 * epochs, CBLOCK)
    scratch = list_scratch(sizes) + [
        pltpu.VMEM((slots + 1, LANES, LANES), F32),
        pltpu.VMEM((slots * station_blocks + 1, 4 * epochs, SBLOCK), BF16),
        pltpu.VMEM((2, 1, CBLOCK), F32),
        pltpu.VMEM((2, SBLOCK, LANES), F32),
        pltpu.VMEM((2, SBLOCK, LANES), F32),
    ]
    if ranks is None:
        kernel, shapes, aliases = near_kernel, [total, (2, LANES)], {}
    else:
        kernel, cells = far_kernel, (epochs, cell_blocks * CBLOCK)
        shapes = [cells, cells, (ranks, 1, LANES), total]
        aliases = {slots + len(terms) + 1: 3}
    return pl.pallas_call(
        functools.partial(kernel, sizes),
        out_shape=tuple(jax.ShapeDtypeStruct(shape, F32) for shape in shapes),
        in_specs=[VMEM] * (slots + len(terms) + 1 + len(others)),
        out_specs=(VMEM,) * len(shapes),
        scratch_shapes=scratch,
        input_output_aliases=aliases,
        compiler_params=params(),
        cost_estimate=estimate(sizes),
        name="near" if ranks is None else "far",
    )(*messages, *terms, cell_rows, *others)


def finish_kernel(
    stats_ref, constant_ref, slope_ref, model_ref, direction_ref, residual_ref, image_ref,
    model_out, residual_out, direction_out, new_model, new_residual, new_direction, sent,
):
    stats = stats_ref[...][:, 0, :]
    gamma_old, direction_square, image_square = (
        jnp.sum(stats[:, i : i + 1], axis=0, keepdims=True) for i in range(3)
    )
    step = gamma_old / (image_square + DAMPING * direction_square + GUARD)
    ahead = step - stats[:, 3:4]
    reach = ahead * stats[:, 6:7]
    gamma_new = jnp.sum(stats[:, 4:5] - 2.0 * ahead * stats[:, 5:6] + reach * reach, axis=0, keepdims=True)
    ratio = gamma_new / (gamma_old + GUARD)
    copies = []

    def send(i, source, target, at):
        copies.append(pltpu.make_async_copy(source.at[:, at], target.at[:, at], sent.at[i]))
        copies[-1].start()

    for q in range(image_ref.shape[1]):
        at = pl.ds(q * SBLOCK, SBLOCK)
        new_residual[:, at] = residual_ref[q] - step * image_ref[0, q]
    send(0, new_residual, residual_out, pl.ds(0, new_residual.shape[1]))
    cells = model_ref.shape[1] // FINISH_PARTS
    for part in range(FINISH_PARTS):

        def block(w, unused):
            at = pl.ds(pl.multiple_of(part * cells + w * CBLOCK, CBLOCK), CBLOCK)
            direction = direction_ref[:, at]
            new_model[:, at] = model_ref[:, at] + step * direction
            new_direction[:, at] = (constant_ref[:, at] - step * slope_ref[:, at]) + ratio * direction
            return 0

        lax.fori_loop(0, cells // CBLOCK, block, 0, unroll=2)
        send(1 + 2 * part, new_model, model_out, pl.ds(part * cells, cells))
        send(2 + 2 * part, new_direction, direction_out, pl.ds(part * cells, cells))
    for copy in copies:
        copy.wait()


FINISH_PARTS = 4


def finish(stats, constant, slope, model_field, direction, residual, image):
    blocks, epochs, _ = residual.shape
    outs = (model_field.shape, (epochs, blocks * SBLOCK), direction.shape)
    return pl.pallas_call(
        finish_kernel,
        out_shape=tuple(jax.ShapeDtypeStruct(shape, F32) for shape in outs),
        in_specs=[VMEM] * 7,
        out_specs=(pl.BlockSpec(memory_space=pl.ANY),) * 3,
        scratch_shapes=[pltpu.VMEM(shape, F32) for shape in outs]
        + [pltpu.SemaphoreType.DMA((1 + 2 * FINISH_PARTS,))],
        compiler_params=params(),
        name="finish",
    )(stats, constant, slope, model_field, direction, residual, image)


def after(arrays, others):
    return lax.optimization_barrier((arrays, others))[0]


def shards(model_field, direction, old_grad, residual, block_pairs, depth_band, station_offsets):
    ranks = lax.axis_size("tile")
    epochs, cells = model_field.shape
    station_blocks, pairs = block_pairs.shape
    cell_blocks = cells // CBLOCK

    def to_partner(array):
        return lax.ppermute(array, "tile", [(i, i ^ 1) for i in range(ranks)])

    def across(message):
        ends = [(i, i + 1) for i in range(1, ranks - 1, 2)]
        return lax.ppermute(message, "tile", ends + [(j, i) for i, j in ends])

    sizes = (cell_blocks, station_blocks, pairs, epochs)
    near_slots, far_slots = (*sizes, (0, -1)), (*sizes, (1, 2, -2))

    own, residual = pack(station_offsets, block_pairs, residual)
    partner = to_partner(own)
    near = [own, partner]
    partner_residual = to_partner(residual)
    values, cell_rows, turned = prepare(2.0 / math.sqrt(cells), after(depth_band, own), direction)
    arrived = across(pair_up(own, after(partner, values)))
    residuals = pair_up(residual, partner_residual)
    arrived = after(arrived, residuals)
    far = [arrived[0], arrived[1], to_partner(arrived[0])]

    far_residuals = across(residuals)
    parts = forward(far_slots, far, values, turned)
    parts, far_residuals = after((parts, far_residuals), (far_residuals, parts))
    returned = to_partner(parts[2])
    given = across(far_parts(parts, returned))
    mine = forward(near_slots, after(near, returned), values, turned)
    given = after(given, mine)
    mine = small_call(add_kernel, mine.shape, "add", mine, given)
    images = both_images(mine, to_partner(mine))

    far_images = across(images)
    near_total, sums = adjoint(near_slots, near, [residuals, images], cell_rows, direction, old_grad)
    far_images = after(far_images, near_total)
    thirds = to_partner(pair_up(far_residuals[0], far_images[0]))
    constant, slope, stats, _ = adjoint(
        far_slots, far, [far_residuals, far_images, thirds], cell_rows,
        near_total, sums, model_field, direction, images, ranks=ranks,
    )
    stats = lax.all_to_all(stats, "tile", 0, 0)
    return finish(stats, constant, slope, model_field, direction, residual, images)


def solution(mesh):
    wide = P(None, ("groups", "tile"))
    mapped = jax.shard_map(
        shards,
        mesh=mesh,
        in_specs=(wide, wide, wide, wide, P(("groups", "tile"), None), P(("groups", "tile")), wide),
        out_specs=(wide, wide, wide),
        check_vma=False,
    )

    def step(*arrays):
        with jax.sharding.use_abstract_mesh(mesh.abstract_mesh):
            return mapped(*arrays)

    return step
```

```python
import functools
import math

import jax
import jax.numpy as jnp
from jax import lax
from jax.experimental import pallas as pl
from jax.experimental.pallas import tpu as pltpu
from jax.sharding import PartitionSpec as P

CBLOCK = 512
SBLOCK = 256
REACH = 2
BANDS = 16
COL_SIDE = 32
DEPTH_RANGE = 2.0
DEPTH_SHIFT = 0.25
DAMPING = 1.0
GUARD = 1e-06

F32 = jnp.float32
BF16 = jnp.bfloat16
LANES = 128
TILE = 256
HALF = TILE // 2
GROUP = HALF // 2

SMEM = pl.BlockSpec(memory_space=pltpu.SMEM)
VMEM = pl.BlockSpec(memory_space=pltpu.VMEM)


def params(mebibytes=16):
    return pltpu.CompilerParams(vmem_limit_bytes=mebibytes * 2**20)


def parts_of(number, size):
    assert size & (size - 1) == 0
    return number >> (size.bit_length() - 1), number & (size - 1)


def split(values):
    high = values.astype(BF16)
    return high, (values - high.astype(F32)).astype(BF16)


def dot(left, right):
    return jnp.dot(left, right, preferred_element_type=F32)


def pack_kernel(offsets_any, pairs_any, residual_any, message_ref, residual_ref, offsets_ref, pairs_ref, rows_ref, sent):
    copies = [
        pltpu.make_async_copy(offsets_any, offsets_ref, sent.at[0]),
        pltpu.make_async_copy(pairs_any, pairs_ref, sent.at[1]),
        pltpu.make_async_copy(residual_any, rows_ref, sent.at[2]),
    ]
    for copy in copies:
        copy.start()
    lines = offsets_ref.shape[1] // LANES
    rows, pairs = pairs_ref.shape
    message_ref[pl.ds(2 * lines, rows), :] = jnp.zeros((rows, LANES), F32)
    for copy in copies:
        copy.wait()
    for i in range(lines):
        at = pl.ds(i * LANES, LANES)
        message_ref[pl.ds(i, 1), :] = offsets_ref[pl.ds(0, 1), at]
        message_ref[pl.ds(lines + i, 1), :] = offsets_ref[pl.ds(1, 1), at]
    message_ref[pl.ds(2 * lines, rows), pl.ds(0, pairs)] = pairs_ref[...].astype(F32) + 1.0
    for q in range(rows):
        residual_ref[q] = rows_ref[:, pl.ds(q * SBLOCK, SBLOCK)]


def in_hbm(array):
    return pltpu.with_memory_space_constraint(array, pltpu.HBM)


def pack(station_offsets, block_pairs, residual):
    rows = 2 * station_offsets.shape[1] // LANES + block_pairs.shape[0]
    return pl.pallas_call(
        pack_kernel,
        out_shape=(jax.ShapeDtypeStruct((rows, LANES), F32), jax.ShapeDtypeStruct((block_pairs.shape[0], residual.shape[0], SBLOCK), F32)),
        in_specs=[pl.BlockSpec(memory_space=pl.ANY)] * 3,
        out_specs=(VMEM, VMEM),
        scratch_shapes=[
            pltpu.VMEM(station_offsets.shape, F32),
            pltpu.VMEM(block_pairs.shape, jnp.int32),
            pltpu.VMEM(residual.shape, F32),
            pltpu.SemaphoreType.DMA((3,)),
        ],
        compiler_params=params(2),
        name="pack",
    )(in_hbm(station_offsets), in_hbm(block_pairs), in_hbm(residual))


def far_parts_kernel(parts_ref, third_ref, message_ref):
    message_ref[0] = parts_ref[0] + third_ref[...]
    message_ref[1] = parts_ref[1]


def far_parts(parts, third):
    return small_call(far_parts_kernel, (2, *third.shape), "far_parts", parts, third)


def both_images_kernel(mine_ref, theirs_ref, images_ref):
    images_ref[0] = mine_ref[0] + theirs_ref[1]
    images_ref[1] = mine_ref[1] + theirs_ref[0]


def both_images(mine, theirs):
    return small_call(both_images_kernel, mine.shape, "both_images", mine, theirs)


def add_kernel(left_ref, right_ref, sum_ref):
    sum_ref[...] = left_ref[...] + right_ref[...]


def pair_kernel(first_ref, second_ref, message_ref):
    message_ref[0] = first_ref[...]
    message_ref[1] = second_ref[...]


def pair_up(first, second):
    return small_call(pair_kernel, (2, *first.shape), "pair", first, second)


def small_call(kernel, shape, name, *arrays):
    return pl.pallas_call(
        kernel,
        out_shape=jax.ShapeDtypeStruct(shape, F32),
        in_specs=[VMEM] * len(arrays),
        out_specs=VMEM,
        compiler_params=params(2),
        name=name,
    )(*arrays)


def prepare_kernel(scale, band_ref, band_row_ref, direction_ref, values_ref, cells_ref, turned_ref):
    blocks = values_ref.shape[0]
    epochs = direction_ref.shape[0]

    @pl.when(pl.program_id(0) == 0)
    def first():
        depth = (band_ref[...].astype(F32) + 0.5) * (DEPTH_RANGE / BANDS)
        turned_ref[...] = (depth * depth).T

    def block(w, unused):
        at = pl.ds(pl.multiple_of(w * CBLOCK, CBLOCK), CBLOCK)
        row = (band_row_ref[:, at].astype(F32) + 0.5) * (DEPTH_RANGE / BANDS)
        shifted = row + DEPTH_SHIFT
        factor = row * scale * (shifted * jnp.sqrt(shifted))
        cells_ref[pl.ds(0, 1), at] = row * row
        cells_ref[pl.ds(1, 1), at] = factor
        high, low = split(direction_ref[:, at] * factor)
        values_ref[w, pl.ds(0, epochs), :] = high
        values_ref[w, pl.ds(epochs, epochs), :] = low
        return 0

    lax.fori_loop(0, blocks, block, 0, unroll=4)


PARTS = 2


def prepare(scale, depth_band, direction):
    epochs, cells = direction.shape
    blocks = cells // CBLOCK
    return pl.pallas_call(
        functools.partial(prepare_kernel, scale),
        grid=(PARTS,),
        out_shape=(
            jax.ShapeDtypeStruct((blocks, 2 * epochs, CBLOCK), BF16),
            jax.ShapeDtypeStruct((2, cells), F32),
            jax.ShapeDtypeStruct((cells // LANES, LANES), F32),
        ),
        in_specs=[
            pl.BlockSpec((cells // LANES, LANES), lambda i: (0, 0)),
            pl.BlockSpec((1, cells // PARTS), lambda i: (0, i)),
            pl.BlockSpec((epochs, cells // PARTS), lambda i: (0, i)),
        ],
        out_specs=(
            pl.BlockSpec((blocks // PARTS, 2 * epochs, CBLOCK), lambda i: (i, 0, 0)),
            pl.BlockSpec((2, cells // PARTS), lambda i: (0, i)),
            VMEM,
        ),
        compiler_params=params(8),
        cost_estimate=pl.CostEstimate(flops=8 * epochs * cells, bytes_accessed=12 * epochs * cells, transcendentals=0),
        name="prepare",
    )(
        in_hbm(depth_band.reshape(cells // LANES, LANES)),
        in_hbm(depth_band.reshape(1, cells)),
        in_hbm(direction),
    )


def tile_offset(place):
    return place * (2 * (lax.axis_index("tile") & 1) - 1)


def send_codes(sizes, messages, codes_ref, scalars_ref, sent):
    cell_blocks, station_blocks, pairs, epochs, places = sizes
    q = lax.broadcasted_iota(jnp.int32, (station_blocks, LANES), 0)
    for slot, message_ref in enumerate(messages):
        codes = message_ref[pl.ds(message_ref.shape[0] - station_blocks, station_blocks), :]
        within = codes.astype(jnp.int32) - (cell_blocks * (REACH - tile_offset(places[slot])) + 1)
        hit = jnp.logical_and(within >= 0, within < cell_blocks)
        code = (slot * station_blocks + q) * cell_blocks + within
        codes_ref[pl.ds(slot * station_blocks, station_blocks), :] = jnp.where(hit, code, -1)
    copy = pltpu.make_async_copy(codes_ref, scalars_ref, sent)
    copy.start()
    return copy


def list_pairs(sizes, copy, scalars_ref, list_ref):
    cell_blocks, station_blocks, pairs, epochs, places = sizes
    slots = len(places)
    copy.wait()
    count = jnp.int32(0)
    for row in range(slots * station_blocks):
        for i in range(pairs):
            code = scalars_ref[row, i]
            list_ref[count] = code
            count = count + (code >= 0).astype(jnp.int32)
    for i in range(2 * UNROLL):
        list_ref[count + i] = slots * station_blocks * cell_blocks
    return count


def list_scratch(sizes):
    cell_blocks, station_blocks, pairs, epochs, places = sizes
    slots = len(places)
    return [
        pltpu.SMEM((slots * station_blocks * pairs + 2 * UNROLL,), jnp.int32),
        pltpu.VMEM((slots * station_blocks, LANES), jnp.int32),
        pltpu.SMEM((slots * station_blocks, LANES), jnp.int32),
        pltpu.SemaphoreType.DMA(()),
    ]


UNROLL = 4


def pipelined(count, stage, issue, collect):
    stage(0, 0)
    stage(1, 1)
    issue(0, 0)

    def rounds(first, number, size):
        def step(j, unused):
            for k in range(size):
                i = first + size * j + k
                issue(i + 1, (k + 1) % 2)
                stage(i + 2, k % 2)
                collect(i, k % 2)
            return 0

        lax.fori_loop(0, number, step, 0)
        return first + size * number

    whole = count // UNROLL
    done = rounds(0, whole, UNROLL)
    done = rounds(done, (count > 1 + done).astype(jnp.int32), UNROLL // 2)
    collect(done, 0)


def doubled(array, group):
    groups = [array[:, i : i + group] for i in range(0, array.shape[1], group)]
    return jnp.concatenate([group for group in groups for _ in range(2)], axis=1)


def multiply_add(sums_ref, left, pieces, group, unit, register):
    rows = pieces[0][0].shape[0]
    tile = []
    for i in range(0, len(pieces), group // rows):
        high, low = zip(*pieces[i : i + group // rows])
        tile += high + low
    pltpu.matmul_push_rhs(jnp.concatenate(tile, axis=0), register, unit)
    pltpu.matmul_acc_lhs(sums_ref, left, load_staged_rhs=register)


def accumulators(rows):
    return [pltpu.ACC(unit)((rows, TILE), F32) for unit in (0, 1)] * 2


def inverse_cube(squared):
    return lax.rsqrt(squared * squared * squared)


def forward_kernel(sizes, *refs):
    cell_blocks, station_blocks, pairs, epochs, places = sizes
    slots = len(places)
    messages = refs[:slots]
    values_ref, turned_ref = refs[slots : slots + 2]
    images_ref, list_ref, codes_ref, scalars_ref, sent, *scratch = refs[slots + 2 :]
    across_ref, along_ref, image_ref, gaps_ref, lines_ref, depths_ref = scratch
    copy = send_codes(sizes, messages, codes_ref, scalars_ref, sent)
    dummy = slots * station_blocks
    per_block = SBLOCK // LANES
    lines = station_blocks * per_block
    across_ref[pl.ds(dummy, 1), :] = jnp.zeros((1, SBLOCK), F32)
    along_ref[pl.ds(dummy, 1), :] = jnp.zeros((1, SBLOCK), F32)
    image_ref[...] = jnp.zeros_like(image_ref)
    for slot in range(slots):
        for i in range(lines):
            place = (pl.ds(slot * station_blocks + i // per_block, 1), pl.ds(i % per_block * LANES, LANES))
            across_ref[place] = messages[slot][pl.ds(i, 1), :] + tile_offset(places[slot]).astype(F32)
            along_ref[place] = messages[slot][pl.ds(lines + i, 1), :]
    count = list_pairs(sizes, copy, scalars_ref, list_ref)
    column = lax.broadcasted_iota(jnp.int32, (COL_SIDE, SBLOCK), 0).astype(F32)
    column = (column + 0.5) / COL_SIDE
    rows = CBLOCK // COL_SIDE
    line = (lax.broadcasted_iota(jnp.int32, (rows, SBLOCK), 0).astype(F32) + 0.5) / COL_SIDE

    def stage(i, k):
        code = list_ref[i]
        q, w = parts_of(code, cell_blocks)
        across = across_ref[pl.ds(q, 1), :] - column
        gaps_ref[k] = across * across
        along = along_ref[pl.ds(q, 1), :] - (w & 1).astype(F32) * (rows / COL_SIDE) - line
        lines_ref[k] = along * along
        turned = pltpu.roll(turned_ref[...], (LANES - w * (CBLOCK // LANES)) & (LANES - 1), 1)
        for part in range(CBLOCK // LANES):
            depths_ref[k, pl.ds(part * LANES, LANES), :] = jnp.broadcast_to(turned[:, part : part + 1], (LANES, LANES))

    def issue(sums, i, k):
        w = list_ref[i] & (cell_blocks - 1)
        across = gaps_ref[k]
        for tile in range(CBLOCK // HALF):
            pieces = []
            for at in range(0, HALF, COL_SIDE):
                y = (tile * HALF + at) // COL_SIDE
                depth = depths_ref[k, pl.ds(y * COL_SIDE, COL_SIDE), :]
                depth = jnp.concatenate([depth] * (SBLOCK // LANES), axis=1)
                along = lines_ref[k, pl.ds(y, 1), :]
                pieces.append(split(inverse_cube((across + along) + depth)))
            left = doubled(values_ref[w, :, pl.ds(tile * HALF, HALF)], HALF)
            multiply_add(sums[2 * k + tile % 2], left, pieces, HALF, tile % 2, tile // 2)

    def collect(sums, i, k):
        q, _ = parts_of(list_ref[i], cell_blocks)
        both = pltpu.matmul_pop(sums[2 * k]) + pltpu.matmul_pop(sums[2 * k + 1])
        image_ref[q] += both[:epochs] + both[epochs:]

    def run(*sums):
        pipelined(count, stage, functools.partial(issue, sums), functools.partial(collect, sums))

    pl.run_scoped(run, *accumulators(2 * epochs))
    for slot in range(slots):
        images_ref[slot] = image_ref[pl.ds(slot * station_blocks, station_blocks)]


def forward(sizes, messages, values, turned):
    cell_blocks, station_blocks, pairs, epochs, places = sizes
    slots = len(places)
    rows = (slots * station_blocks + 8) // 8 * 8
    return pl.pallas_call(
        functools.partial(forward_kernel, sizes),
        out_shape=jax.ShapeDtypeStruct((slots, station_blocks, epochs, SBLOCK), F32),
        in_specs=[VMEM] * (slots + 2),
        out_specs=VMEM,
        scratch_shapes=list_scratch(sizes)
        + [
            pltpu.VMEM((rows, SBLOCK), F32),
            pltpu.VMEM((rows, SBLOCK), F32),
            pltpu.VMEM((slots * station_blocks + 1, epochs, SBLOCK), F32),
            pltpu.VMEM((2, COL_SIDE, SBLOCK), F32),
            pltpu.VMEM((2, CBLOCK // COL_SIDE, SBLOCK), F32),
            pltpu.VMEM((2, CBLOCK, LANES), F32),
        ],
        compiler_params=params(),
        cost_estimate=estimate(sizes, 0.1 if slots > 2 else 1),
        name="forward",
    )(*messages, values, turned)


def estimate(sizes, part=1):
    cell_blocks, station_blocks, pairs, epochs, places = sizes
    slots = len(places)
    entries = station_blocks * pairs * slots // (2 * REACH + 1) * SBLOCK * CBLOCK
    return pl.CostEstimate(flops=int(2 * 1200 * entries * part), bytes_accessed=2**20, transcendentals=entries)


def adjoint_sums(sizes, messages, residuals, images, cells_ref, total_ref, scratch, clear):
    cell_blocks, station_blocks, pairs, epochs, places = sizes
    slots = len(places)
    list_ref, codes_ref, scalars_ref, sent, stations_ref, terms_ref, depths_ref, gaps_ref, lines_ref = scratch
    copy = send_codes(sizes, messages, codes_ref, scalars_ref, sent)
    dummy = slots * station_blocks
    stations_ref[slots] = jnp.zeros(stations_ref.shape[1:], F32)
    per_block = SBLOCK // LANES
    lane_rows = station_blocks * per_block
    for slot in range(slots):
        shift = tile_offset(places[slot]).astype(F32)
        rows = [messages[slot][pl.ds(0, lane_rows), :] + shift, messages[slot][pl.ds(lane_rows, lane_rows), :]]
        rows.append(jnp.zeros((LANES - 2 * lane_rows, LANES), F32))
        stations_ref[slot] = jnp.concatenate(rows, axis=0).T
    if clear:
        total_ref[...] = jnp.zeros_like(total_ref)
    count = list_pairs(sizes, copy, scalars_ref, list_ref)
    terms_ref[dummy] = jnp.zeros(terms_ref.shape[1:], BF16)
    for slot in range(slots):
        for q in range(station_blocks):
            stacked = doubled(jnp.concatenate([residuals[slot][q], images[slot][q]], axis=0), GROUP)
            high, low = split(stacked)
            terms_ref[slot * station_blocks + q, pl.ds(0, 2 * epochs), :] = high
            terms_ref[slot * station_blocks + q, pl.ds(2 * epochs, 2 * epochs), :] = low
    lane = lax.broadcasted_iota(jnp.int32, (1, LANES), 1)
    column = ((lane % COL_SIDE).astype(F32) + 0.5) / COL_SIDE
    line = ((lane // COL_SIDE).astype(F32) + 0.5) / COL_SIDE
    rows = CBLOCK // COL_SIDE
    chunks = CBLOCK // LANES
    stride = LANES / COL_SIDE / COL_SIDE

    def stage(i, k):
        code = list_ref[i]
        q, w = parts_of(code, cell_blocks)
        slot, within = parts_of(q, station_blocks)
        depths_ref[k] = cells_ref[pl.ds(0, 1), pl.ds(pl.multiple_of(w * CBLOCK, CBLOCK), CBLOCK)]
        lines = line + (w & 1).astype(F32) * (rows / COL_SIDE)
        places = pltpu.roll(stations_ref[slot], (LANES - within * per_block) & (LANES - 1), 1)
        for part in range(per_block):
            at = pl.ds(part * LANES, LANES)
            across = jnp.broadcast_to(places[:, part : part + 1], (LANES, LANES)) - column
            gaps_ref[k, at, :] = across * across
            along = jnp.broadcast_to(places[:, lane_rows + part : lane_rows + part + 1], (LANES, LANES))
            lines_ref[k, at, :] = along - lines

    def issue(sums, i, k):
        q, _ = parts_of(list_ref[i], cell_blocks)
        depth = depths_ref[k]
        for part in range(per_block):
            pieces = ([], [])
            for at in range(part * LANES, (part + 1) * LANES, 16):
                across = gaps_ref[k, pl.ds(at, 16), :]
                along = lines_ref[k, pl.ds(at, 16), :]
                level = across + along * along
                slope = stride * stride - 2 * stride * along
                for unit in range(2):
                    near = []
                    for chunk in range(unit * chunks // 2, (unit + 1) * chunks // 2):
                        squared = level + depth[:, chunk * LANES : (chunk + 1) * LANES]
                        near.append(split(inverse_cube(squared)))
                        if chunk < chunks - 1:
                            level = level + slope
                            slope = slope + 2 * stride * stride
                    pieces[unit].append([jnp.concatenate(terms, axis=1) for terms in zip(*near)])
            left = terms_ref[q, :, pl.ds(part * TILE, TILE)]
            for unit in range(2):
                multiply_add(sums[2 * k + unit], left, pieces[unit], GROUP, unit, part)

    def collect(sums, i, k):
        w = list_ref[i] & (cell_blocks - 1)
        for unit in range(2):
            both = pltpu.matmul_pop(sums[2 * k + unit])
            total_ref[w, :, pl.ds(unit * TILE, TILE)] += both[: 2 * epochs] + both[2 * epochs :]

    def run(*sums):
        pipelined(count, stage, functools.partial(issue, sums), functools.partial(collect, sums))

    pl.run_scoped(run, *accumulators(4 * epochs))


def slot_refs(slots, refs):
    messages, (residuals, images), rest = refs[:slots], refs[slots : slots + 2], refs[slots + 2 :]
    residuals, images = [residuals.at[0], residuals.at[1]], [images.at[0], images.at[1]]
    if slots == 3:
        third, *rest = rest
        residuals.append(third.at[0])
        images.append(third.at[1])
    return messages, residuals, images, rest


def near_kernel(sizes, *refs):
    cell_blocks, station_blocks, pairs, epochs, places = sizes
    slots = len(places)
    messages, residuals, images, rest = slot_refs(slots, refs)
    cells_ref, total_ref, *scratch = rest
    adjoint_sums(sizes, messages, residuals, images, cells_ref, total_ref, scratch, True)


def squares_kernel(old_ref, direction_ref, sums_ref):
    epochs, cells = direction_ref.shape

    def add(w, sums):
        at = pl.ds(pl.multiple_of(w * CBLOCK, CBLOCK), CBLOCK)
        old, direction = old_ref[:, at], direction_ref[:, at]
        return sums[0] + old * old, sums[1] + direction * direction

    zero = jnp.zeros((epochs, CBLOCK), F32)
    for i, total in enumerate(lax.fori_loop(0, cells // CBLOCK, add, (zero, zero), unroll=4)):
        sums_ref[pl.ds(i, 1), :] = jnp.broadcast_to(jnp.sum(total).reshape(1, 1), (1, LANES))


def far_kernel(sizes, *refs):
    cell_blocks, station_blocks, pairs, epochs, places = sizes
    slots = len(places)
    messages, residuals, images, rest = slot_refs(slots, refs)
    cells_ref, _, sums_ref, model_ref, direction_ref, image_ref = rest[:6]
    constant_ref, slope_ref, stats_ref, total_ref, *scratch = rest[6:]
    adjoint_sums(sizes, messages, residuals, images, cells_ref, total_ref, scratch, False)
    zero = jnp.zeros((epochs, CBLOCK), F32)

    def combine(w, sums):
        at = pl.ds(pl.multiple_of(w * CBLOCK, CBLOCK), CBLOCK)
        total = total_ref[w] * cells_ref[pl.ds(1, 1), at]
        constant = total[:epochs] - DAMPING * model_ref[:, at]
        slope = total[epochs:] + DAMPING * direction_ref[:, at]
        constant_ref[:, at] = constant
        slope_ref[:, at] = slope
        return sums[0] + constant * slope, sums[1] + slope * slope

    cross, square = lax.fori_loop(0, cell_blocks, combine, (zero, zero), unroll=2)
    square = jnp.sum(square).reshape(1, 1)
    cross = jnp.sum(cross).reshape(1, 1)
    local_step = jnp.where(square > 0, cross / jnp.where(square > 0, square, 1.0), 0.0)

    def remainder(w, sums):
        at = pl.ds(pl.multiple_of(w * CBLOCK, CBLOCK), CBLOCK)
        slope = slope_ref[:, at]
        left = constant_ref[:, at] - local_step * slope
        return sums[0] + left * left, sums[1] + left * slope

    left_square, left_cross = lax.fori_loop(0, cell_blocks, remainder, (zero, zero), unroll=2)
    image = image_ref[0]
    stats = [
        sums_ref[pl.ds(0, 1), pl.ds(0, 1)],
        sums_ref[pl.ds(1, 1), pl.ds(0, 1)],
        jnp.sum(image * image).reshape(1, 1),
        local_step,
        jnp.sum(left_square).reshape(1, 1),
        jnp.sum(left_cross).reshape(1, 1),
        jnp.sqrt(square),
    ]
    lane = lax.broadcasted_iota(jnp.int32, (1, LANES), 1)
    row = jnp.zeros((1, LANES), F32)
    for i, value in enumerate(stats):
        row = jnp.where(lane == i, value, row)
    for i in range(stats_ref.shape[0]):
        stats_ref[i] = row


def adjoint(sizes, messages, terms, cell_rows, *others, ranks=None):
    cell_blocks, station_blocks, pairs, epochs, places = sizes
    slots = len(places)
    total = (cell_blocks, 2 * epochs, CBLOCK)
    scratch = list_scratch(sizes) + [
        pltpu.VMEM((slots + 1, LANES, LANES), F32),
        pltpu.VMEM((slots * station_blocks + 1, 4 * epochs, 2 * SBLOCK), BF16),
        pltpu.VMEM((2, 1, CBLOCK), F32),
        pltpu.VMEM((2, SBLOCK, LANES), F32),
        pltpu.VMEM((2, SBLOCK, LANES), F32),
    ]
    if ranks is None:
        kernel, shapes, aliases = near_kernel, [total], {}
    else:
        kernel, cells = far_kernel, (epochs, cell_blocks * CBLOCK)
        shapes = [cells, cells, (ranks, 1, LANES), total]
        aliases = {slots + len(terms) + 1: 3}
    return pl.pallas_call(
        functools.partial(kernel, sizes),
        out_shape=tuple(jax.ShapeDtypeStruct(shape, F32) for shape in shapes),
        in_specs=[VMEM] * (slots + len(terms) + 1 + len(others)),
        out_specs=(VMEM,) * len(shapes),
        scratch_shapes=scratch,
        input_output_aliases=aliases,
        compiler_params=params(),
        cost_estimate=estimate(sizes),
        name="near" if ranks is None else "far",
    )(*messages, *terms, cell_rows, *others)


def finish_kernel(
    stats_ref, constant_ref, slope_ref, model_ref, direction_ref, residual_ref, image_ref,
    model_out, residual_out, direction_out, new_model, new_residual, new_direction, sent,
):
    stats = stats_ref[...][:, 0, :]
    gamma_old, direction_square, image_square = (
        jnp.sum(stats[:, i : i + 1], axis=0, keepdims=True) for i in range(3)
    )
    step = gamma_old / (image_square + DAMPING * direction_square + GUARD)
    ahead = step - stats[:, 3:4]
    reach = ahead * stats[:, 6:7]
    gamma_new = jnp.sum(stats[:, 4:5] - 2.0 * ahead * stats[:, 5:6] + reach * reach, axis=0, keepdims=True)
    ratio = gamma_new / (gamma_old + GUARD)
    copies = []

    def send(i, source, target, at):
        copies.append(pltpu.make_async_copy(source.at[:, at], target.at[:, at], sent.at[i]))
        copies[-1].start()

    for q in range(image_ref.shape[1]):
        at = pl.ds(q * SBLOCK, SBLOCK)
        new_residual[:, at] = residual_ref[q] - step * image_ref[0, q]
    send(0, new_residual, residual_out, pl.ds(0, new_residual.shape[1]))
    cells = model_ref.shape[1] // FINISH_PARTS
    for part in range(FINISH_PARTS):

        def block(w, unused):
            at = pl.ds(pl.multiple_of(part * cells + w * CBLOCK, CBLOCK), CBLOCK)
            direction = direction_ref[:, at]
            new_model[:, at] = model_ref[:, at] + step * direction
            new_direction[:, at] = (constant_ref[:, at] - step * slope_ref[:, at]) + ratio * direction
            return 0

        lax.fori_loop(0, cells // CBLOCK, block, 0, unroll=2)
        send(1 + 2 * part, new_model, model_out, pl.ds(part * cells, cells))
        send(2 + 2 * part, new_direction, direction_out, pl.ds(part * cells, cells))
    for copy in copies:
        copy.wait()


FINISH_PARTS = 4


def finish(stats, constant, slope, model_field, direction, residual, image):
    blocks, epochs, _ = residual.shape
    outs = (model_field.shape, (epochs, blocks * SBLOCK), direction.shape)
    return pl.pallas_call(
        finish_kernel,
        out_shape=tuple(jax.ShapeDtypeStruct(shape, F32) for shape in outs),
        in_specs=[VMEM] * 7,
        out_specs=(pl.BlockSpec(memory_space=pl.ANY),) * 3,
        scratch_shapes=[pltpu.VMEM(shape, F32) for shape in outs]
        + [pltpu.SemaphoreType.DMA((1 + 2 * FINISH_PARTS,))],
        compiler_params=params(),
        name="finish",
    )(stats, constant, slope, model_field, direction, residual, image)


def after(arrays, others):
    return lax.optimization_barrier((arrays, others))[0]


def shards(model_field, direction, old_grad, residual, block_pairs, depth_band, station_offsets):
    ranks = lax.axis_size("tile")
    epochs, cells = model_field.shape
    station_blocks, pairs = block_pairs.shape
    cell_blocks = cells // CBLOCK

    def to_partner(array):
        return lax.ppermute(array, "tile", [(i, i ^ 1) for i in range(ranks)])

    def across(message):
        ends = [(i, i + 1) for i in range(1, ranks - 1, 2)]
        return lax.ppermute(message, "tile", ends + [(j, i) for i, j in ends])

    sizes = (cell_blocks, station_blocks, pairs, epochs)
    near_slots, far_slots = (*sizes, (0, -1)), (*sizes, (1, 2, -2))

    own, residual = pack(station_offsets, block_pairs, residual)
    partner = to_partner(own)
    near = [own, partner]
    partner_residual = to_partner(residual)
    values, cell_rows, turned = prepare(2.0 / math.sqrt(cells), after(depth_band, own), direction)
    arrived = across(pair_up(own, after(partner, values)))
    residuals = pair_up(residual, partner_residual)
    arrived = after(arrived, residuals)
    far = [arrived[0], arrived[1], to_partner(arrived[0])]

    far_residuals = across(residuals)
    parts = forward(far_slots, far, values, turned)
    parts, far_residuals = after((parts, far_residuals), (far_residuals, parts))
    returned = to_partner(parts[2])
    given = across(far_parts(parts, returned))
    mine = forward(near_slots, after(near, returned), values, turned)
    sums = small_call(squares_kernel, (2, LANES), "squares", *after((old_grad, direction), mine))
    given = after(given, (mine, sums))
    mine = small_call(add_kernel, mine.shape, "add", mine, given)
    images = both_images(mine, to_partner(mine))

    far_images = across(images)
    (near_total,) = adjoint(near_slots, near, [residuals, images], cell_rows)
    far_images = after(far_images, near_total)
    thirds = to_partner(pair_up(far_residuals[0], far_images[0]))
    constant, slope, stats, _ = adjoint(
        far_slots, far, [far_residuals, far_images, thirds], cell_rows,
        near_total, sums, model_field, direction, images, ranks=ranks,
    )
    stats = lax.all_to_all(stats, "tile", 0, 0)
    return finish(stats, constant, slope, model_field, direction, residual, images)


def solution(mesh):
    wide = P(None, ("groups", "tile"))
    mapped = jax.shard_map(
        shards,
        mesh=mesh,
        in_specs=(wide, wide, wide, wide, P(("groups", "tile"), None), P(("groups", "tile")), wide),
        out_specs=(wide, wide, wide),
        check_vma=False,
    )

    def step(*arrays):
        with jax.sharding.use_abstract_mesh(mesh.abstract_mesh):
            return mapped(*arrays)

    return step
```

```python
import functools
import math

import jax
import jax.numpy as jnp
from jax import lax
from jax.experimental import pallas as pl
from jax.experimental.pallas import tpu as pltpu
from jax.sharding import PartitionSpec as P

CBLOCK = 512
SBLOCK = 256
REACH = 2
BANDS = 16
COL_SIDE = 32
DEPTH_RANGE = 2.0
DEPTH_SHIFT = 0.25
DAMPING = 1.0
GUARD = 1e-06

F32 = jnp.float32
BF16 = jnp.bfloat16
LANES = 128
TILE = 256
HALF = TILE // 2
GROUP = HALF // 2

SMEM = pl.BlockSpec(memory_space=pltpu.SMEM)
VMEM = pl.BlockSpec(memory_space=pltpu.VMEM)


def params(mebibytes=16):
    return pltpu.CompilerParams(vmem_limit_bytes=mebibytes * 2**20)


def parts_of(number, size):
    assert size & (size - 1) == 0
    return number >> (size.bit_length() - 1), number & (size - 1)


def split(values):
    high = values.astype(BF16)
    return high, (values - high.astype(F32)).astype(BF16)


def dot(left, right):
    return jnp.dot(left, right, preferred_element_type=F32)


def pack_kernel(offsets_any, pairs_any, residual_any, message_ref, residual_ref, offsets_ref, pairs_ref, rows_ref, sent):
    copies = [
        pltpu.make_async_copy(offsets_any, offsets_ref, sent.at[0]),
        pltpu.make_async_copy(pairs_any, pairs_ref, sent.at[1]),
        pltpu.make_async_copy(residual_any, rows_ref, sent.at[2]),
    ]
    for copy in copies:
        copy.start()
    lines = offsets_ref.shape[1] // LANES
    rows, pairs = pairs_ref.shape
    message_ref[pl.ds(2 * lines, 8), :] = jnp.zeros((8, LANES), F32)
    for copy in copies:
        copy.wait()
    for i in range(lines):
        at = pl.ds(i * LANES, LANES)
        message_ref[pl.ds(i, 1), :] = offsets_ref[pl.ds(0, 1), at]
        message_ref[pl.ds(lines + i, 1), :] = offsets_ref[pl.ds(1, 1), at]
    codes = pairs_ref[...].astype(F32) + 1.0
    for i in range(rows):
        message_ref[pl.ds(2 * lines, 1), pl.ds(i * pairs, pairs)] = codes[i : i + 1, :]
    for q in range(rows):
        residual_ref[q] = rows_ref[:, pl.ds(q * SBLOCK, SBLOCK)]


def in_hbm(array):
    return pltpu.with_memory_space_constraint(array, pltpu.HBM)


def pack(station_offsets, block_pairs, residual):
    assert block_pairs.size <= LANES
    rows = 2 * station_offsets.shape[1] // LANES + 8
    return pl.pallas_call(
        pack_kernel,
        out_shape=(jax.ShapeDtypeStruct((rows, LANES), F32), jax.ShapeDtypeStruct((block_pairs.shape[0], residual.shape[0], SBLOCK), F32)),
        in_specs=[pl.BlockSpec(memory_space=pl.ANY)] * 3,
        out_specs=(VMEM, VMEM),
        scratch_shapes=[
            pltpu.VMEM(station_offsets.shape, F32),
            pltpu.VMEM(block_pairs.shape, jnp.int32),
            pltpu.VMEM(residual.shape, F32),
            pltpu.SemaphoreType.DMA((3,)),
        ],
        compiler_params=params(2),
        name="pack",
    )(in_hbm(station_offsets), in_hbm(block_pairs), in_hbm(residual))


def far_parts_kernel(parts_ref, third_ref, message_ref):
    message_ref[0] = parts_ref[0] + third_ref[...]
    message_ref[1] = parts_ref[1]


def far_parts(parts, third):
    return small_call(far_parts_kernel, (2, *third.shape), "far_parts", parts, third)


def both_images_kernel(mine_ref, theirs_ref, images_ref):
    images_ref[0] = mine_ref[0] + theirs_ref[1]
    images_ref[1] = mine_ref[1] + theirs_ref[0]


def both_images(mine, theirs):
    return small_call(both_images_kernel, mine.shape, "both_images", mine, theirs)


def add_kernel(left_ref, right_ref, sum_ref):
    sum_ref[...] = left_ref[...] + right_ref[...]


def pair_kernel(first_ref, second_ref, message_ref):
    message_ref[0] = first_ref[...]
    message_ref[1] = second_ref[...]


def pair_up(first, second):
    return small_call(pair_kernel, (2, *first.shape), "pair", first, second)


def small_call(kernel, shape, name, *arrays):
    return pl.pallas_call(
        kernel,
        out_shape=jax.ShapeDtypeStruct(shape, F32),
        in_specs=[VMEM] * len(arrays),
        out_specs=VMEM,
        compiler_params=params(2),
        name=name,
    )(*arrays)


def prepare_kernel(scale, band_ref, band_row_ref, direction_ref, values_ref, cells_ref, turned_ref):
    blocks = values_ref.shape[0]
    epochs = direction_ref.shape[0]

    @pl.when(pl.program_id(0) == 0)
    def first():
        depth = (band_ref[...].astype(F32) + 0.5) * (DEPTH_RANGE / BANDS)
        turned_ref[...] = (depth * depth).T

    def block(w, unused):
        at = pl.ds(pl.multiple_of(w * CBLOCK, CBLOCK), CBLOCK)
        row = (band_row_ref[:, at].astype(F32) + 0.5) * (DEPTH_RANGE / BANDS)
        shifted = row + DEPTH_SHIFT
        factor = row * scale * (shifted * jnp.sqrt(shifted))
        cells_ref[pl.ds(0, 1), at] = row * row
        cells_ref[pl.ds(1, 1), at] = factor
        high, low = split(direction_ref[:, at] * factor)
        values_ref[w, pl.ds(0, epochs), :] = high
        values_ref[w, pl.ds(epochs, epochs), :] = low
        return 0

    lax.fori_loop(0, blocks, block, 0, unroll=4)


PARTS = 2


def prepare(scale, depth_band, direction):
    epochs, cells = direction.shape
    blocks = cells // CBLOCK
    return pl.pallas_call(
        functools.partial(prepare_kernel, scale),
        grid=(PARTS,),
        out_shape=(
            jax.ShapeDtypeStruct((blocks, 2 * epochs, CBLOCK), BF16),
            jax.ShapeDtypeStruct((2, cells), F32),
            jax.ShapeDtypeStruct((cells // LANES, LANES), F32),
        ),
        in_specs=[
            pl.BlockSpec((cells // LANES, LANES), lambda i: (0, 0)),
            pl.BlockSpec((1, cells // PARTS), lambda i: (0, i)),
            pl.BlockSpec((epochs, cells // PARTS), lambda i: (0, i)),
        ],
        out_specs=(
            pl.BlockSpec((blocks // PARTS, 2 * epochs, CBLOCK), lambda i: (i, 0, 0)),
            pl.BlockSpec((2, cells // PARTS), lambda i: (0, i)),
            VMEM,
        ),
        compiler_params=params(8),
        cost_estimate=pl.CostEstimate(flops=8 * epochs * cells, bytes_accessed=12 * epochs * cells, transcendentals=0),
        name="prepare",
    )(
        in_hbm(depth_band.reshape(cells // LANES, LANES)),
        in_hbm(depth_band.reshape(1, cells)),
        in_hbm(direction),
    )


def tile_offset(place):
    return place * (2 * (lax.axis_index("tile") & 1) - 1)


def send_codes(sizes, messages, codes_ref, scalars_ref, sent):
    cell_blocks, station_blocks, pairs, epochs, places = sizes
    q = parts_of(lax.broadcasted_iota(jnp.int32, (1, LANES), 1), pairs)[0]
    for slot, message_ref in enumerate(messages):
        codes = message_ref[pl.ds(2 * station_blocks * SBLOCK // LANES, 1), :]
        within = codes.astype(jnp.int32) - (cell_blocks * (REACH - tile_offset(places[slot])) + 1)
        hit = jnp.logical_and(within >= 0, within < cell_blocks)
        code = (slot * station_blocks + q) * cell_blocks + within
        codes_ref[pl.ds(slot, 1), :] = jnp.where(hit, code, -1)
    copy = pltpu.make_async_copy(codes_ref, scalars_ref, sent)
    copy.start()
    return copy


def list_pairs(sizes, copy, scalars_ref, list_ref):
    cell_blocks, station_blocks, pairs, epochs, places = sizes
    slots = len(places)
    copy.wait()
    count = jnp.int32(0)
    for slot in range(slots):
        for i in range(station_blocks * pairs):
            code = scalars_ref[slot, i]
            list_ref[count] = code
            count = count + (code >= 0).astype(jnp.int32)
    for i in range(2 * UNROLL):
        list_ref[count + i] = slots * station_blocks * cell_blocks
    return count


def list_scratch(sizes):
    cell_blocks, station_blocks, pairs, epochs, places = sizes
    slots = len(places)
    return [
        pltpu.SMEM((slots * station_blocks * pairs + 2 * UNROLL,), jnp.int32),
        pltpu.VMEM((slots, LANES), jnp.int32),
        pltpu.SMEM((slots, LANES), jnp.int32),
        pltpu.SemaphoreType.DMA(()),
    ]


UNROLL = 4


def pipelined(count, stage, issue, collect):
    stage(0, 0)
    stage(1, 1)
    issue(0, 0)

    def rounds(first, number, size):
        def step(j, unused):
            for k in range(size):
                i = first + size * j + k
                issue(i + 1, (k + 1) % 2)
                stage(i + 2, k % 2)
                collect(i, k % 2)
            return 0

        lax.fori_loop(0, number, step, 0)
        return first + size * number

    whole = count // UNROLL
    done = rounds(0, whole, UNROLL)
    done = rounds(done, (count > 1 + done).astype(jnp.int32), UNROLL // 2)
    collect(done, 0)


def doubled(array, group):
    groups = [array[:, i : i + group] for i in range(0, array.shape[1], group)]
    return jnp.concatenate([group for group in groups for _ in range(2)], axis=1)


def multiply_add(sums_ref, left, pieces, group, unit, register):
    rows = pieces[0][0].shape[0]
    tile = []
    for i in range(0, len(pieces), group // rows):
        high, low = zip(*pieces[i : i + group // rows])
        tile += high + low
    pltpu.matmul_push_rhs(jnp.concatenate(tile, axis=0), register, unit)
    pltpu.matmul_acc_lhs(sums_ref, left, load_staged_rhs=register)


def accumulators(rows):
    return [pltpu.ACC(unit)((rows, TILE), F32) for unit in (0, 1)] * 2


def inverse_cube(squared):
    return lax.rsqrt(squared * squared * squared)


def forward_kernel(sizes, *refs):
    cell_blocks, station_blocks, pairs, epochs, places = sizes
    slots = len(places)
    messages = refs[:slots]
    values_ref, turned_ref = refs[slots : slots + 2]
    images_ref, list_ref, codes_ref, scalars_ref, sent, *scratch = refs[slots + 2 :]
    across_ref, along_ref, image_ref, gaps_ref, lines_ref, depths_ref = scratch
    copy = send_codes(sizes, messages, codes_ref, scalars_ref, sent)
    dummy = slots * station_blocks
    per_block = SBLOCK // LANES
    lines = station_blocks * per_block
    across_ref[pl.ds(dummy, 1), :] = jnp.zeros((1, SBLOCK), F32)
    along_ref[pl.ds(dummy, 1), :] = jnp.zeros((1, SBLOCK), F32)
    image_ref[...] = jnp.zeros_like(image_ref)
    for slot in range(slots):
        for i in range(lines):
            place = (pl.ds(slot * station_blocks + i // per_block, 1), pl.ds(i % per_block * LANES, LANES))
            across_ref[place] = messages[slot][pl.ds(i, 1), :] + tile_offset(places[slot]).astype(F32)
            along_ref[place] = messages[slot][pl.ds(lines + i, 1), :]
    count = list_pairs(sizes, copy, scalars_ref, list_ref)
    column = lax.broadcasted_iota(jnp.int32, (COL_SIDE, SBLOCK), 0).astype(F32)
    column = (column + 0.5) / COL_SIDE
    rows = CBLOCK // COL_SIDE
    line = (lax.broadcasted_iota(jnp.int32, (rows, SBLOCK), 0).astype(F32) + 0.5) / COL_SIDE

    def stage(i, k):
        code = list_ref[i]
        q, w = parts_of(code, cell_blocks)
        across = across_ref[pl.ds(q, 1), :] - column
        gaps_ref[k] = across * across
        along = along_ref[pl.ds(q, 1), :] - (w & 1).astype(F32) * (rows / COL_SIDE) - line
        lines_ref[k] = along * along
        turned = pltpu.roll(turned_ref[...], (LANES - w * (CBLOCK // LANES)) & (LANES - 1), 1)
        for part in range(CBLOCK // LANES):
            depths_ref[k, pl.ds(part * LANES, LANES), :] = jnp.broadcast_to(turned[:, part : part + 1], (LANES, LANES))

    def issue(sums, i, k):
        w = list_ref[i] & (cell_blocks - 1)
        across = gaps_ref[k]
        for tile in range(CBLOCK // HALF):
            pieces = []
            for at in range(0, HALF, COL_SIDE):
                y = (tile * HALF + at) // COL_SIDE
                depth = depths_ref[k, pl.ds(y * COL_SIDE, COL_SIDE), :]
                depth = jnp.concatenate([depth] * (SBLOCK // LANES), axis=1)
                along = lines_ref[k, pl.ds(y, 1), :]
                pieces.append(split(inverse_cube((across + along) + depth)))
            left = doubled(values_ref[w, :, pl.ds(tile * HALF, HALF)], HALF)
            multiply_add(sums[2 * k + tile % 2], left, pieces, HALF, tile % 2, tile // 2)

    def collect(sums, i, k):
        q, _ = parts_of(list_ref[i], cell_blocks)
        both = pltpu.matmul_pop(sums[2 * k]) + pltpu.matmul_pop(sums[2 * k + 1])
        image_ref[q] += both[:epochs] + both[epochs:]

    def run(*sums):
        pipelined(count, stage, functools.partial(issue, sums), functools.partial(collect, sums))

    pl.run_scoped(run, *accumulators(2 * epochs))
    for slot in range(slots):
        images_ref[slot] = image_ref[pl.ds(slot * station_blocks, station_blocks)]


def forward(sizes, messages, values, turned):
    cell_blocks, station_blocks, pairs, epochs, places = sizes
    slots = len(places)
    rows = (slots * station_blocks + 8) // 8 * 8
    return pl.pallas_call(
        functools.partial(forward_kernel, sizes),
        out_shape=jax.ShapeDtypeStruct((slots, station_blocks, epochs, SBLOCK), F32),
        in_specs=[VMEM] * (slots + 2),
        out_specs=VMEM,
        scratch_shapes=list_scratch(sizes)
        + [
            pltpu.VMEM((rows, SBLOCK), F32),
            pltpu.VMEM((rows, SBLOCK), F32),
            pltpu.VMEM((slots * station_blocks + 1, epochs, SBLOCK), F32),
            pltpu.VMEM((2, COL_SIDE, SBLOCK), F32),
            pltpu.VMEM((2, CBLOCK // COL_SIDE, SBLOCK), F32),
            pltpu.VMEM((2, CBLOCK, LANES), F32),
        ],
        compiler_params=params(),
        cost_estimate=estimate(sizes, 0.1 if slots > 2 else 1),
        name="forward",
    )(*messages, values, turned)


def estimate(sizes, part=1):
    cell_blocks, station_blocks, pairs, epochs, places = sizes
    slots = len(places)
    entries = station_blocks * pairs * slots // (2 * REACH + 1) * SBLOCK * CBLOCK
    return pl.CostEstimate(flops=int(2 * 1200 * entries * part), bytes_accessed=2**20, transcendentals=entries)


def adjoint_sums(sizes, messages, residuals, images, cells_ref, total_ref, scratch, clear):
    cell_blocks, station_blocks, pairs, epochs, places = sizes
    slots = len(places)
    list_ref, codes_ref, scalars_ref, sent, stations_ref, terms_ref, depths_ref, gaps_ref, lines_ref = scratch
    copy = send_codes(sizes, messages, codes_ref, scalars_ref, sent)
    dummy = slots * station_blocks
    stations_ref[slots] = jnp.zeros(stations_ref.shape[1:], F32)
    per_block = SBLOCK // LANES
    lane_rows = station_blocks * per_block
    for slot in range(slots):
        shift = tile_offset(places[slot]).astype(F32)
        rows = [messages[slot][pl.ds(0, lane_rows), :] + shift, messages[slot][pl.ds(lane_rows, lane_rows), :]]
        rows.append(jnp.zeros((LANES - 2 * lane_rows, LANES), F32))
        stations_ref[slot] = jnp.concatenate(rows, axis=0).T
    if clear:
        total_ref[...] = jnp.zeros_like(total_ref)
    count = list_pairs(sizes, copy, scalars_ref, list_ref)
    terms_ref[dummy] = jnp.zeros(terms_ref.shape[1:], BF16)
    for slot in range(slots):
        for q in range(station_blocks):
            stacked = doubled(jnp.concatenate([residuals[slot][q], images[slot][q]], axis=0), GROUP)
            high, low = split(stacked)
            terms_ref[slot * station_blocks + q, pl.ds(0, 2 * epochs), :] = high
            terms_ref[slot * station_blocks + q, pl.ds(2 * epochs, 2 * epochs), :] = low
    lane = lax.broadcasted_iota(jnp.int32, (1, LANES), 1)
    column = ((lane % COL_SIDE).astype(F32) + 0.5) / COL_SIDE
    line = ((lane // COL_SIDE).astype(F32) + 0.5) / COL_SIDE
    rows = CBLOCK // COL_SIDE
    chunks = CBLOCK // LANES
    stride = LANES / COL_SIDE / COL_SIDE

    def stage(i, k):
        code = list_ref[i]
        q, w = parts_of(code, cell_blocks)
        slot, within = parts_of(q, station_blocks)
        depths_ref[k] = cells_ref[pl.ds(0, 1), pl.ds(pl.multiple_of(w * CBLOCK, CBLOCK), CBLOCK)]
        lines = line + (w & 1).astype(F32) * (rows / COL_SIDE)
        places = pltpu.roll(stations_ref[slot], (LANES - within * per_block) & (LANES - 1), 1)
        for part in range(per_block):
            at = pl.ds(part * LANES, LANES)
            across = jnp.broadcast_to(places[:, part : part + 1], (LANES, LANES)) - column
            gaps_ref[k, at, :] = across * across
            along = jnp.broadcast_to(places[:, lane_rows + part : lane_rows + part + 1], (LANES, LANES))
            lines_ref[k, at, :] = along - lines

    def issue(sums, i, k):
        q, _ = parts_of(list_ref[i], cell_blocks)
        depth = depths_ref[k]
        for part in range(per_block):
            pieces = ([], [])
            for at in range(part * LANES, (part + 1) * LANES, 16):
                across = gaps_ref[k, pl.ds(at, 16), :]
                along = lines_ref[k, pl.ds(at, 16), :]
                level = across + along * along
                slope = stride * stride - 2 * stride * along
                for unit in range(2):
                    near = []
                    for chunk in range(unit * chunks // 2, (unit + 1) * chunks // 2):
                        squared = level + depth[:, chunk * LANES : (chunk + 1) * LANES]
                        near.append(split(inverse_cube(squared)))
                        if chunk < chunks - 1:
                            level = level + slope
                            slope = slope + 2 * stride * stride
                    pieces[unit].append([jnp.concatenate(terms, axis=1) for terms in zip(*near)])
            left = terms_ref[q, :, pl.ds(part * TILE, TILE)]
            for unit in range(2):
                multiply_add(sums[2 * k + unit], left, pieces[unit], GROUP, unit, part)

    def collect(sums, i, k):
        w = list_ref[i] & (cell_blocks - 1)
        for unit in range(2):
            both = pltpu.matmul_pop(sums[2 * k + unit])
            total_ref[w, :, pl.ds(unit * TILE, TILE)] += both[: 2 * epochs] + both[2 * epochs :]

    def run(*sums):
        pipelined(count, stage, functools.partial(issue, sums), functools.partial(collect, sums))

    pl.run_scoped(run, *accumulators(4 * epochs))


def slot_refs(slots, refs):
    messages, (residuals, images), rest = refs[:slots], refs[slots : slots + 2], refs[slots + 2 :]
    residuals, images = [residuals.at[0], residuals.at[1]], [images.at[0], images.at[1]]
    if slots == 3:
        third, *rest = rest
        residuals.append(third.at[0])
        images.append(third.at[1])
    return messages, residuals, images, rest


def near_kernel(sizes, *refs):
    cell_blocks, station_blocks, pairs, epochs, places = sizes
    slots = len(places)
    messages, residuals, images, rest = slot_refs(slots, refs)
    cells_ref, total_ref, *scratch = rest
    adjoint_sums(sizes, messages, residuals, images, cells_ref, total_ref, scratch, True)


def squares_kernel(old_ref, direction_ref, sums_ref):
    epochs, cells = direction_ref.shape

    def add(w, sums):
        at = pl.ds(pl.multiple_of(w * CBLOCK, CBLOCK), CBLOCK)
        old, direction = old_ref[:, at], direction_ref[:, at]
        return sums[0] + old * old, sums[1] + direction * direction

    zero = jnp.zeros((epochs, CBLOCK), F32)
    for i, total in enumerate(lax.fori_loop(0, cells // CBLOCK, add, (zero, zero), unroll=4)):
        sums_ref[pl.ds(i, 1), :] = jnp.broadcast_to(jnp.sum(total).reshape(1, 1), (1, LANES))


def far_kernel(sizes, *refs):
    cell_blocks, station_blocks, pairs, epochs, places = sizes
    slots = len(places)
    messages, residuals, images, rest = slot_refs(slots, refs)
    cells_ref, _, sums_ref, model_ref, direction_ref, image_ref = rest[:6]
    constant_ref, slope_ref, stats_ref, total_ref, *scratch = rest[6:]
    adjoint_sums(sizes, messages, residuals, images, cells_ref, total_ref, scratch, False)
    zero = jnp.zeros((epochs, CBLOCK), F32)

    def combine(w, sums):
        at = pl.ds(pl.multiple_of(w * CBLOCK, CBLOCK), CBLOCK)
        total = total_ref[w] * cells_ref[pl.ds(1, 1), at]
        constant = total[:epochs] - DAMPING * model_ref[:, at]
        slope = total[epochs:] + DAMPING * direction_ref[:, at]
        constant_ref[:, at] = constant
        slope_ref[:, at] = slope
        return sums[0] + constant * slope, sums[1] + slope * slope

    cross, square = lax.fori_loop(0, cell_blocks, combine, (zero, zero), unroll=4)
    square = jnp.sum(square).reshape(1, 1)
    cross = jnp.sum(cross).reshape(1, 1)
    local_step = jnp.where(square > 0, cross / jnp.where(square > 0, square, 1.0), 0.0)

    def remainder(w, sums):
        at = pl.ds(pl.multiple_of(w * CBLOCK, CBLOCK), CBLOCK)
        slope = slope_ref[:, at]
        left = constant_ref[:, at] - local_step * slope
        return sums[0] + left * left, sums[1] + left * slope

    left_square, left_cross = lax.fori_loop(0, cell_blocks, remainder, (zero, zero), unroll=4)
    image = image_ref[0]
    stats = [
        sums_ref[pl.ds(0, 1), pl.ds(0, 1)],
        sums_ref[pl.ds(1, 1), pl.ds(0, 1)],
        jnp.sum(image * image).reshape(1, 1),
        local_step,
        jnp.sum(left_square).reshape(1, 1),
        jnp.sum(left_cross).reshape(1, 1),
        jnp.sqrt(square),
    ]
    lane = lax.broadcasted_iota(jnp.int32, (1, LANES), 1)
    row = jnp.zeros((1, LANES), F32)
    for i, value in enumerate(stats):
        row = jnp.where(lane == i, value, row)
    for i in range(stats_ref.shape[0]):
        stats_ref[i] = row


def adjoint(sizes, messages, terms, cell_rows, *others, ranks=None):
    cell_blocks, station_blocks, pairs, epochs, places = sizes
    slots = len(places)
    total = (cell_blocks, 2 * epochs, CBLOCK)
    scratch = list_scratch(sizes) + [
        pltpu.VMEM((slots + 1, LANES, LANES), F32),
        pltpu.VMEM((slots * station_blocks + 1, 4 * epochs, 2 * SBLOCK), BF16),
        pltpu.VMEM((2, 1, CBLOCK), F32),
        pltpu.VMEM((2, SBLOCK, LANES), F32),
        pltpu.VMEM((2, SBLOCK, LANES), F32),
    ]
    if ranks is None:
        kernel, shapes, aliases = near_kernel, [total], {}
    else:
        kernel, cells = far_kernel, (epochs, cell_blocks * CBLOCK)
        shapes = [cells, cells, (ranks, 1, LANES), total]
        aliases = {slots + len(terms) + 1: 3}
    return pl.pallas_call(
        functools.partial(kernel, sizes),
        out_shape=tuple(jax.ShapeDtypeStruct(shape, F32) for shape in shapes),
        in_specs=[VMEM] * (slots + len(terms) + 1 + len(others)),
        out_specs=(VMEM,) * len(shapes),
        scratch_shapes=scratch,
        input_output_aliases=aliases,
        compiler_params=params(),
        cost_estimate=estimate(sizes),
        name="near" if ranks is None else "far",
    )(*messages, *terms, cell_rows, *others)


def finish_kernel(
    stats_ref, constant_ref, slope_ref, model_ref, direction_ref, residual_ref, image_ref,
    model_out, residual_out, direction_out, new_model, new_residual, new_direction, sent,
):
    stats = stats_ref[...][:, 0, :]
    gamma_old, direction_square, image_square = (
        jnp.sum(stats[:, i : i + 1], axis=0, keepdims=True) for i in range(3)
    )
    step = gamma_old / (image_square + DAMPING * direction_square + GUARD)
    ahead = step - stats[:, 3:4]
    reach = ahead * stats[:, 6:7]
    gamma_new = jnp.sum(stats[:, 4:5] - 2.0 * ahead * stats[:, 5:6] + reach * reach, axis=0, keepdims=True)
    ratio = gamma_new / (gamma_old + GUARD)
    copies = []

    def send(i, source, target, at):
        copies.append(pltpu.make_async_copy(source.at[:, at], target.at[:, at], sent.at[i]))
        copies[-1].start()

    for q in range(image_ref.shape[1]):
        at = pl.ds(q * SBLOCK, SBLOCK)
        new_residual[:, at] = residual_ref[q] - step * image_ref[0, q]
    send(0, new_residual, residual_out, pl.ds(0, new_residual.shape[1]))
    cells = model_ref.shape[1] // FINISH_PARTS
    for part in range(FINISH_PARTS):

        def block(w, unused):
            at = pl.ds(pl.multiple_of(part * cells + w * CBLOCK, CBLOCK), CBLOCK)
            direction = direction_ref[:, at]
            new_model[:, at] = model_ref[:, at] + step * direction
            new_direction[:, at] = (constant_ref[:, at] - step * slope_ref[:, at]) + ratio * direction
            return 0

        lax.fori_loop(0, cells // CBLOCK, block, 0, unroll=4)
        send(1 + 2 * part, new_model, model_out, pl.ds(part * cells, cells))
        send(2 + 2 * part, new_direction, direction_out, pl.ds(part * cells, cells))
    for copy in copies:
        copy.wait()


FINISH_PARTS = 4


def finish(stats, constant, slope, model_field, direction, residual, image):
    blocks, epochs, _ = residual.shape
    outs = (model_field.shape, (epochs, blocks * SBLOCK), direction.shape)
    return pl.pallas_call(
        finish_kernel,
        out_shape=tuple(jax.ShapeDtypeStruct(shape, F32) for shape in outs),
        in_specs=[VMEM] * 7,
        out_specs=(pl.BlockSpec(memory_space=pl.ANY),) * 3,
        scratch_shapes=[pltpu.VMEM(shape, F32) for shape in outs]
        + [pltpu.SemaphoreType.DMA((1 + 2 * FINISH_PARTS,))],
        compiler_params=params(),
        name="finish",
    )(stats, constant, slope, model_field, direction, residual, image)


def after(arrays, others):
    return lax.optimization_barrier((arrays, others))[0]


def shards(model_field, direction, old_grad, residual, block_pairs, depth_band, station_offsets):
    ranks = lax.axis_size("tile")
    epochs, cells = model_field.shape
    station_blocks, pairs = block_pairs.shape
    cell_blocks = cells // CBLOCK

    def to_partner(array):
        return lax.ppermute(array, "tile", [(i, i ^ 1) for i in range(ranks)])

    def across(message):
        ends = [(i, i + 1) for i in range(1, ranks - 1, 2)]
        return lax.ppermute(message, "tile", ends + [(j, i) for i, j in ends])

    sizes = (cell_blocks, station_blocks, pairs, epochs)
    near_slots, far_slots = (*sizes, (0, -1)), (*sizes, (1, 2, -2))

    own, residual = pack(station_offsets, block_pairs, residual)
    partner = to_partner(own)
    near = [own, partner]
    partner_residual = to_partner(residual)
    values, cell_rows, turned = prepare(2.0 / math.sqrt(cells), after(depth_band, own), direction)
    arrived = across(pair_up(own, after(partner, values)))
    residuals = pair_up(residual, partner_residual)
    arrived = after(arrived, residuals)
    far = [arrived[0], arrived[1], to_partner(arrived[0])]

    far_residuals = across(residuals)
    parts = forward(far_slots, far, values, turned)
    parts, far_residuals = after((parts, far_residuals), (far_residuals, parts))
    returned = to_partner(parts[2])
    given = across(far_parts(parts, returned))
    mine = forward(near_slots, after(near, returned), values, turned)
    sums = small_call(squares_kernel, (2, LANES), "squares", *after((old_grad, direction), mine))
    given = after(given, (mine, sums))
    mine = small_call(add_kernel, mine.shape, "add", mine, given)
    images = both_images(mine, to_partner(mine))

    far_images = across(images)
    (near_total,) = adjoint(near_slots, near, [residuals, images], cell_rows)
    far_images = after(far_images, near_total)
    thirds = to_partner(pair_up(far_residuals[0], far_images[0]))
    constant, slope, stats, _ = adjoint(
        far_slots, far, [far_residuals, far_images, thirds], cell_rows,
        near_total, sums, model_field, direction, images, ranks=ranks,
    )
    stats = lax.all_to_all(stats, "tile", 0, 0)
    return finish(stats, constant, slope, model_field, direction, residual, images)


def solution(mesh):
    wide = P(None, ("groups", "tile"))
    mapped = jax.shard_map(
        shards,
        mesh=mesh,
        in_specs=(wide, wide, wide, wide, P(("groups", "tile"), None), P(("groups", "tile")), wide),
        out_specs=(wide, wide, wide),
        check_vma=False,
    )

    def step(*arrays):
        with jax.sharding.use_abstract_mesh(mesh.abstract_mesh):
            return mapped(*arrays)

    return step
```

```python
import functools
import math

import jax
import jax.numpy as jnp
from jax import lax
from jax.experimental import pallas as pl
from jax.experimental.pallas import tpu as pltpu
from jax.sharding import PartitionSpec as P

CBLOCK = 512
SBLOCK = 256
REACH = 2
BANDS = 16
COL_SIDE = 32
DEPTH_RANGE = 2.0
DEPTH_SHIFT = 0.25
DAMPING = 1.0
GUARD = 1e-06

F32 = jnp.float32
BF16 = jnp.bfloat16
LANES = 128
TILE = 256
HALF = TILE // 2
GROUP = HALF // 2

SMEM = pl.BlockSpec(memory_space=pltpu.SMEM)
VMEM = pl.BlockSpec(memory_space=pltpu.VMEM)


def params(mebibytes=16):
    return pltpu.CompilerParams(vmem_limit_bytes=mebibytes * 2**20)


def parts_of(number, size):
    assert size & (size - 1) == 0
    return number >> (size.bit_length() - 1), number & (size - 1)


def split(values):
    high = values.astype(BF16)
    return high, (values - high.astype(F32)).astype(BF16)


def dot(left, right):
    return jnp.dot(left, right, preferred_element_type=F32)


def pack_kernel(offsets_any, pairs_any, residual_any, message_ref, residual_ref, offsets_ref, pairs_ref, rows_ref, sent):
    copies = [
        pltpu.make_async_copy(offsets_any, offsets_ref, sent.at[0]),
        pltpu.make_async_copy(pairs_any, pairs_ref, sent.at[1]),
        pltpu.make_async_copy(residual_any, rows_ref, sent.at[2]),
    ]
    for copy in copies:
        copy.start()
    lines = offsets_ref.shape[1] // LANES
    rows, pairs = pairs_ref.shape
    message_ref[pl.ds(2 * lines, 8), :] = jnp.zeros((8, LANES), F32)
    for copy in copies:
        copy.wait()
    for i in range(lines):
        at = pl.ds(i * LANES, LANES)
        message_ref[pl.ds(i, 1), :] = offsets_ref[pl.ds(0, 1), at]
        message_ref[pl.ds(lines + i, 1), :] = offsets_ref[pl.ds(1, 1), at]
    codes = pairs_ref[...].astype(F32) + 1.0
    for i in range(rows):
        message_ref[pl.ds(2 * lines, 1), pl.ds(i * pairs, pairs)] = codes[i : i + 1, :]
    for q in range(rows):
        residual_ref[q] = rows_ref[:, pl.ds(q * SBLOCK, SBLOCK)]


def in_hbm(array):
    return pltpu.with_memory_space_constraint(array, pltpu.HBM)


def pack(station_offsets, block_pairs, residual):
    assert block_pairs.size <= LANES
    rows = 2 * station_offsets.shape[1] // LANES + 8
    return pl.pallas_call(
        pack_kernel,
        out_shape=(jax.ShapeDtypeStruct((rows, LANES), F32), jax.ShapeDtypeStruct((block_pairs.shape[0], residual.shape[0], SBLOCK), F32)),
        in_specs=[pl.BlockSpec(memory_space=pl.ANY)] * 3,
        out_specs=(VMEM, VMEM),
        scratch_shapes=[
            pltpu.VMEM(station_offsets.shape, F32),
            pltpu.VMEM(block_pairs.shape, jnp.int32),
            pltpu.VMEM(residual.shape, F32),
            pltpu.SemaphoreType.DMA((3,)),
        ],
        compiler_params=params(2),
        name="pack",
    )(in_hbm(station_offsets), in_hbm(block_pairs), in_hbm(residual))


def far_parts_kernel(parts_ref, third_ref, message_ref):
    message_ref[0] = parts_ref[0] + third_ref[...]
    message_ref[1] = parts_ref[1]


def far_parts(parts, third):
    return small_call(far_parts_kernel, (2, *third.shape), "far_parts", parts, third)


def both_images_kernel(mine_ref, theirs_ref, images_ref):
    images_ref[0] = mine_ref[0] + theirs_ref[1]
    images_ref[1] = mine_ref[1] + theirs_ref[0]


def both_images(mine, theirs):
    return small_call(both_images_kernel, mine.shape, "both_images", mine, theirs)


def thirds_kernel(residuals_ref, images_ref, message_ref):
    message_ref[0] = residuals_ref[0]
    message_ref[1] = images_ref[0]


def add_kernel(left_ref, right_ref, sum_ref):
    sum_ref[...] = left_ref[...] + right_ref[...]


def pair_kernel(first_ref, second_ref, message_ref):
    message_ref[0] = first_ref[...]
    message_ref[1] = second_ref[...]


def pair_up(first, second):
    return small_call(pair_kernel, (2, *first.shape), "pair", first, second)


def small_call(kernel, shape, name, *arrays):
    return pl.pallas_call(
        kernel,
        out_shape=jax.ShapeDtypeStruct(shape, F32),
        in_specs=[VMEM] * len(arrays),
        out_specs=VMEM,
        compiler_params=params(2),
        name=name,
    )(*arrays)


def prepare_kernel(scale, band_ref, band_row_ref, direction_ref, values_ref, cells_ref, turned_ref):
    blocks = values_ref.shape[0]
    epochs = direction_ref.shape[0]

    @pl.when(pl.program_id(0) == 0)
    def first():
        depth = (band_ref[...].astype(F32) + 0.5) * (DEPTH_RANGE / BANDS)
        turned_ref[...] = (depth * depth).T

    def block(w, unused):
        at = pl.ds(pl.multiple_of(w * CBLOCK, CBLOCK), CBLOCK)
        row = (band_row_ref[:, at].astype(F32) + 0.5) * (DEPTH_RANGE / BANDS)
        shifted = row + DEPTH_SHIFT
        factor = row * scale * (shifted * jnp.sqrt(shifted))
        cells_ref[pl.ds(0, 1), at] = row * row
        cells_ref[pl.ds(1, 1), at] = factor
        high, low = split(direction_ref[:, at] * factor)
        values_ref[w, pl.ds(0, epochs), :] = high
        values_ref[w, pl.ds(epochs, epochs), :] = low
        return 0

    lax.fori_loop(0, blocks, block, 0, unroll=4)


PARTS = 2


def prepare(scale, depth_band, direction):
    epochs, cells = direction.shape
    blocks = cells // CBLOCK
    return pl.pallas_call(
        functools.partial(prepare_kernel, scale),
        grid=(PARTS,),
        out_shape=(
            jax.ShapeDtypeStruct((blocks, 2 * epochs, CBLOCK), BF16),
            jax.ShapeDtypeStruct((2, cells), F32),
            jax.ShapeDtypeStruct((cells // LANES, LANES), F32),
        ),
        in_specs=[
            pl.BlockSpec((cells // LANES, LANES), lambda i: (0, 0)),
            pl.BlockSpec((1, cells // PARTS), lambda i: (0, i)),
            pl.BlockSpec((epochs, cells // PARTS), lambda i: (0, i)),
        ],
        out_specs=(
            pl.BlockSpec((blocks // PARTS, 2 * epochs, CBLOCK), lambda i: (i, 0, 0)),
            pl.BlockSpec((2, cells // PARTS), lambda i: (0, i)),
            VMEM,
        ),
        compiler_params=params(8),
        cost_estimate=pl.CostEstimate(flops=8 * epochs * cells, bytes_accessed=12 * epochs * cells, transcendentals=0),
        name="prepare",
    )(
        in_hbm(depth_band.reshape(cells // LANES, LANES)),
        in_hbm(depth_band.reshape(1, cells)),
        in_hbm(direction),
    )


def tile_offset(place):
    return place * (2 * (lax.axis_index("tile") & 1) - 1)


def send_codes(sizes, messages, codes_ref, scalars_ref, sent):
    cell_blocks, station_blocks, pairs, epochs, places = sizes
    q = parts_of(lax.broadcasted_iota(jnp.int32, (1, LANES), 1), pairs)[0]
    for slot, message_ref in enumerate(messages):
        codes = message_ref[pl.ds(2 * station_blocks * SBLOCK // LANES, 1), :]
        within = codes.astype(jnp.int32) - (cell_blocks * (REACH - tile_offset(places[slot])) + 1)
        hit = jnp.logical_and(within >= 0, within < cell_blocks)
        code = (slot * station_blocks + q) * cell_blocks + within
        codes_ref[pl.ds(slot, 1), :] = jnp.where(hit, code, -1)
    copy = pltpu.make_async_copy(codes_ref, scalars_ref, sent)
    copy.start()
    return copy


def list_pairs(sizes, copy, scalars_ref, list_ref):
    cell_blocks, station_blocks, pairs, epochs, places = sizes
    slots = len(places)
    copy.wait()
    count = jnp.int32(0)
    for slot in range(slots):
        for i in range(station_blocks * pairs):
            code = scalars_ref[slot, i]
            list_ref[count] = code
            count = count + (code >= 0).astype(jnp.int32)
    for i in range(2 * UNROLL):
        list_ref[count + i] = slots * station_blocks * cell_blocks
    return count


def list_scratch(sizes):
    cell_blocks, station_blocks, pairs, epochs, places = sizes
    slots = len(places)
    return [
        pltpu.SMEM((slots * station_blocks * pairs + 2 * UNROLL,), jnp.int32),
        pltpu.VMEM((slots, LANES), jnp.int32),
        pltpu.SMEM((slots, LANES), jnp.int32),
        pltpu.SemaphoreType.DMA(()),
    ]


UNROLL = 4


def pipelined(count, stage, issue, collect):
    stage(0, 0)
    stage(1, 1)
    issue(0, 0)

    def rounds(first, number, size):
        def step(j, unused):
            for k in range(size):
                i = first + size * j + k
                issue(i + 1, (k + 1) % 2)
                stage(i + 2, k % 2)
                collect(i, k % 2)
            return 0

        lax.fori_loop(0, number, step, 0)
        return first + size * number

    whole = count // UNROLL
    done = rounds(0, whole, UNROLL)
    done = rounds(done, (count > 1 + done).astype(jnp.int32), UNROLL // 2)
    collect(done, 0)


def doubled(array, group):
    groups = [array[:, i : i + group] for i in range(0, array.shape[1], group)]
    return jnp.concatenate([group for group in groups for _ in range(2)], axis=1)


def multiply_add(sums_ref, left, pieces, group, unit, register):
    rows = pieces[0][0].shape[0]
    tile = []
    for i in range(0, len(pieces), group // rows):
        high, low = zip(*pieces[i : i + group // rows])
        tile += high + low
    pltpu.matmul_push_rhs(jnp.concatenate(tile, axis=0), register, unit)
    pltpu.matmul_acc_lhs(sums_ref, left, load_staged_rhs=register)


def accumulators(rows):
    return [pltpu.ACC(unit)((rows, TILE), F32) for unit in (0, 1)] * 2


def inverse_cube(squared):
    return lax.rsqrt(squared * squared * squared)


def forward_kernel(sizes, *refs):
    cell_blocks, station_blocks, pairs, epochs, places = sizes
    slots = len(places)
    messages = refs[:slots]
    values_ref, turned_ref = refs[slots : slots + 2]
    outs = 1 + (slots > 2)
    images_refs = refs[slots + 2 : slots + 2 + outs]
    list_ref, codes_ref, scalars_ref, sent, *scratch = refs[slots + 2 + outs :]
    across_ref, along_ref, image_ref, gaps_ref, lines_ref, depths_ref = scratch
    copy = send_codes(sizes, messages, codes_ref, scalars_ref, sent)
    dummy = slots * station_blocks
    per_block = SBLOCK // LANES
    lines = station_blocks * per_block
    across_ref[pl.ds(dummy, 1), :] = jnp.zeros((1, SBLOCK), F32)
    along_ref[pl.ds(dummy, 1), :] = jnp.zeros((1, SBLOCK), F32)
    image_ref[...] = jnp.zeros_like(image_ref)
    for slot in range(slots):
        for i in range(lines):
            place = (pl.ds(slot * station_blocks + i // per_block, 1), pl.ds(i % per_block * LANES, LANES))
            across_ref[place] = messages[slot][pl.ds(i, 1), :] + tile_offset(places[slot]).astype(F32)
            along_ref[place] = messages[slot][pl.ds(lines + i, 1), :]
    count = list_pairs(sizes, copy, scalars_ref, list_ref)
    column = lax.broadcasted_iota(jnp.int32, (COL_SIDE, SBLOCK), 0).astype(F32)
    column = (column + 0.5) / COL_SIDE
    rows = CBLOCK // COL_SIDE
    line = (lax.broadcasted_iota(jnp.int32, (rows, SBLOCK), 0).astype(F32) + 0.5) / COL_SIDE

    def stage(i, k):
        code = list_ref[i]
        q, w = parts_of(code, cell_blocks)
        across = across_ref[pl.ds(q, 1), :] - column
        gaps_ref[k] = across * across
        along = along_ref[pl.ds(q, 1), :] - (w & 1).astype(F32) * (rows / COL_SIDE) - line
        lines_ref[k] = along * along
        turned = pltpu.roll(turned_ref[...], (LANES - w * (CBLOCK // LANES)) & (LANES - 1), 1)
        for part in range(CBLOCK // LANES):
            depths_ref[k, pl.ds(part * LANES, LANES), :] = jnp.broadcast_to(turned[:, part : part + 1], (LANES, LANES))

    def issue(sums, i, k):
        w = list_ref[i] & (cell_blocks - 1)
        across = gaps_ref[k]
        for tile in range(CBLOCK // HALF):
            pieces = []
            for at in range(0, HALF, COL_SIDE):
                y = (tile * HALF + at) // COL_SIDE
                depth = depths_ref[k, pl.ds(y * COL_SIDE, COL_SIDE), :]
                depth = jnp.concatenate([depth] * (SBLOCK // LANES), axis=1)
                along = lines_ref[k, pl.ds(y, 1), :]
                pieces.append(split(inverse_cube((across + along) + depth)))
            left = doubled(values_ref[w, :, pl.ds(tile * HALF, HALF)], HALF)
            multiply_add(sums[2 * k + tile % 2], left, pieces, HALF, tile % 2, tile // 2)

    def collect(sums, i, k):
        q, _ = parts_of(list_ref[i], cell_blocks)
        both = pltpu.matmul_pop(sums[2 * k]) + pltpu.matmul_pop(sums[2 * k + 1])
        image_ref[q] += both[:epochs] + both[epochs:]

    def run(*sums):
        pipelined(count, stage, functools.partial(issue, sums), functools.partial(collect, sums))

    pl.run_scoped(run, *accumulators(2 * epochs))
    for slot in range(slots):
        image = image_ref[pl.ds(slot * station_blocks, station_blocks)]
        if slot < 2:
            images_refs[0][slot] = image
        else:
            images_refs[1][...] = image


def forward(sizes, messages, values, turned):
    cell_blocks, station_blocks, pairs, epochs, places = sizes
    slots = len(places)
    rows = (slots * station_blocks + 8) // 8 * 8
    block = (station_blocks, epochs, SBLOCK)
    shapes = [(2, *block), block][: slots - 1]
    return pl.pallas_call(
        functools.partial(forward_kernel, sizes),
        out_shape=tuple(jax.ShapeDtypeStruct(shape, F32) for shape in shapes),
        in_specs=[VMEM] * (slots + 2),
        out_specs=(VMEM,) * len(shapes),
        scratch_shapes=list_scratch(sizes)
        + [
            pltpu.VMEM((rows, SBLOCK), F32),
            pltpu.VMEM((rows, SBLOCK), F32),
            pltpu.VMEM((slots * station_blocks + 1, epochs, SBLOCK), F32),
            pltpu.VMEM((2, COL_SIDE, SBLOCK), F32),
            pltpu.VMEM((2, CBLOCK // COL_SIDE, SBLOCK), F32),
            pltpu.VMEM((2, CBLOCK, LANES), F32),
        ],
        compiler_params=params(),
        cost_estimate=estimate(sizes, 0.1 if slots > 2 else 1),
        name="forward",
    )(*messages, values, turned)


def estimate(sizes, part=1):
    cell_blocks, station_blocks, pairs, epochs, places = sizes
    slots = len(places)
    entries = station_blocks * pairs * slots // (2 * REACH + 1) * SBLOCK * CBLOCK
    return pl.CostEstimate(flops=int(2 * 1200 * entries * part), bytes_accessed=2**20, transcendentals=entries)


def adjoint_sums(sizes, messages, residuals, images, cells_ref, total_ref, scratch, clear):
    cell_blocks, station_blocks, pairs, epochs, places = sizes
    slots = len(places)
    list_ref, codes_ref, scalars_ref, sent, stations_ref, terms_ref, depths_ref, gaps_ref, lines_ref = scratch
    copy = send_codes(sizes, messages, codes_ref, scalars_ref, sent)
    dummy = slots * station_blocks
    stations_ref[slots] = jnp.zeros(stations_ref.shape[1:], F32)
    per_block = SBLOCK // LANES
    lane_rows = station_blocks * per_block
    for slot in range(slots):
        shift = tile_offset(places[slot]).astype(F32)
        rows = [messages[slot][pl.ds(0, lane_rows), :] + shift, messages[slot][pl.ds(lane_rows, lane_rows), :]]
        rows.append(jnp.zeros((LANES - 2 * lane_rows, LANES), F32))
        stations_ref[slot] = jnp.concatenate(rows, axis=0).T
    if clear:
        total_ref[...] = jnp.zeros_like(total_ref)
    count = list_pairs(sizes, copy, scalars_ref, list_ref)
    terms_ref[dummy] = jnp.zeros(terms_ref.shape[1:], BF16)
    for slot in range(slots):
        for q in range(station_blocks):
            stacked = doubled(jnp.concatenate([residuals[slot][q], images[slot][q]], axis=0), GROUP)
            high, low = split(stacked)
            terms_ref[slot * station_blocks + q, pl.ds(0, 2 * epochs), :] = high
            terms_ref[slot * station_blocks + q, pl.ds(2 * epochs, 2 * epochs), :] = low
    lane = lax.broadcasted_iota(jnp.int32, (1, LANES), 1)
    column = ((lane % COL_SIDE).astype(F32) + 0.5) / COL_SIDE
    line = ((lane // COL_SIDE).astype(F32) + 0.5) / COL_SIDE
    rows = CBLOCK // COL_SIDE
    chunks = CBLOCK // LANES
    stride = LANES / COL_SIDE / COL_SIDE

    def stage(i, k):
        code = list_ref[i]
        q, w = parts_of(code, cell_blocks)
        slot, within = parts_of(q, station_blocks)
        depths_ref[k] = cells_ref[pl.ds(0, 1), pl.ds(pl.multiple_of(w * CBLOCK, CBLOCK), CBLOCK)]
        lines = line + (w & 1).astype(F32) * (rows / COL_SIDE)
        places = pltpu.roll(stations_ref[slot], (LANES - within * per_block) & (LANES - 1), 1)
        for part in range(per_block):
            at = pl.ds(part * LANES, LANES)
            across = jnp.broadcast_to(places[:, part : part + 1], (LANES, LANES)) - column
            gaps_ref[k, at, :] = across * across
            along = jnp.broadcast_to(places[:, lane_rows + part : lane_rows + part + 1], (LANES, LANES))
            lines_ref[k, at, :] = along - lines

    def issue(sums, i, k):
        q, _ = parts_of(list_ref[i], cell_blocks)
        depth = depths_ref[k]
        for part in range(per_block):
            pieces = ([], [])
            for at in range(part * LANES, (part + 1) * LANES, 16):
                across = gaps_ref[k, pl.ds(at, 16), :]
                along = lines_ref[k, pl.ds(at, 16), :]
                level = across + along * along
                slope = stride * stride - 2 * stride * along
                for unit in range(2):
                    near = []
                    for chunk in range(unit * chunks // 2, (unit + 1) * chunks // 2):
                        squared = level + depth[:, chunk * LANES : (chunk + 1) * LANES]
                        near.append(split(inverse_cube(squared)))
                        if chunk < chunks - 1:
                            level = level + slope
                            slope = slope + 2 * stride * stride
                    pieces[unit].append([jnp.concatenate(terms, axis=1) for terms in zip(*near)])
            left = terms_ref[q, :, pl.ds(part * TILE, TILE)]
            for unit in range(2):
                multiply_add(sums[2 * k + unit], left, pieces[unit], GROUP, unit, part)

    def collect(sums, i, k):
        w = list_ref[i] & (cell_blocks - 1)
        for unit in range(2):
            both = pltpu.matmul_pop(sums[2 * k + unit])
            total_ref[w, :, pl.ds(unit * TILE, TILE)] += both[: 2 * epochs] + both[2 * epochs :]

    def run(*sums):
        pipelined(count, stage, functools.partial(issue, sums), functools.partial(collect, sums))

    pl.run_scoped(run, *accumulators(4 * epochs))


def slot_refs(slots, refs):
    messages, (residuals, images), rest = refs[:slots], refs[slots : slots + 2], refs[slots + 2 :]
    residuals, images = [residuals.at[0], residuals.at[1]], [images.at[0], images.at[1]]
    if slots == 3:
        third, *rest = rest
        residuals.append(third.at[0])
        images.append(third.at[1])
    return messages, residuals, images, rest


def near_kernel(sizes, *refs):
    cell_blocks, station_blocks, pairs, epochs, places = sizes
    slots = len(places)
    messages, residuals, images, rest = slot_refs(slots, refs)
    cells_ref, total_ref, *scratch = rest
    adjoint_sums(sizes, messages, residuals, images, cells_ref, total_ref, scratch, True)


def squares_kernel(old_ref, direction_ref, sums_ref):
    epochs, cells = direction_ref.shape

    def add(w, sums):
        at = pl.ds(pl.multiple_of(w * CBLOCK, CBLOCK), CBLOCK)
        old, direction = old_ref[:, at], direction_ref[:, at]
        return sums[0] + old * old, sums[1] + direction * direction

    zero = jnp.zeros((epochs, CBLOCK), F32)
    for i, total in enumerate(lax.fori_loop(0, cells // CBLOCK, add, (zero, zero), unroll=4)):
        sums_ref[pl.ds(i, 1), :] = jnp.broadcast_to(jnp.sum(total).reshape(1, 1), (1, LANES))


def far_kernel(sizes, *refs):
    cell_blocks, station_blocks, pairs, epochs, places = sizes
    slots = len(places)
    messages, residuals, images, rest = slot_refs(slots, refs)
    cells_ref, _, sums_ref, model_ref, direction_ref, image_ref = rest[:6]
    constant_ref, slope_ref, stats_ref, total_ref, *scratch = rest[6:]
    adjoint_sums(sizes, messages, residuals, images, cells_ref, total_ref, scratch, False)
    zero = jnp.zeros((epochs, CBLOCK), F32)

    def combine(w, sums):
        at = pl.ds(pl.multiple_of(w * CBLOCK, CBLOCK), CBLOCK)
        total = total_ref[w] * cells_ref[pl.ds(1, 1), at]
        constant = total[:epochs] - DAMPING * model_ref[:, at]
        slope = total[epochs:] + DAMPING * direction_ref[:, at]
        constant_ref[:, at] = constant
        slope_ref[:, at] = slope
        return sums[0] + constant * slope, sums[1] + slope * slope

    cross, square = lax.fori_loop(0, cell_blocks, combine, (zero, zero), unroll=4)
    square = jnp.sum(square).reshape(1, 1)
    cross = jnp.sum(cross).reshape(1, 1)
    local_step = jnp.where(square > 0, cross / jnp.where(square > 0, square, 1.0), 0.0)

    def remainder(w, sums):
        at = pl.ds(pl.multiple_of(w * CBLOCK, CBLOCK), CBLOCK)
        slope = slope_ref[:, at]
        left = constant_ref[:, at] - local_step * slope
        return sums[0] + left * left, sums[1] + left * slope

    left_square, left_cross = lax.fori_loop(0, cell_blocks, remainder, (zero, zero), unroll=4)
    image = image_ref[0]
    stats = [
        sums_ref[pl.ds(0, 1), pl.ds(0, 1)],
        sums_ref[pl.ds(1, 1), pl.ds(0, 1)],
        jnp.sum(image * image).reshape(1, 1),
        local_step,
        jnp.sum(left_square).reshape(1, 1),
        jnp.sum(left_cross).reshape(1, 1),
        jnp.sqrt(square),
    ]
    lane = lax.broadcasted_iota(jnp.int32, (1, LANES), 1)
    row = jnp.zeros((1, LANES), F32)
    for i, value in enumerate(stats):
        row = jnp.where(lane == i, value, row)
    for i in range(stats_ref.shape[0]):
        stats_ref[i] = row


def adjoint(sizes, messages, terms, cell_rows, *others, ranks=None):
    cell_blocks, station_blocks, pairs, epochs, places = sizes
    slots = len(places)
    total = (cell_blocks, 2 * epochs, CBLOCK)
    scratch = list_scratch(sizes) + [
        pltpu.VMEM((slots + 1, LANES, LANES), F32),
        pltpu.VMEM((slots * station_blocks + 1, 4 * epochs, 2 * SBLOCK), BF16),
        pltpu.VMEM((2, 1, CBLOCK), F32),
        pltpu.VMEM((2, SBLOCK, LANES), F32),
        pltpu.VMEM((2, SBLOCK, LANES), F32),
    ]
    if ranks is None:
        kernel, shapes, aliases = near_kernel, [total], {}
    else:
        kernel, cells = far_kernel, (epochs, cell_blocks * CBLOCK)
        shapes = [cells, cells, (ranks, 1, LANES), total]
        aliases = {slots + len(terms) + 1: 3}
    return pl.pallas_call(
        functools.partial(kernel, sizes),
        out_shape=tuple(jax.ShapeDtypeStruct(shape, F32) for shape in shapes),
        in_specs=[VMEM] * (slots + len(terms) + 1 + len(others)),
        out_specs=(VMEM,) * len(shapes),
        scratch_shapes=scratch,
        input_output_aliases=aliases,
        compiler_params=params(),
        cost_estimate=estimate(sizes),
        name="near" if ranks is None else "far",
    )(*messages, *terms, cell_rows, *others)


def finish_kernel(
    stats_ref, constant_ref, slope_ref, model_ref, direction_ref, residual_ref, image_ref,
    model_out, residual_out, direction_out, new_model, new_residual, new_direction, sent,
):
    stats = stats_ref[...][:, 0, :]
    gamma_old, direction_square, image_square = (
        jnp.sum(stats[:, i : i + 1], axis=0, keepdims=True) for i in range(3)
    )
    step = gamma_old / (image_square + DAMPING * direction_square + GUARD)
    ahead = step - stats[:, 3:4]
    reach = ahead * stats[:, 6:7]
    gamma_new = jnp.sum(stats[:, 4:5] - 2.0 * ahead * stats[:, 5:6] + reach * reach, axis=0, keepdims=True)
    ratio = gamma_new / (gamma_old + GUARD)
    copies = []

    def send(i, source, target, at):
        copies.append(pltpu.make_async_copy(source.at[:, at], target.at[:, at], sent.at[i]))
        copies[-1].start()

    for q in range(image_ref.shape[1]):
        at = pl.ds(q * SBLOCK, SBLOCK)
        new_residual[:, at] = residual_ref[q] - step * image_ref[0, q]
    send(0, new_residual, residual_out, pl.ds(0, new_residual.shape[1]))
    cells = model_ref.shape[1] // FINISH_PARTS
    for part in range(FINISH_PARTS):

        def block(w, unused):
            at = pl.ds(pl.multiple_of(part * cells + w * CBLOCK, CBLOCK), CBLOCK)
            direction = direction_ref[:, at]
            new_model[:, at] = model_ref[:, at] + step * direction
            new_direction[:, at] = (constant_ref[:, at] - step * slope_ref[:, at]) + ratio * direction
            return 0

        lax.fori_loop(0, cells // CBLOCK, block, 0, unroll=4)
        send(1 + 2 * part, new_model, model_out, pl.ds(part * cells, cells))
        send(2 + 2 * part, new_direction, direction_out, pl.ds(part * cells, cells))
    for copy in copies:
        copy.wait()


FINISH_PARTS = 4


def finish(stats, constant, slope, model_field, direction, residual, image):
    blocks, epochs, _ = residual.shape
    outs = (model_field.shape, (epochs, blocks * SBLOCK), direction.shape)
    return pl.pallas_call(
        finish_kernel,
        out_shape=tuple(jax.ShapeDtypeStruct(shape, F32) for shape in outs),
        in_specs=[VMEM] * 7,
        out_specs=(pl.BlockSpec(memory_space=pl.ANY),) * 3,
        scratch_shapes=[pltpu.VMEM(shape, F32) for shape in outs]
        + [pltpu.SemaphoreType.DMA((1 + 2 * FINISH_PARTS,))],
        compiler_params=params(),
        name="finish",
    )(stats, constant, slope, model_field, direction, residual, image)


def after(arrays, others):
    return lax.optimization_barrier((arrays, others))[0]


def shards(model_field, direction, old_grad, residual, block_pairs, depth_band, station_offsets):
    ranks = lax.axis_size("tile")
    epochs, cells = model_field.shape
    station_blocks, pairs = block_pairs.shape
    cell_blocks = cells // CBLOCK

    def to_partner(array):
        return lax.ppermute(array, "tile", [(i, i ^ 1) for i in range(ranks)])

    def across(message):
        ends = [(i, i + 1) for i in range(1, ranks - 1, 2)]
        return lax.ppermute(message, "tile", ends + [(j, i) for i, j in ends])

    sizes = (cell_blocks, station_blocks, pairs, epochs)
    near_slots, far_slots = (*sizes, (0, -1)), (*sizes, (1, 2, -2))

    own, residual = pack(station_offsets, block_pairs, residual)
    partner = to_partner(own)
    near = [own, partner]
    partner_residual = to_partner(residual)
    values, cell_rows, turned = prepare(2.0 / math.sqrt(cells), after(depth_band, own), direction)
    arrived = across(pair_up(own, after(partner, values)))
    residuals = pair_up(residual, partner_residual)
    arrived = after(arrived, residuals)
    far = [arrived[0], arrived[1], to_partner(arrived[0])]

    far_residuals = across(residuals)
    parts, third = forward(far_slots, far, values, turned)
    (third, far_residuals) = after((third, far_residuals), (far_residuals, third))
    returned = to_partner(third)
    given = across(far_parts(parts, returned))
    (mine,) = forward(near_slots, after(near, returned), values, turned)
    sums = small_call(squares_kernel, (2, LANES), "squares", *after((old_grad, direction), mine))
    given = after(given, (mine, sums))
    mine = small_call(add_kernel, mine.shape, "add", mine, given)
    images = both_images(mine, to_partner(mine))

    far_images = across(images)
    (near_total,) = adjoint(near_slots, near, [residuals, images], cell_rows)
    far_images = after(far_images, near_total)
    thirds = to_partner(small_call(thirds_kernel, far_images.shape, "thirds", far_residuals, far_images))
    constant, slope, stats, _ = adjoint(
        far_slots, far, [far_residuals, far_images, thirds], cell_rows,
        near_total, sums, model_field, direction, images, ranks=ranks,
    )
    stats = lax.all_to_all(stats, "tile", 0, 0)
    return finish(stats, constant, slope, model_field, direction, residual, images)


def solution(mesh):
    wide = P(None, ("groups", "tile"))
    mapped = jax.shard_map(
        shards,
        mesh=mesh,
        in_specs=(wide, wide, wide, wide, P(("groups", "tile"), None), P(("groups", "tile")), wide),
        out_specs=(wide, wide, wide),
        check_vma=False,
    )

    def step(*arrays):
        with jax.sharding.use_abstract_mesh(mesh.abstract_mesh):
            return mapped(*arrays)

    return step
```
